512 devices in a mesh: dp: 8 (over x, core), seq: 64 (over z, y).
Axes of the slice: x: 4, y: 8, z: 8, core: 2. Of those that a mesh axis runs over, the one named last changes fastest.
Arguments:
- inputs: bfloat16 [8, 16384, 960], P('dp', 'seq'), may hold values from -6 to 6
- cotangent: bfloat16 [8, 16384, 960], P('dp', 'seq'), may hold values from -6 to 6
- kernel: bfloat16 [16384, 960], P('seq'), may hold values from -6 to 6
- mix_in: bfloat16 [16384, 256], P('seq'), may hold values from -0.375 to 0.375
- mix_out: bfloat16 [16384, 256], P('seq'), may hold values from -0.375 to 0.375
- twiddle_self: bfloat16 [2, 6, 16384], P(None, None, 'seq'), may hold values from 0.796875 to 1.1953125
- twiddle_cross: bfloat16 [2, 6, 16384], P(None, None, 'seq'), may hold values from -0.59765625 to 0.59765625
- norm_gain: bfloat16 [960], replicated, may hold values from 0.5 to 1.5
- up_weight: bfloat16 [240, 1920], replicated, may hold values from -0.375 to 0.375
- down_weight: bfloat16 [240, 1920], replicated, may hold values from -0.25 to 0.25
Outputs:
- output: bfloat16 [8, 16384, 960], P('dp', 'seq')
- input_grad: bfloat16 [8, 16384, 960], P('dp', 'seq')
- kernel_grad: bfloat16 [16384, 960], P('seq')
- up_grad: float32 [240, 1920], P(None, 'seq')
- down_grad: float32 [240, 1920], P(None, 'seq')
- gain_grad: float32 [960], P('seq')
The draws below stay inside these ranges and needn't reach their ends.
All inputs are finite; a program needn't handle non-finite values.
Results may differ from the reference program's by a relative error of at most 0.02.
Values may be sent and summed in bfloat16 or wider, within the bound.
A program may use at most 64 MiB of HBM per device.

```python
import jax
import jax.numpy as jnp
from jax import lax

D = 960
FF = 1920
BLOCKS = 4
TOK_DEV = 256
BATCH = 8
TOKENS = 16384
SECTIONS = 6
DG = 240
FFG = 480
N_SEQ = 64


def level_of(own_key, shape, split, least, top_value):
    level, own = 1.0, jax.random.fold_in(own_key, 6)
    for position, blocks in split:
        heights = jnp.exp(jax.random.uniform(jax.random.fold_in(own, position), (blocks,), jnp.float32, least / len(split), top_value / len(split)))
        level = level * jnp.repeat(heights, shape[position] // blocks).reshape([-1 if axis == position else 1 for axis in range(len(shape))])
    return level


def normal_values(stream_key, shape, width, bound, cuts=(), held_as=jnp.bfloat16):
    loudness = level_of(stream_key, shape, cuts, -0.22, 0.18) if cuts else 1.0
    values = jax.random.normal(stream_key, shape, jnp.float32) * width * loudness
    return jnp.minimum(jnp.maximum(values, -bound), bound).astype(held_as)


def setup_inputs(seed: int = 0) -> dict:
    arg_keys = jax.random.split(jax.random.key(seed), 11)
    inputs = normal_values(arg_keys[0], (BATCH, TOKENS, D), 1.0, 6.0, ((0, 8), (1, 64)))
    cotangent = normal_values(arg_keys[1], (BATCH, TOKENS, D), 1.0, 6.0, ((0, 8), (1, 64)))
    kernel = normal_values(arg_keys[2], (TOKENS, D), 1.0, 6.0, ((0, 64),))
    mix_in = normal_values(arg_keys[3], (TOKENS, TOK_DEV), TOK_DEV ** -0.5, 0.375, ((0, 64),))
    mix_out = normal_values(arg_keys[4], (TOKENS, TOK_DEV), TOK_DEV ** -0.5, 0.375, ((0, 64),))
    twiddle_self = jnp.clip(0.796875 + 0.3984375 * jax.random.uniform(arg_keys[5], (2, SECTIONS, TOKENS), jnp.float32) ** level_of(arg_keys[5], (2, SECTIONS, TOKENS), ((2, 64),), -0.2, 0.2), 0.796875, 1.1953125).astype(jnp.bfloat16)
    twiddle_cross = jnp.clip(jax.random.uniform(arg_keys[6], (2, SECTIONS, TOKENS), jnp.float32, -0.59765625, 0.59765625) * level_of(arg_keys[6], (2, SECTIONS, TOKENS), ((2, 64),), -0.4, 0.0), -0.59765625, 0.59765625).astype(jnp.bfloat16)
    norm_gain = jnp.clip(1.0 + 0.1 * jax.random.normal(arg_keys[7], (D,), jnp.float32), 0.5, 1.5).astype(jnp.bfloat16)
    up_weight = normal_values(arg_keys[8], (DG, FF), DG ** -0.5, 0.375)
    down_weight = normal_values(arg_keys[9], (DG, FF), FFG ** -0.5, 0.25)
    return dict(inputs=inputs, cotangent=cotangent, kernel=kernel, mix_in=mix_in, mix_out=mix_out, twiddle_self=twiddle_self, twiddle_cross=twiddle_cross, norm_gain=norm_gain, up_weight=up_weight, down_weight=down_weight)


root_half = 0.7978845608028654
cubic_term = 0.044715

def rounded(values):
    return lax.optimization_barrier(values.astype(jnp.bfloat16))

def gelu_value(preact):
    inner_arg = root_half * (preact + cubic_term * preact * preact * preact)
    return 0.5 * preact * (1.0 + jnp.tanh(inner_arg))

def gelu_slope(preact):
    inner_arg = root_half * (preact + cubic_term * preact * preact * preact)
    tangent = jnp.tanh(inner_arg)
    return 0.5 * (1.0 + tangent) + 0.5 * preact * (1.0 - tangent * tangent) * root_half * (1.0 + 3.0 * cubic_term * preact * preact)

def partner_rows(values, stride):
    shard_count = values.shape[0]
    grouped = values.reshape((shard_count // (2 * stride), 2, stride) + values.shape[1:])
    return jnp.flip(grouped, axis=1).reshape(values.shape)

def forward_sections(values, self_rows, cross_rows):
    for section_index in range(SECTIONS):
        partner = partner_rows(values, 2 ** section_index)
        values = rounded(self_rows[section_index][..., None] * values.astype(jnp.float32) + cross_rows[section_index][..., None] * partner.astype(jnp.float32))
    return values

def backward_sections(gradient, self_rows, cross_rows):
    for section_index in reversed(range(SECTIONS)):
        stride = 2 ** section_index
        partner = partner_rows(gradient, stride)
        partner_cross = partner_rows(cross_rows[section_index], stride)
        gradient = rounded(self_rows[section_index][..., None] * gradient.astype(jnp.float32) + partner_cross[..., None] * partner.astype(jnp.float32))
    return gradient

def reference(inputs, cotangent, kernel, mix_in, mix_out, twiddle_self, twiddle_cross, norm_gain, up_weight, down_weight):
    shard_count = N_SEQ
    self_rows = twiddle_self.astype(jnp.float32).reshape(2, SECTIONS, shard_count, TOK_DEV)
    cross_rows = twiddle_cross.astype(jnp.float32).reshape(2, SECTIONS, shard_count, TOK_DEV)
    in_blocks = mix_in.astype(jnp.float32).reshape(shard_count, TOK_DEV, TOK_DEV)
    out_blocks = mix_out.astype(jnp.float32).reshape(shard_count, TOK_DEV, TOK_DEV)
    kernel_wide = kernel.astype(jnp.float32).reshape(shard_count, TOK_DEV, D)
    gain_wide = norm_gain.astype(jnp.float32)
    up_blocks = up_weight.astype(jnp.float32).reshape(DG, BLOCKS, FFG)
    down_blocks = down_weight.astype(jnp.float32).reshape(DG, BLOCKS, FFG)

    def one_sequence(running, sequence_pair):
        kernel_sum, up_sum, down_sum, gain_sum = running
        seq_in, seq_cot = sequence_pair
        shaped_in = seq_in.astype(jnp.float32).reshape(shard_count, TOK_DEV, D)
        premixed = rounded(jnp.einsum('sqr,srd->sqd', in_blocks, shaped_in))
        spectrum = forward_sections(premixed, self_rows[0], cross_rows[0])
        weighted = rounded(spectrum.astype(jnp.float32) * kernel_wide)
        mixed_seq = forward_sections(weighted, self_rows[1], cross_rows[1])
        hidden = rounded(shaped_in + jnp.einsum('sqr,srd->sqd', out_blocks, mixed_seq.astype(jnp.float32)))
        widened = hidden.astype(jnp.float32).reshape(TOKENS, D)
        row_scale = lax.rsqrt(lax.optimization_barrier(jnp.mean(widened * widened, axis=-1, keepdims=True)) + 1e-06)
        normed = rounded(widened * row_scale * gain_wide)
        normed_blocks = normed.astype(jnp.float32).reshape(TOKENS, BLOCKS, DG)
        pre_act = jnp.einsum('tgd,dgf->tgf', normed_blocks, up_blocks)
        activation = rounded(gelu_value(pre_act))
        act_wide = activation.astype(jnp.float32)
        channel_out = jnp.einsum('tgf,jgf->tgj', act_wide, down_blocks)
        output = (widened + channel_out.transpose(0, 2, 1).reshape(TOKENS, D)).astype(jnp.bfloat16)
        cot_blocks = seq_cot.astype(jnp.float32).reshape(TOKENS, DG, BLOCKS).transpose(0, 2, 1)
        down_term = jnp.einsum('tgf,tgj->jgf', act_wide, cot_blocks)
        act_cot = jnp.einsum('tgj,jgf->tgf', cot_blocks, down_blocks)
        pre_grad = rounded(act_cot * gelu_slope(pre_act)).astype(jnp.float32)
        up_term = jnp.einsum('tgf,tgd->dgf', pre_grad, normed_blocks)
        normed_grad = jnp.einsum('tgf,dgf->tgd', pre_grad, up_blocks).reshape(TOKENS, D)
        gain_term = lax.optimization_barrier(jnp.sum(normed_grad * widened * row_scale, axis=0))
        gained = normed_grad * gain_wide
        hidden_grad = rounded(seq_cot.astype(jnp.float32) + row_scale * gained - widened * row_scale ** 3 * lax.optimization_barrier(jnp.mean(gained * widened, axis=-1, keepdims=True)))
        hidden_blocks = hidden_grad.astype(jnp.float32).reshape(shard_count, TOK_DEV, D)
        mixed_grad = rounded(jnp.einsum('sqr,sqd->srd', out_blocks, hidden_blocks))
        weighted_grad = backward_sections(mixed_grad, self_rows[1], cross_rows[1])
        kernel_term = spectrum.astype(jnp.float32) * weighted_grad.astype(jnp.float32)
        spectrum_grad = rounded(weighted_grad.astype(jnp.float32) * kernel_wide)
        pre_cot = backward_sections(spectrum_grad, self_rows[0], cross_rows[0])
        input_grad = (hidden_blocks + jnp.einsum('sqr,sqd->srd', in_blocks, pre_cot.astype(jnp.float32))).astype(jnp.bfloat16).reshape(TOKENS, D)
        running = (kernel_sum + kernel_term, up_sum + up_term, down_sum + down_term, gain_sum + gain_term)
        return (running, (output, input_grad))
    start_sums = (jnp.zeros((shard_count, TOK_DEV, D), jnp.float32), jnp.zeros((DG, BLOCKS, FFG), jnp.float32), jnp.zeros((DG, BLOCKS, FFG), jnp.float32), jnp.zeros((D,), jnp.float32))
    final_sums, (outputs_all, input_grads) = lax.scan(one_sequence, start_sums, (inputs, cotangent))
    kernel_sum, up_sum, down_sum, gain_sum = final_sums
    scale_factor = (BATCH * TOKENS) ** (-0.5)
    kernel_grad = kernel_sum.reshape(TOKENS, D).astype(jnp.bfloat16)
    return (outputs_all, input_grads, kernel_grad, (up_sum * scale_factor).reshape(DG, FF), (down_sum * scale_factor).reshape(DG, FF), gain_sum * scale_factor)
```

```python
import jax
import jax.numpy as jnp
from jax import lax
from jax.experimental import pallas as pl
from jax.experimental.pallas import tpu as pltpu
from jax.sharding import PartitionSpec as P

MESH = pl.DeviceIdType.MESH
BF = jnp.bfloat16
F32 = jnp.float32

D = 960
GROUPS = 4
DG = 240
FFG = 480
SIDE = 8
PIECE = 16
ROOT_HALF = 0.7978845608028654
CUBIC = 0.044715
SCALE = 131072.0**-0.5
GAIN_WINDOWS = ((0, 256), (128, 512), (384, 768), (640, 960))
HIDDEN_WINDOWS = ((0, 512), (384, 1024), (896, 1536), (1408, 1920))


def dot(a, b):
    return lax.dot_general(a, b, (((1,), (0,)), ((), ())), preferred_element_type=F32)


def dot_tn(a, b):
    return lax.dot_general(a, b, (((0,), (0,)), ((), ())), preferred_element_type=F32)


def dot_nt(a, b):
    return lax.dot_general(a, b, (((1,), (1,)), ((), ())), preferred_element_type=F32)


def iotas(shape):
    return lax.broadcasted_iota(jnp.int32, shape, 0), lax.broadcasted_iota(jnp.int32, shape, 1)


def ones_where(mask):
    return jnp.where(mask, 1.0, 0.0).astype(BF)


def repeat(count, body, start=0):
    def step(index, carry):
        body(index)
        return carry

    lax.fori_loop(start, count, step, 0)


def wrapped(value):
    return lax.rem(value + 2 * SIDE, SIDE)


def await_bytes(view, sem):
    pltpu.make_async_copy(view, view, sem).wait()


def mix(values, selfs, crosses, bits, transposed):
    for k, bit in bits:
        stride = 1 << bit
        if transposed:
            scaled = [crosses[a][k] * values[a] for a in range(SIDE)]
            values = [selfs[a][k] * values[a] + scaled[a ^ stride] for a in range(SIDE)]
        else:
            values = [selfs[a][k] * values[a] + crosses[a][k] * values[a ^ stride] for a in range(SIDE)]
    return values


def kernel(
    x_hbm, cot_hbm, ker_hbm, min_hbm, mout_hbm, ts_hbm, tc_hbm, gain_hbm, up_hbm, down_hbm,
    out_hbm, ig_hbm, kg_hbm, ug_hbm, dg_hbm, gn_hbm,
    xv, kv, cotv, min_ref, mout_ref, ts_ref, tc_ref, gain_ref, up_ref, down_ref,
    outv, igv, kgv, ugv, dgv, gnv,
    eye, mint, moutt, twp, xg, cotg, cotn, upp, dnp, ww, acot, pa, act, pgr, hg, ng, ngr, hgr, acc, gaing, rowscale, wsum,
    src1, a1, ks, kt, ff, sp, src2, m2, src3, a3, src4, m4,
    kgb, kra, kgh, krb, kgs, kgf, gg, r1a, h1, r1b, fin, rf,
    in_s, out_s, s1, v1, s2, v2, s3, v3, s4, v4,
    ks_s, ks_v, ka_s, ka_v, kb_s, kb_v, kr_s, kr_v, kc_s, kc_v, kf_s, kf_v, kh_s, kh_v, ki_s, ki_v,
    ga_s, ga_v, gb_s, gb_v, gf_s, gf_v,
):
    loads = []

    def load(src, dst):
        copy = pltpu.make_async_copy(src, dst, in_s.at[len(loads)])
        copy.start()
        loads.append(copy)
        return copy

    def load_groups(src, dst):
        return [load(src.at[pl.ds(g * DG, DG)], dst.at[g, pl.ds(0, DG)]) for g in range(GROUPS)]

    tw_here = [load(ts_hbm, ts_ref), load(tc_hbm, tc_ref)]
    ker_here = load_groups(ker_hbm, kv)
    x_here = [load(min_hbm, min_ref)] + load_groups(x_hbm, xv)
    rest_here = load_groups(cot_hbm, cotv)
    rest_here += [load(gain_hbm, gain_ref), load(up_hbm, up_ref), load(down_hbm, down_ref), load(mout_hbm, mout_ref)]

    me = lax.axis_index("seq")
    z, y = lax.div(me, SIDE), lax.rem(me, SIDE)
    i = lax.axis_index("dp")
    chip, core = lax.div(i, 2), lax.rem(i, 2)
    mate = i + 1 - 2 * core
    yo = wrapped(i - y)

    barrier = pltpu.get_barrier_semaphore()

    def greet_seq(step):
        pl.semaphore_signal(
            barrier, inc=1, device_id={"seq": lax.rem(me + step, 64)}, device_id_type=MESH
        )

    def greet_dp(step):
        pl.semaphore_signal(barrier, inc=1, device_id={"dp": wrapped(i + step)}, device_id_type=MESH)

    repeat(64, greet_seq, 1)
    repeat(8, greet_dp, 1)

    def send(src, dst, ssem, rsem, device):
        pltpu.make_async_remote_copy(
            src_ref=src, dst_ref=dst, send_sem=ssem, recv_sem=rsem, device_id=device, device_id_type=MESH
        ).start()

    def send_part(part, src, dst, ssem, rsem):
        def one(dz, dy):
            tz, ty = wrapped(z + dz), wrapped(y + dy)
            send(src(tz, ty), dst, ssem.at[dz], rsem, {"seq": tz * SIDE + ty})

        if part == 0:
            pltpu.make_async_copy(src(z, y), dst, rsem).start()
            one(4, 0)

        def pair(t):
            one(part, lax.rem(5 * t, SIDE))
            one((4, 7, 6, 5)[part], lax.rem(5 * t, SIDE))

        repeat(SIDE, pair, 1 if part == 0 else 0)

    def await_sent(buffer, ssem):
        await_bytes(buffer.at[0, pl.ds(0, 7)], ssem.at[0])
        for dz in range(1, SIDE):
            await_bytes(buffer.at[0], ssem.at[dz])

    def store_grouped(ref, g, value):
        split = value.reshape(SIDE, 2, PIECE, 256)
        ref[:, g, :, 0:256] = split[:, 0]
        ref[:, 4 + g, :, 0:256] = split[:, 1]

    def load_grouped(ref, g):
        return jnp.stack([ref[:, g, :, 0:256], ref[:, 4 + g, :, 0:256]], axis=1).reshape(256, 256)

    def slot(chip_at, core_at):
        return wrapped(2 * chip_at + core_at - y)

    def to_chips(buffer, ssem, rsem):
        send(buffer.at[yo], buffer.at[yo], ssem.at[0], rsem.at[0], {"dp": mate})

        def step_to(step):
            send(
                buffer.at[yo], buffer.at[yo], ssem.at[step], rsem.at[step],
                {"dp": 2 * lax.rem(chip + step, 4) + core},
            )

        repeat(4, step_to, 1)

    def to_mate(buffer, rsem, ssem2, rsem2):
        def step_to(step):
            held = buffer.at[slot(lax.rem(chip + 4 - step, 4), core)]
            await_bytes(held, rsem.at[step])
            send(held, held, ssem2.at[step], rsem2.at[step], {"dp": mate})

        repeat(4, step_to, 1)

    def from_mate(buffer, rsem, rsem2):
        await_bytes(buffer.at[slot(chip, 1 - core)], rsem.at[0])

        def step_from(step):
            await_bytes(buffer.at[slot(lax.rem(chip + 4 - step, 4), 1 - core)], rsem2.at[step])

        repeat(4, step_from, 1)

    r, l = iotas((256, 256))
    eye[...] = ones_where(r == l)
    twp[...] = jnp.zeros_like(twp)
    for copy in tw_here:
        copy.wait()
    for k in range(6):
        for which in range(2):
            twp[which, pl.ds(DG + k, 1)] = ts_ref[k, which : which + 1].astype(F32)
            twp[which, pl.ds(DG + 8 + k, 1)] = tc_ref[k, which : which + 1].astype(F32)
    for copy in ker_here:
        copy.wait()
    for g in range(GROUPS):
        kv[g, pl.ds(DG, PIECE)] = twp[1, pl.ds(DG, PIECE)].astype(BF)
        store_grouped(ks, g, dot_nt(eye[...], kv[g]).astype(BF))
    columns = dot_nt(eye[...], twp[0].astype(BF))
    for copy in x_here:
        copy.wait()
    for g in range(GROUPS):
        xv[g, pl.ds(DG, PIECE)] = jnp.zeros((PIECE, 256), BF)
        store_grouped(src1, g, (dot_nt(min_ref[...], xv[g]) + columns).astype(BF))

    pl.semaphore_wait(barrier, 70)

    def share_kernel(dz):
        tz = wrapped(z + dz)
        send(ks.at[tz, yo], kt.at[y, z], ks_s.at[1], ks_v, {"seq": tz * SIDE + yo})

    repeat(SIDE, share_kernel, 1)

    @pl.when(yo != y)
    def _():
        send(ks.at[z, yo], kt.at[y, z], ks_s.at[0], ks_v, {"seq": z * SIDE + yo})

    @pl.when(yo == y)
    def _():
        pltpu.make_async_copy(ks.at[z, yo], kt.at[y, z], ks_v).start()

    first = (lambda tz, ty: src1.at[tz, ty], a1.at[z, y], s1, v1.at[z])
    send_part(0, *first)
    send_part(1, *first)
    await_bytes(kt.at[yo], ks_v)
    to_chips(kt, ka_s, ka_v)
    send_part(2, *first)
    send_part(3, *first)

    for copy in rest_here:
        copy.wait()
    for g in range(GROUPS):
        xg[g] = dot_nt(eye[...], xv[g]).astype(BF)
        cotv[g, pl.ds(DG, PIECE)] = jnp.zeros((PIECE, 256), BF)
    mint[...] = dot_nt(eye[...], min_ref[...]).astype(BF)
    moutt[...] = dot_nt(eye[...], mout_ref[...]).astype(BF)
    for g in range(GROUPS):
        cotn[g] = dot_nt(eye[...], cotv[g]).astype(BF)
        picked = jnp.zeros((256, 256), F32)
        for part in range(GROUPS):
            j, lane = iotas((256, 256))
            picked = picked + dot(ones_where((part * DG + lane == 4 * j + g) & (lane < DG)), cotv[part])
        cotg[g] = dot_nt(eye[...], picked.astype(BF)).astype(BF)
        low, high = GAIN_WINDOWS[g]
        channel, lane = iotas((high - low, 256))
        gain_rows = jnp.broadcast_to(gain_ref[:, low:high].astype(F32), (PIECE, high - low)).astype(BF)
        gaing[g] = dot(gain_rows, ones_where((channel + low == g * DG + lane) & (lane < DG)))[0:8]
    to_mate(kt, ka_v, kb_s, kb_v)
    for g in range(GROUPS):
        low, high = HIDDEN_WINDOWS[g]
        column, hidden_unit = iotas((high - low, 512))
        chosen = (column + low == g * FFG + hidden_unit - 2 * (hidden_unit >> 5)) & ((hidden_unit & 31) < 30)
        chooser = ones_where(chosen)
        upp[g, 0:DG] = dot(up_ref[:, low:high], chooser).astype(BF)
        dnp[g, 0:DG] = dot(down_ref[:, low:high], chooser).astype(BF)
        upp[g, DG:256] = jnp.zeros((256 - DG, 512), BF)
        dnp[g, DG:256] = jnp.zeros((256 - DG, 512), BF)

    def twiddles(slab):
        wide = slab.astype(F32)
        return [wide[:, 112 + k : 113 + k] for k in range(6)], [wide[:, 120 + k : 121 + k] for k in range(6)]

    def input_twiddles(shards):
        pairs = [twiddles(a1[sz, sy, :, 128:256]) for sz, sy in shards]
        return [p[0] for p in pairs], [p[1] for p in pairs]

    def output_twiddles(shards):
        pairs = [twiddles(kt[sy, sz, :, 128:256]) for sz, sy in shards]
        return [p[0] for p in pairs], [p[1] for p in pairs]

    low_bits = ((0, 0), (1, 1), (2, 2))
    high_bits = ((3, 0), (4, 1), (5, 2))
    low_back = tuple(reversed(low_bits))
    high_back = tuple(reversed(high_bits))

    def row_of(sz):
        return [(sz, a) for a in range(SIDE)]

    def column_of(sy):
        return [(a, sy) for a in range(SIDE)]

    def forward_one(step):
        sz = wrapped(z + step)
        await_bytes(a1.at[sz], v1.at[sz])
        shards = row_of(sz)
        values = [a1[p, q].astype(F32) for p, q in shards]
        values = mix(values, *input_twiddles(shards), low_bits, False)
        for (p, q), value in zip(shards, values):
            ff[p, q] = value

    repeat(SIDE, forward_one)
    from_mate(kt, ka_v, kb_v)

    def forward_two(sy):
        shards = column_of(sy)
        values = mix([ff[p, q] for p, q in shards], *input_twiddles(shards), high_bits, False)
        for (p, q), value in zip(shards, values):
            rounded = value.astype(BF)
            sp[p, q] = rounded
            ff[p, q] = rounded.astype(F32) * kt[q, p].astype(F32)

    repeat(SIDE, forward_two)

    def forward_three(sz):
        shards = row_of(sz)
        values = mix([ff[p, q] for p, q in shards], *output_twiddles(shards), low_bits, False)
        for (p, q), value in zip(shards, values):
            ff[p, q] = value

    repeat(SIDE, forward_three)

    def forward_four(sy):
        shards = column_of(sy)
        values = mix([ff[p, q] for p, q in shards], *output_twiddles(shards), high_bits, False)
        for (p, q), value in zip(shards, values):
            src2[p, q] = value.astype(BF)

    repeat(SIDE, forward_four)
    for part in range(4):
        send_part(part, lambda tz, ty: src2.at[tz, ty], m2.at[z, y], s2, v2.at[z])

    for g in range(GROUPS):
        acot[g] = dot(cotg[g], dnp[g])
        channel, j = iotas((D, 256))
        spread = ones_where((channel == 4 * j + g) & (j < DG))
        ww[:, pl.ds(g * 512, 512)] = dot(spread, dnp[g]).astype(BF)

    for sz in range(SIDE):
        await_bytes(m2.at[sz], v2.at[sz])

    lane_here = lax.broadcasted_iota(jnp.int32, (256, 256), 1) < DG
    squares = jnp.zeros((256, 1), F32)
    for g in range(GROUPS):
        value = xg[g].astype(F32) + dot(mout_ref[...], load_grouped(m2, g))
        value = jnp.where(lane_here, value, 0.0).astype(BF)
        hg[g] = value
        wide = value.astype(F32)
        squares = squares + jnp.sum(wide * wide, axis=1, keepdims=True)
    scale_column = lax.rsqrt(squares * (1.0 / D) + 1e-06)
    rowscale[...] = jnp.broadcast_to(scale_column, (256, 128))

    for g in range(GROUPS):
        wide = hg[g].astype(F32)
        ng[g] = (wide * rowscale[:, 0:1] * gaing[g, 0:1]).astype(BF)
        pa[...] = dot(ng[g], upp[g])

        def activate(tile, g=g):
            rows = pl.ds(pl.multiple_of(tile * 32, 32), 32)
            p = pa[rows]
            square = p * p
            tangent = jnp.tanh(p * (ROOT_HALF + (ROOT_HALF * CUBIC) * square))
            half_more = 0.5 + 0.5 * tangent
            act[rows, pl.ds(g * 512, 512)] = (p * half_more).astype(BF)
            inner = ROOT_HALF + (3.0 * ROOT_HALF * CUBIC) * square
            slope = half_more + 0.5 * p * (1.0 - tangent * tangent) * inner
            pgr[g, rows] = (acot[g, rows] * slope).astype(BF)

        repeat(8, activate)
        ngr[g] = dot_nt(pgr[g], upp[g])

    means = jnp.zeros((256, 1), F32)
    for g in range(GROUPS):
        means = means + jnp.sum(ngr[g] * gaing[g, 0:1] * hg[g].astype(F32), axis=1, keepdims=True)
    scale_column = rowscale[:, 0:1]
    means = means * (1.0 / D) * scale_column * scale_column * scale_column
    for g in range(GROUPS):
        gained = ngr[g] * gaing[g, 0:1]
        hgr[g] = (cotn[g].astype(F32) + scale_column * gained - hg[g].astype(F32) * means).astype(BF)
        store_grouped(src3, g, dot(moutt[...], hgr[g]).astype(BF))
    for part in range(4):
        send_part(part, lambda tz, ty: src3.at[tz, ty], a3.at[y, z], s3, v3.at[y])

    row_here = (lax.broadcasted_iota(jnp.int32, (512, 256), 0) & 31) == 30
    for g in range(GROUPS):
        gain_term = jnp.sum(ngr[g] * hg[g].astype(F32) * rowscale[:, 0:1], axis=0, keepdims=True)
        up_term = jnp.where(row_here, gain_term, dot_tn(pgr[g], ng[g]))
        down_term = dot_tn(act[:, pl.ds(g * 512, 512)], cotg[g])
        for kind, term in ((0, up_term), (1, down_term)):
            split = term.astype(BF).reshape(16, 2, PIECE, 256)
            for half in range(2):
                for side in range(2):
                    gg[side, 2 * kind + half, pl.ds(g * 16, 16)] = split[:, half, :, side * 128 : side * 128 + 128]

    send(gg.at[1 - core], r1a, ga_s, ga_v, {"dp": mate})

    acc[...] = dot_nt(ww[...], act[...])
    for g in range(GROUPS):
        rows = pl.ds(g * DG, DG)
        outv[rows] = (acc[rows] + dot_nt(eye[0:DG], hg[g])).astype(BF)
    pltpu.make_async_copy(outv, out_hbm, out_s.at[0]).start()

    await_bytes(r1a, ga_v)

    def pair_sum(step):
        for slab in range(4):
            part = pl.ds(pl.multiple_of(step * 8, 8), 8)
            both = gg[core, slab, part].astype(F32) + r1a[slab, part].astype(F32)
            h1[slab, part] = both.astype(BF)

    repeat(8, pair_sum)

    def spread_terms(step):
        other = lax.rem(chip + step, 4)
        send(h1.at[other], r1b.at[chip], gb_s.at[step], gb_v.at[step], {"dp": other * 2 + core})

    repeat(4, spread_terms, 1)

    def backward_one(step):
        sy = wrapped(y + step)
        await_bytes(a3.at[sy], v3.at[sy])
        shards = column_of(sy)
        values = [a3[q, p].astype(F32) for p, q in shards]
        values = mix(values, *output_twiddles(shards), high_back, True)
        for (p, q), value in zip(shards, values):
            ff[p, q] = value

    repeat(SIDE, backward_one)

    def backward_two(sz):
        shards = row_of(sz)
        values = mix([ff[p, q] for p, q in shards], *output_twiddles(shards), low_back, True)
        for (p, q), value in zip(shards, values):
            wide = value.astype(BF).astype(F32)
            owner = wrapped(q + y)
            kgb[lax.rem(owner, 2), lax.div(owner, 2), p] = (sp[p, q].astype(F32) * wide).astype(BF)
            ff[p, q] = wide * kt[q, p].astype(F32)

    repeat(SIDE, backward_two)

    send(kgb.at[1 - core], kra, kr_s, kr_v, {"dp": mate})

    def backward_three(sy):
        shards = column_of(sy)
        values = mix([ff[p, q] for p, q in shards], *input_twiddles(shards), high_back, True)
        for (p, q), value in zip(shards, values):
            ff[p, q] = value

    repeat(SIDE, backward_three)

    await_bytes(kra, kr_v)

    def kernel_pair(sz):
        for at in range(4):
            kgh[at, sz] = (kgb[core, at, sz].astype(F32) + kra[at, sz].astype(F32)).astype(BF)

    repeat(SIDE, kernel_pair)

    def spread_kernel_terms(step):
        other = lax.rem(chip + step, 4)
        send(kgh.at[other], krb.at[chip], kc_s.at[step], kc_v.at[step], {"dp": other * 2 + core})

    repeat(4, spread_kernel_terms, 1)

    def backward_four(sz):
        shards = row_of(sz)
        values = mix([ff[p, q] for p, q in shards], *input_twiddles(shards), low_back, True)
        for (p, q), value in zip(shards, values):
            src4[p, q, :, 0:256] = value.astype(BF)

    repeat(SIDE, backward_four)

    others = [lax.rem(chip + step, 4) for step in (1, 2, 3)]

    def terms_here(step):
        await_bytes(r1b.at[lax.rem(chip + 4 - step, 4)], gb_v.at[step])

    repeat(4, terms_here, 1)

    def chip_sum(sz):
        part = pl.ds(pl.multiple_of(sz * 8, 8), 8)
        four = h1[chip, part].astype(F32)
        for other in others:
            four = four + r1b[other, part].astype(F32)
        src4[sz, :, :, 256:384] = four.astype(BF)

    repeat(SIDE, chip_sum)

    last = (lambda tz, ty: src4.at[tz, ty], m4.at[z, y], s4, v4.at[z])
    send_part(0, *last)
    send_part(1, *last)

    def kernel_terms_here(step):
        await_bytes(krb.at[lax.rem(chip + 4 - step, 4)], kc_v.at[step])

    repeat(4, kernel_terms_here, 1)

    def kernel_sum(sz):
        four = kgh[chip, sz].astype(F32)
        for other in others:
            four = four + krb[other, sz].astype(F32)
        kgs[sz] = four.astype(BF)

    repeat(SIDE, kernel_sum)

    def return_kernel(dz):
        tz = wrapped(z + dz)
        send(kgs.at[tz], kgf.at[y, z], kf_s.at[1], kf_v, {"seq": tz * SIDE + yo})

    repeat(SIDE, return_kernel, 1)

    @pl.when(yo != y)
    def _():
        send(kgs.at[z], kgf.at[y, z], kf_s.at[0], kf_v, {"seq": z * SIDE + yo})

    @pl.when(yo == y)
    def _():
        pltpu.make_async_copy(kgs.at[z], kgf.at[y, z], kf_v).start()

    send_part(2, *last)
    send_part(3, *last)

    await_bytes(kgf.at[yo], kf_v)
    to_chips(kgf, kh_s, kh_v)
    to_mate(kgf, kh_v, ki_s, ki_v)
    from_mate(kgf, kh_v, ki_v)
    for g in range(GROUPS):
        held = jnp.stack([kgf[g], kgf[4 + g]], axis=1).reshape(256, 256)
        kgv[pl.ds(g * DG, DG)] = dot_nt(eye[0:DG], held).astype(BF)
    pltpu.make_async_copy(kgv, kg_hbm, out_s.at[1]).start()

    shard_sum = jnp.zeros((PIECE, 128), F32)
    for sz in range(SIDE):
        await_bytes(m4.at[sz], v4.at[sz])
        for sy in range(SIDE):
            shard_sum = shard_sum + m4[sz, sy, :, 256:384].astype(F32)
    shard_sum = shard_sum * SCALE
    fin[...] = shard_sum
    rf[i] = shard_sum

    def spread_grads(step):
        send(fin, rf.at[i], gf_s.at[step], gf_v.at[step], {"dp": wrapped(i + step)})

    repeat(SIDE, spread_grads, 1)

    for g in range(GROUPS):
        value = (hgr[g].astype(F32) + dot(mint[...], load_grouped(m4, g))).astype(BF)
        igv[pl.ds(g * DG, DG)] = dot_nt(eye[0:DG], value).astype(BF)
    pltpu.make_async_copy(igv, ig_hbm, out_s.at[2]).start()

    def grads_here(step):
        await_bytes(rf.at[wrapped(i - step)], gf_v.at[step])

    repeat(SIDE, grads_here, 1)
    for share in range(SIDE):
        kind, half, side = share // 4, (share // 2) % 2, share % 2
        wsum[kind, pl.ds(half * PIECE, PIECE), pl.ds(side * 128, 128)] = rf[share]
    ugv[...] = wsum[0, 0:30, 0:DG]
    dgv[...] = wsum[1, 0:30, 0:DG]
    j, lane = iotas((256, 128))
    picker = jnp.where(j == lane + 15 * lax.rem(me, 16), 1.0, 0.0)
    gains = jnp.broadcast_to(wsum[0, 30:31], (8, 256))
    picked = lax.dot_general(
        gains, picker, (((1,), (0,)), ((), ())), precision=lax.Precision.HIGHEST, preferred_element_type=F32
    )
    gnv[...] = picked[0:1, 0:15]
    pltpu.make_async_copy(ugv, ug_hbm, out_s.at[3]).start()
    pltpu.make_async_copy(dgv, dg_hbm, out_s.at[4]).start()
    pltpu.make_async_copy(gnv, gn_hbm, out_s.at[5]).start()

    for buffer, sem in ((src1, s1), (src2, s2), (src3, s3), (src4, s4)):
        await_sent(buffer, sem)
    await_bytes(ks.at[0, pl.ds(0, 7)], ks_s.at[1])
    await_bytes(kgs.at[pl.ds(0, 7)], kf_s.at[1])

    @pl.when(yo != y)
    def _():
        await_bytes(ks.at[0, 0], ks_s.at[0])
        await_bytes(kgs.at[0], kf_s.at[0])

    await_bytes(kt.at[0], ka_s.at[0])
    await_bytes(kgf.at[0], kh_s.at[0])
    await_bytes(r1a, ga_s)
    await_bytes(kra, kr_s)

    def chips_left(step):
        await_bytes(kt.at[0], ka_s.at[step])
        await_bytes(kt.at[0], kb_s.at[step])
        await_bytes(kgf.at[0], kh_s.at[step])
        await_bytes(kgf.at[0], ki_s.at[step])
        await_bytes(kgh.at[0], kc_s.at[step])
        await_bytes(h1.at[0], gb_s.at[step])

    repeat(4, chips_left, 1)

    def grads_left(step):
        await_bytes(fin, gf_s.at[step])

    repeat(SIDE, grads_left, 1)
    outs = ((outv, out_hbm), (kgv, kg_hbm), (igv, ig_hbm), (ugv, ug_hbm), (dgv, dg_hbm), (gnv, gn_hbm))
    for index, (held, there) in enumerate(outs):
        pltpu.make_async_copy(held, there, out_s.at[index]).wait()


def settle(*refs):
    held, there, sems = refs[:6], refs[6:12], refs[12]
    copies = [pltpu.make_async_copy(held[index], there[index], sems.at[index]) for index in range(6)]
    for copy in copies:
        copy.start()
    for copy in copies:
        copy.wait()


def local(
    inputs, cotangent, kernel_values, mix_in, mix_out, twiddle_self, twiddle_cross, norm_gain, up_weight, down_weight
):
    hbm = pl.BlockSpec(memory_space=pltpu.HBM)
    dma = pltpu.SemaphoreType.DMA
    vmem = pltpu.VMEM
    exchange = vmem((SIDE, SIDE, PIECE, 256), BF)
    longer = vmem((SIDE, SIDE, PIECE, 384), BF)
    grouped = vmem((GROUPS, 256, 256), BF)
    square = vmem((256, 256), BF)
    quarter = vmem((4, SIDE, PIECE, 256), BF)
    terms = vmem((4, 64, PIECE, 128), BF)
    wide = (D, 256)
    scratch = dict(
        xv=grouped, kv=grouped, cotv=grouped, min_ref=square, mout_ref=square,
        ts_ref=vmem((6, 2, 256), BF), tc_ref=vmem((6, 2, 256), BF), gain_ref=vmem((1, D), BF),
        up_ref=vmem((DG, 1920), BF), down_ref=vmem((DG, 1920), BF),
        outv=vmem(wide, BF), igv=vmem(wide, BF), kgv=vmem(wide, BF),
        ugv=vmem((30, DG), F32), dgv=vmem((30, DG), F32), gnv=vmem((1, 15), F32),
        eye=square, mint=square, moutt=square, twp=vmem((2, 256, 256), F32),
        xg=grouped, cotg=grouped, cotn=grouped,
        upp=vmem((GROUPS, 256, 512), BF), dnp=vmem((GROUPS, 256, 512), BF), ww=vmem((D, 2048), BF),
        acot=vmem((GROUPS, 256, 512), F32), pa=vmem((256, 512), F32), act=vmem((256, 2048), BF),
        pgr=vmem((GROUPS, 256, 512), BF), hg=grouped, ng=grouped, ngr=vmem((GROUPS, 256, 256), F32),
        hgr=grouped, acc=vmem(wide, F32), gaing=vmem((GROUPS, 8, 256), F32), rowscale=vmem((256, 128), F32),
        wsum=vmem((2, 32, 256), F32),
        src1=exchange, a1=exchange, ks=exchange, kt=exchange, ff=vmem((SIDE, SIDE, PIECE, 256), F32), sp=exchange,
        src2=exchange, m2=exchange, src3=exchange, a3=exchange, src4=longer, m4=longer,
        kgb=vmem((2, 4, SIDE, PIECE, 256), BF), kra=quarter, kgh=quarter, krb=quarter,
        kgs=vmem((SIDE, PIECE, 256), BF), kgf=exchange,
        gg=vmem((2, 4, 64, PIECE, 128), BF), r1a=terms, h1=terms, r1b=terms,
        fin=vmem((PIECE, 128), F32), rf=vmem((SIDE, PIECE, 128), F32),
        in_s=dma((19,)), out_s=dma((6,)),
        s1=dma((SIDE,)), v1=dma((SIDE,)), s2=dma((SIDE,)), v2=dma((SIDE,)),
        s3=dma((SIDE,)), v3=dma((SIDE,)), s4=dma((SIDE,)), v4=dma((SIDE,)),
        ks_s=dma((2,)), ks_v=dma, ka_s=dma((4,)), ka_v=dma((4,)), kb_s=dma((4,)), kb_v=dma((4,)),
        kr_s=dma, kr_v=dma, kc_s=dma((4,)), kc_v=dma((4,)), kf_s=dma((2,)), kf_v=dma,
        kh_s=dma((4,)), kh_v=dma((4,)), ki_s=dma((4,)), ki_v=dma((4,)),
        ga_s=dma, ga_v=dma, gb_s=dma((4,)), gb_v=dma((4,)), gf_s=dma((SIDE,)), gf_v=dma((SIDE,)),
    )
    shape = jax.ShapeDtypeStruct
    results = [shape(wide, BF)] * 3 + [shape((30, DG), F32)] * 2 + [shape((1, 15), F32)]
    held = pl.pallas_call(
        kernel,
        out_shape=results,
        in_specs=[hbm] * 10,
        out_specs=[hbm] * 6,
        scratch_shapes=scratch,
        compiler_params=pltpu.CompilerParams(
            collective_id=0, has_side_effects=True, vmem_limit_bytes=58 * 1024 * 1024
        ),
        cost_estimate=pl.CostEstimate(flops=4_000_000_000, bytes_accessed=6_000_000, transcendentals=600_000),
    )(
        inputs[0].T, cotangent[0].T, kernel_values.T, mix_in, mix_out,
        twiddle_self.transpose(1, 0, 2), twiddle_cross.transpose(1, 0, 2),
        norm_gain[None, :], up_weight, down_weight,
    )
    output, input_grad, kernel_grad, up_grad, down_grad, gain_grad = pl.pallas_call(
        settle,
        out_shape=results,
        in_specs=[hbm] * 6,
        out_specs=[hbm] * 6,
        scratch_shapes=[dma((6,))],
        compiler_params=pltpu.CompilerParams(vmem_limit_bytes=58 * 1024 * 1024),
        cost_estimate=pl.CostEstimate(flops=0, bytes_accessed=3_000_000, transcendentals=0),
    )(*held)
    return output.T[None], input_grad.T[None], kernel_grad.T, up_grad.T, down_grad.T, gain_grad[0]


def solution(mesh):
    in_specs = (
        P("dp", "seq", None),
        P("dp", "seq", None),
        P("seq", None),
        P("seq", None),
        P("seq", None),
        P(None, None, "seq"),
        P(None, None, "seq"),
        P(),
        P(),
        P(),
    )
    out_specs = (
        P("dp", "seq", None),
        P("dp", "seq", None),
        P("seq", None),
        P(None, "seq"),
        P(None, "seq"),
        P("seq"),
    )
    return jax.shard_map(local, mesh=mesh, in_specs=in_specs, out_specs=out_specs, check_vma=False)
```

```python
import jax
import jax.numpy as jnp
from jax import lax
from jax.experimental import pallas as pl
from jax.experimental.pallas import tpu as pltpu
from jax.sharding import PartitionSpec as P

MESH = pl.DeviceIdType.MESH
BF = jnp.bfloat16
F32 = jnp.float32

D = 960
GROUPS = 4
DG = 240
FFG = 480
SIDE = 8
PIECE = 16
ROOT_HALF = 0.7978845608028654
CUBIC = 0.044715
SCALE = 131072.0**-0.5
GAIN_WINDOWS = ((0, 256), (128, 512), (384, 768), (640, 960))
HIDDEN_WINDOWS = ((0, 512), (384, 1024), (896, 1536), (1408, 1920))


def dot(a, b):
    return lax.dot_general(a, b, (((1,), (0,)), ((), ())), preferred_element_type=F32)


def dot_tn(a, b):
    return lax.dot_general(a, b, (((0,), (0,)), ((), ())), preferred_element_type=F32)


def dot_nt(a, b):
    return lax.dot_general(a, b, (((1,), (1,)), ((), ())), preferred_element_type=F32)


def iotas(shape):
    return lax.broadcasted_iota(jnp.int32, shape, 0), lax.broadcasted_iota(jnp.int32, shape, 1)


def ones_where(mask):
    return jnp.where(mask, 1.0, 0.0).astype(BF)


def repeat(count, body, start=0):
    def step(index, carry):
        body(index)
        return carry

    lax.fori_loop(start, count, step, 0)


def wrapped(value):
    return lax.rem(value + 2 * SIDE, SIDE)


def await_bytes(view, sem):
    pltpu.make_async_copy(view, view, sem).wait()


def mix(values, selfs, crosses, bits, transposed):
    for k, bit in bits:
        stride = 1 << bit
        if transposed:
            scaled = [crosses(a, k) * values[a] for a in range(SIDE)]
            values = [selfs(a, k) * values[a] + scaled[a ^ stride] for a in range(SIDE)]
        else:
            values = [selfs(a, k) * values[a] + crosses(a, k) * values[a ^ stride] for a in range(SIDE)]
    return values


def kernel(
    x_hbm, cot_hbm, ker_hbm, min_hbm, mout_hbm, ts_hbm, tc_hbm, gain_hbm, up_hbm, down_hbm,
    out_hbm, ig_hbm, kg_hbm, ug_hbm, dg_hbm, gn_hbm,
    xv, kv, cotv, min_ref, mout_ref, ts_ref, tc_ref, gain_ref, up_ref, down_ref,
    outv, igv, kgv, ugv, dgv, gnv,
    eye, mint, moutt, twp, xg, cotg, cotn, upp, dnp, ww, acot, pa, act, pgr, hg, ng, ngr, hgr, acc, gaing, rowscale, wsum,
    src1, a1, ks, kt, ff, sp, src2, m2, src3, a3, src4, m4, src5, m5, twb,
    kgb, kra, kgh, krb, kgs, kgf, gg, r1a, h1, r1b, fin, rf,
    in_s, out_s, s1, v1, s2, v2, s3, v3, s4, v4, s5, v5,
    ks_s, ks_v, ka_s, ka_v, kb_s, kb_v, kr_s, kr_v, kc_s, kc_v, kf_s, kf_v, kh_s, kh_v, ki_s, ki_v,
    ga_s, ga_v, gb_s, gb_v, gf_s, gf_v,
):
    loads = []

    def load(src, dst):
        copy = pltpu.make_async_copy(src, dst, in_s.at[len(loads)])
        copy.start()
        loads.append(copy)
        return copy

    def load_groups(src, dst):
        return [load(src.at[pl.ds(g * DG, DG)], dst.at[g, pl.ds(0, DG)]) for g in range(GROUPS)]

    tw_here = [load(ts_hbm, ts_ref), load(tc_hbm, tc_ref)]
    ker_here = load_groups(ker_hbm, kv)
    x_here = [load(min_hbm, min_ref)] + load_groups(x_hbm, xv)
    rest_here = load_groups(cot_hbm, cotv)
    rest_here += [load(gain_hbm, gain_ref), load(up_hbm, up_ref), load(down_hbm, down_ref), load(mout_hbm, mout_ref)]

    me = lax.axis_index("seq")
    z, y = lax.div(me, SIDE), lax.rem(me, SIDE)
    i = lax.axis_index("dp")
    chip, core = lax.div(i, 2), lax.rem(i, 2)
    mate = i + 1 - 2 * core
    yo = wrapped(i - y)

    barrier = pltpu.get_barrier_semaphore()

    def greet_seq(step):
        pl.semaphore_signal(
            barrier, inc=1, device_id={"seq": lax.rem(me + step, 64)}, device_id_type=MESH
        )

    def greet_dp(step):
        pl.semaphore_signal(barrier, inc=1, device_id={"dp": wrapped(i + step)}, device_id_type=MESH)

    repeat(64, greet_seq, 1)
    repeat(8, greet_dp, 1)

    def send(src, dst, ssem, rsem, device):
        pltpu.make_async_remote_copy(
            src_ref=src, dst_ref=dst, send_sem=ssem, recv_sem=rsem, device_id=device, device_id_type=MESH
        ).start()

    def send_part(part, src, dst, ssem, rsem):
        def one(dz, dy):
            tz, ty = wrapped(z + dz), wrapped(y + dy)
            send(src(tz, ty), dst, ssem.at[dz], rsem, {"seq": tz * SIDE + ty})

        if part == 0:
            pltpu.make_async_copy(src(z, y), dst, rsem).start()
            one(4, 0)

        def pair(t):
            one(part, lax.rem(5 * t, SIDE))
            one((4, 7, 6, 5)[part], lax.rem(5 * t, SIDE))

        repeat(SIDE, pair, 1 if part == 0 else 0)

    def await_sent(buffer, ssem):
        await_bytes(buffer.at[0, pl.ds(0, 7)], ssem.at[0])
        for dz in range(1, SIDE):
            await_bytes(buffer.at[0], ssem.at[dz])

    def store_grouped(ref, g, value):
        split = value.reshape(SIDE, 2, PIECE, 256)
        for h in range(2):
            ref[h, :, g] = split[:, 0, :, 128 * h : 128 * h + 128]
            ref[h, :, 4 + g] = split[:, 1, :, 128 * h : 128 * h + 128]

    def load_grouped(ref, g):
        halves = [jnp.stack([ref[h, :, g], ref[h, :, 4 + g]], axis=1).reshape(256, 128) for h in range(2)]
        return jnp.concatenate(halves, axis=1)

    def slot(chip_at, core_at):
        return wrapped(2 * chip_at + core_at - y)

    def to_chips(buffer, ssem, rsem):
        send(buffer.at[yo], buffer.at[yo], ssem.at[0], rsem.at[0], {"dp": mate})

        def step_to(step):
            send(
                buffer.at[yo], buffer.at[yo], ssem.at[step], rsem.at[step],
                {"dp": 2 * lax.rem(chip + step, 4) + core},
            )

        repeat(4, step_to, 1)

    def to_mate(buffer, rsem, ssem2, rsem2):
        def step_to(step):
            held = buffer.at[slot(lax.rem(chip + 4 - step, 4), core)]
            await_bytes(held, rsem.at[step])
            send(held, held, ssem2.at[step], rsem2.at[step], {"dp": mate})

        repeat(4, step_to, 1)

    def from_mate(buffer, rsem, rsem2):
        await_bytes(buffer.at[slot(chip, 1 - core)], rsem.at[0])

        def step_from(step):
            await_bytes(buffer.at[slot(lax.rem(chip + 4 - step, 4), 1 - core)], rsem2.at[step])

        repeat(4, step_from, 1)

    r, l = iotas((256, 256))
    eye[...] = ones_where(r == l)
    twp[...] = jnp.zeros_like(twp)
    for copy in tw_here:
        copy.wait()
    for k in range(6):
        for which in range(2):
            twp[which, pl.ds(DG + k, 1)] = ts_ref[k, which : which + 1].astype(F32)
            twp[which, pl.ds(DG + 8 + k, 1)] = tc_ref[k, which : which + 1].astype(F32)
    for copy in ker_here:
        copy.wait()
    for g in range(GROUPS):
        kv[g, pl.ds(DG, PIECE)] = twp[1, pl.ds(DG, PIECE)].astype(BF)
        split = dot_nt(eye[...], kv[g]).astype(BF).reshape(SIDE, 2, PIECE, 256)
        ks[:, g] = split[:, 0]
        ks[:, 4 + g] = split[:, 1]
    columns = dot_nt(eye[...], twp[0].astype(BF))
    for copy in x_here:
        copy.wait()
    for g in range(GROUPS):
        xv[g, pl.ds(DG, PIECE)] = jnp.zeros((PIECE, 256), BF)
        store_grouped(src1, g, (dot_nt(min_ref[...], xv[g]) + columns).astype(BF))

    pl.semaphore_wait(barrier, 70)

    def share_kernel(dz):
        tz = wrapped(z + dz)
        send(ks.at[tz, yo], kt.at[y, z], ks_s.at[1], ks_v, {"seq": tz * SIDE + yo})

    repeat(SIDE, share_kernel, 1)

    @pl.when(yo != y)
    def _():
        send(ks.at[z, yo], kt.at[y, z], ks_s.at[0], ks_v, {"seq": z * SIDE + yo})

    @pl.when(yo == y)
    def _():
        pltpu.make_async_copy(ks.at[z, yo], kt.at[y, z], ks_v).start()

    def half_of(h, src, dst, ssem, rsem, at, group):
        return (lambda tz, ty: src.at[h, tz, ty], dst.at[(h,) + at], ssem.at[h], rsem.at[h, group])

    for h in (1, 0):
        first = half_of(h, src1, a1, s1, v1, (z, y), z)
        send_part(0, *first)
        send_part(1, *first)
        if h == 1:
            await_bytes(kt.at[yo], ks_v)
            to_chips(kt, ka_s, ka_v)
        send_part(2, *first)
        send_part(3, *first)

    for copy in rest_here:
        copy.wait()
    for g in range(GROUPS):
        xg[g] = dot_nt(eye[...], xv[g]).astype(BF)
        cotv[g, pl.ds(DG, PIECE)] = jnp.zeros((PIECE, 256), BF)
    mint[...] = dot_nt(eye[...], min_ref[...]).astype(BF)
    moutt[...] = dot_nt(eye[...], mout_ref[...]).astype(BF)
    for g in range(GROUPS):
        cotn[g] = dot_nt(eye[...], cotv[g]).astype(BF)
        picked = jnp.zeros((256, 256), F32)
        for part in range(GROUPS):
            j, lane = iotas((256, 256))
            picked = picked + dot(ones_where((part * DG + lane == 4 * j + g) & (lane < DG)), cotv[part])
        cotg[g] = dot_nt(eye[...], picked.astype(BF)).astype(BF)
        low, high = GAIN_WINDOWS[g]
        channel, lane = iotas((high - low, 256))
        gain_rows = jnp.broadcast_to(gain_ref[:, low:high].astype(F32), (PIECE, high - low)).astype(BF)
        gaing[g] = dot(gain_rows, ones_where((channel + low == g * DG + lane) & (lane < DG)))[0:8]
    to_mate(kt, ka_v, kb_s, kb_v)
    for g in range(GROUPS):
        low, high = HIDDEN_WINDOWS[g]
        column, hidden_unit = iotas((high - low, 512))
        chosen = (column + low == g * FFG + hidden_unit - 2 * (hidden_unit >> 5)) & ((hidden_unit & 31) < 30)
        chooser = ones_where(chosen)
        upp[g, 0:DG] = dot(up_ref[:, low:high], chooser).astype(BF)
        dnp[g, 0:DG] = dot(down_ref[:, low:high], chooser).astype(BF)
        upp[g, DG:256] = jnp.zeros((256 - DG, 512), BF)
        dnp[g, DG:256] = jnp.zeros((256 - DG, 512), BF)

    def spread_twiddles(which, p, q, slab):
        wide = slab.astype(F32)
        for k in range(6):
            twb[which, p, q, k] = jnp.broadcast_to(wide[:, 112 + k : 113 + k], (PIECE, 128))
            twb[which, p, q, 6 + k] = jnp.broadcast_to(wide[:, 120 + k : 121 + k], (PIECE, 128))

    def mixed(values, which, shards, bits, transposed):
        def selfs(a, k):
            return twb[which, shards[a][0], shards[a][1], k]

        def crosses(a, k):
            return twb[which, shards[a][0], shards[a][1], 6 + k]

        return mix(values, selfs, crosses, bits, transposed)

    low_bits = ((0, 0), (1, 1), (2, 2))
    high_bits = ((3, 0), (4, 1), (5, 2))
    low_back = tuple(reversed(low_bits))
    high_back = tuple(reversed(high_bits))

    def row_of(sz):
        return [(sz, a) for a in range(SIDE)]

    def column_of(sy):
        return [(a, sy) for a in range(SIDE)]

    def two_at_once(lines, read, which, bits, transposed, write):
        def step(t):
            groups = [lines(2 * t), lines(2 * t + 1)]
            held = [[read(p, q) for p, q in shards] for shards in groups]
            held = [mixed(values, which, shards, bits, transposed) for values, shards in zip(held, groups)]
            for shards, values in zip(groups, held):
                for (p, q), value in zip(shards, values):
                    write(p, q, value)

        repeat(SIDE // 2, step)

    def store_wide(p, q, value):
        ff[p, q] = value

    def load_wide(p, q):
        return ff[p, q]

    from_mate(kt, ka_v, kb_v)

    def spread_output_twiddles(sz):
        for p, q in row_of(sz):
            spread_twiddles(1, p, q, kt[q, p, :, 128:256])

    repeat(SIDE, spread_output_twiddles)

    for h in (1, 0):
        lanes = slice(128 * h, 128 * h + 128)

        def forward_one(step, h=h):
            sz = wrapped(z + step)
            await_bytes(a1.at[h, sz], v1.at[h, sz])
            shards = row_of(sz)
            if h == 1:
                for p, q in shards:
                    spread_twiddles(0, p, q, a1[1, p, q])
            values = mixed([a1[h, p, q].astype(F32) for p, q in shards], 0, shards, low_bits, False)
            for (p, q), value in zip(shards, values):
                ff[p, q] = value

        repeat(SIDE, forward_one)

        def weigh(p, q, value, h=h, lanes=lanes):
            rounded = value.astype(BF)
            sp[h, p, q] = rounded
            ff[p, q] = rounded.astype(F32) * kt[q, p, :, lanes].astype(F32)

        def leave(p, q, value, h=h):
            src2[h, p, q] = value.astype(BF)

        two_at_once(column_of, load_wide, 0, high_bits, False, weigh)
        two_at_once(row_of, load_wide, 1, low_bits, False, store_wide)
        two_at_once(column_of, load_wide, 1, high_bits, False, leave)
        for part in range(4):
            send_part(part, *half_of(h, src2, m2, s2, v2, (z, y), z))

    for g in range(GROUPS):
        acot[g] = dot(cotg[g], dnp[g])
        channel, j = iotas((D, 256))
        spread = ones_where((channel == 4 * j + g) & (j < DG))
        ww[:, pl.ds(g * 512, 512)] = dot(spread, dnp[g]).astype(BF)

    for h in (1, 0):
        for sz in range(SIDE):
            await_bytes(m2.at[h, sz], v2.at[h, sz])

    lane_here = lax.broadcasted_iota(jnp.int32, (256, 256), 1) < DG
    squares = jnp.zeros((256, 1), F32)
    for g in range(GROUPS):
        value = xg[g].astype(F32) + dot(mout_ref[...], load_grouped(m2, g))
        value = jnp.where(lane_here, value, 0.0).astype(BF)
        hg[g] = value
        wide = value.astype(F32)
        squares = squares + jnp.sum(wide * wide, axis=1, keepdims=True)
    scale_column = lax.rsqrt(squares * (1.0 / D) + 1e-06)
    rowscale[...] = jnp.broadcast_to(scale_column, (256, 128))

    for g in range(GROUPS):
        wide = hg[g].astype(F32)
        ng[g] = (wide * rowscale[:, 0:1] * gaing[g, 0:1]).astype(BF)
        pa[...] = dot(ng[g], upp[g])

        def activate(tile, g=g):
            rows = pl.ds(pl.multiple_of(tile * 64, 64), 64)
            p = pa[rows]
            square = p * p
            tangent = jnp.tanh(p * (ROOT_HALF + (ROOT_HALF * CUBIC) * square))
            half_more = 0.5 + 0.5 * tangent
            act[rows, pl.ds(g * 512, 512)] = (p * half_more).astype(BF)
            inner = ROOT_HALF + (3.0 * ROOT_HALF * CUBIC) * square
            slope = half_more + 0.5 * p * (1.0 - tangent * tangent) * inner
            pgr[g, rows] = (acot[g, rows] * slope).astype(BF)

        repeat(4, activate)
        ngr[g] = dot_nt(pgr[g], upp[g])

    means = jnp.zeros((256, 1), F32)
    for g in range(GROUPS):
        means = means + jnp.sum(ngr[g] * gaing[g, 0:1] * hg[g].astype(F32), axis=1, keepdims=True)
    scale_column = rowscale[:, 0:1]
    means = means * (1.0 / D) * scale_column * scale_column * scale_column
    for g in range(GROUPS):
        gained = ngr[g] * gaing[g, 0:1]
        hgr[g] = (cotn[g].astype(F32) + scale_column * gained - hg[g].astype(F32) * means).astype(BF)
        store_grouped(src3, g, dot(moutt[...], hgr[g]).astype(BF))
    for h in (1, 0):
        for part in range(4):
            send_part(part, *half_of(h, src3, a3, s3, v3, (y, z), y))

    row_here = (lax.broadcasted_iota(jnp.int32, (512, 256), 0) & 31) == 30
    for g in range(GROUPS):
        gain_term = jnp.sum(ngr[g] * hg[g].astype(F32) * rowscale[:, 0:1], axis=0, keepdims=True)
        up_term = jnp.where(row_here, gain_term, dot_tn(pgr[g], ng[g]))
        down_term = dot_tn(act[:, pl.ds(g * 512, 512)], cotg[g])
        for kind, term in ((0, up_term), (1, down_term)):
            split = term.astype(BF).reshape(16, 2, PIECE, 256)
            for half in range(2):
                for side in range(2):
                    gg[side, 2 * kind + half, pl.ds(g * 16, 16)] = split[:, half, :, side * 128 : side * 128 + 128]

    send(gg.at[1 - core], r1a, ga_s, ga_v, {"dp": mate})

    await_bytes(r1a, ga_v)

    def pair_sum(step):
        for slab in range(4):
            part = pl.ds(pl.multiple_of(step * 8, 8), 8)
            both = gg[core, slab, part].astype(F32) + r1a[slab, part].astype(F32)
            h1[slab, part] = both.astype(BF)

    repeat(8, pair_sum)

    def spread_terms(step):
        other = lax.rem(chip + step, 4)
        send(h1.at[other], r1b.at[chip], gb_s.at[step], gb_v.at[step], {"dp": other * 2 + core})

    repeat(4, spread_terms, 1)

    others = [lax.rem(chip + step, 4) for step in (1, 2, 3)]

    for h in (1, 0):
        lanes = slice(128 * h, 128 * h + 128)

        def backward_one(step, h=h):
            sy = wrapped(y + step)
            await_bytes(a3.at[h, sy], v3.at[h, sy])
            shards = column_of(sy)
            values = mixed([a3[h, q, p].astype(F32) for p, q in shards], 1, shards, high_back, True)
            for (p, q), value in zip(shards, values):
                ff[p, q] = value

        repeat(SIDE, backward_one)

        def weigh_back(p, q, value, h=h, lanes=lanes):
            wide = value.astype(BF).astype(F32)
            owner = wrapped(q + y)
            kgb[lax.rem(owner, 2), lax.div(owner, 2), p, :, lanes] = (sp[h, p, q].astype(F32) * wide).astype(BF)
            ff[p, q] = wide * kt[q, p, :, lanes].astype(F32)

        def leave_back(p, q, value, h=h):
            src4[h, p, q] = value.astype(BF)

        two_at_once(row_of, load_wide, 1, low_back, True, weigh_back)
        if h == 0:
            send(kgb.at[1 - core], kra, kr_s, kr_v, {"dp": mate})
        two_at_once(column_of, load_wide, 0, high_back, True, store_wide)
        two_at_once(row_of, load_wide, 0, low_back, True, leave_back)
        last = half_of(h, src4, m4, s4, v4, (z, y), z)
        send_part(0, *last)
        send_part(1, *last)
        if h == 1:
            send_part(2, *last)
            send_part(3, *last)

    await_bytes(kra, kr_v)

    def kernel_pair(sz):
        for at in range(4):
            kgh[at, sz] = (kgb[core, at, sz].astype(F32) + kra[at, sz].astype(F32)).astype(BF)

    repeat(SIDE, kernel_pair)

    def spread_kernel_terms(step):
        other = lax.rem(chip + step, 4)
        send(kgh.at[other], krb.at[chip], kc_s.at[step], kc_v.at[step], {"dp": other * 2 + core})

    repeat(4, spread_kernel_terms, 1)
    send_part(2, *last)
    send_part(3, *last)

    def terms_here(step):
        await_bytes(r1b.at[lax.rem(chip + 4 - step, 4)], gb_v.at[step])

    repeat(4, terms_here, 1)

    def chip_sum(sz):
        part = pl.ds(pl.multiple_of(sz * 8, 8), 8)
        four = h1[chip, part].astype(F32)
        for other in others:
            four = four + r1b[other, part].astype(F32)
        src5[sz] = four.astype(BF)

    repeat(SIDE, chip_sum)

    def kernel_terms_here(step):
        await_bytes(krb.at[lax.rem(chip + 4 - step, 4)], kc_v.at[step])

    repeat(4, kernel_terms_here, 1)

    def kernel_sum(sz):
        four = kgh[chip, sz].astype(F32)
        for other in others:
            four = four + krb[other, sz].astype(F32)
        kgs[sz] = four.astype(BF)

    repeat(SIDE, kernel_sum)

    def return_kernel(dz):
        tz = wrapped(z + dz)
        send(kgs.at[tz], kgf.at[y, z], kf_s.at[1], kf_v, {"seq": tz * SIDE + yo})

    repeat(SIDE, return_kernel, 1)

    @pl.when(yo != y)
    def _():
        send(kgs.at[z], kgf.at[y, z], kf_s.at[0], kf_v, {"seq": z * SIDE + yo})

    @pl.when(yo == y)
    def _():
        pltpu.make_async_copy(kgs.at[z], kgf.at[y, z], kf_v).start()

    for part in range(4):
        send_part(part, lambda tz, ty: src5.at[tz, ty], m5.at[z, y], s5, v5.at[z])

    acc[...] = dot_nt(ww[...], act[...])
    for g in range(GROUPS):
        rows = pl.ds(g * DG, DG)
        outv[rows] = (acc[rows] + dot_nt(eye[0:DG], hg[g])).astype(BF)
    pltpu.make_async_copy(outv, out_hbm, out_s.at[0]).start()

    await_bytes(kgf.at[yo], kf_v)
    to_chips(kgf, kh_s, kh_v)
    for h in (1, 0):
        for sz in range(SIDE):
            await_bytes(m4.at[h, sz], v4.at[h, sz])
    for g in range(GROUPS):
        value = (hgr[g].astype(F32) + dot(mint[...], load_grouped(m4, g))).astype(BF)
        igv[pl.ds(g * DG, DG)] = dot_nt(eye[0:DG], value).astype(BF)
    pltpu.make_async_copy(igv, ig_hbm, out_s.at[2]).start()

    to_mate(kgf, kh_v, ki_s, ki_v)

    shard_sum = jnp.zeros((PIECE, 128), F32)
    for sz in range(SIDE):
        await_bytes(m5.at[sz], v5.at[sz])
        for sy in range(SIDE):
            shard_sum = shard_sum + m5[sz, sy].astype(F32)
    shard_sum = shard_sum * SCALE
    fin[...] = shard_sum
    rf[i] = shard_sum

    def spread_grads(step):
        send(fin, rf.at[i], gf_s.at[step], gf_v.at[step], {"dp": wrapped(i + step)})

    repeat(SIDE, spread_grads, 1)

    from_mate(kgf, kh_v, ki_v)
    for g in range(GROUPS):
        held = jnp.stack([kgf[g], kgf[4 + g]], axis=1).reshape(256, 256)
        kgv[pl.ds(g * DG, DG)] = dot_nt(eye[0:DG], held).astype(BF)
    pltpu.make_async_copy(kgv, kg_hbm, out_s.at[1]).start()

    def grads_here(step):
        await_bytes(rf.at[wrapped(i - step)], gf_v.at[step])

    repeat(SIDE, grads_here, 1)
    for share in range(SIDE):
        kind, half, side = share // 4, (share // 2) % 2, share % 2
        wsum[kind, pl.ds(half * PIECE, PIECE), pl.ds(side * 128, 128)] = rf[share]
    ugv[...] = wsum[0, 0:30, 0:DG]
    dgv[...] = wsum[1, 0:30, 0:DG]
    j, lane = iotas((256, 128))
    picker = jnp.where(j == lane + 15 * lax.rem(me, 16), 1.0, 0.0)
    gains = jnp.broadcast_to(wsum[0, 30:31], (8, 256))
    picked = lax.dot_general(
        gains, picker, (((1,), (0,)), ((), ())), precision=lax.Precision.HIGHEST, preferred_element_type=F32
    )
    gnv[...] = picked[0:1, 0:15]
    pltpu.make_async_copy(ugv, ug_hbm, out_s.at[3]).start()
    pltpu.make_async_copy(dgv, dg_hbm, out_s.at[4]).start()
    pltpu.make_async_copy(gnv, gn_hbm, out_s.at[5]).start()

    for buffer, sem in ((src1, s1), (src2, s2), (src3, s3), (src4, s4)):
        for h in range(2):
            await_sent(buffer.at[h], sem.at[h])
    await_sent(src5, s5)
    await_bytes(ks.at[0, pl.ds(0, 7)], ks_s.at[1])
    await_bytes(kgs.at[pl.ds(0, 7)], kf_s.at[1])

    @pl.when(yo != y)
    def _():
        await_bytes(ks.at[0, 0], ks_s.at[0])
        await_bytes(kgs.at[0], kf_s.at[0])

    await_bytes(kt.at[0], ka_s.at[0])
    await_bytes(kgf.at[0], kh_s.at[0])
    await_bytes(r1a, ga_s)
    await_bytes(kra, kr_s)

    def chips_left(step):
        await_bytes(kt.at[0], ka_s.at[step])
        await_bytes(kt.at[0], kb_s.at[step])
        await_bytes(kgf.at[0], kh_s.at[step])
        await_bytes(kgf.at[0], ki_s.at[step])
        await_bytes(kgh.at[0], kc_s.at[step])
        await_bytes(h1.at[0], gb_s.at[step])

    repeat(4, chips_left, 1)

    def grads_left(step):
        await_bytes(fin, gf_s.at[step])

    repeat(SIDE, grads_left, 1)
    outs = ((outv, out_hbm), (kgv, kg_hbm), (igv, ig_hbm), (ugv, ug_hbm), (dgv, dg_hbm), (gnv, gn_hbm))
    for index, (held, there) in enumerate(outs):
        pltpu.make_async_copy(held, there, out_s.at[index]).wait()


def settle(*refs):
    source, there, held, sems = refs[:6], refs[6:12], refs[12:18], refs[18]
    loads = [pltpu.make_async_copy(source[index], held[index], sems.at[0, index]) for index in range(6)]
    stores = [pltpu.make_async_copy(held[index], there[index], sems.at[1, index]) for index in range(6)]
    for copy in loads:
        copy.start()
    for load, store in zip(loads, stores):
        load.wait()
        store.start()
    for copy in stores:
        copy.wait()


def local(
    inputs, cotangent, kernel_values, mix_in, mix_out, twiddle_self, twiddle_cross, norm_gain, up_weight, down_weight
):
    hbm = pl.BlockSpec(memory_space=pltpu.HBM)
    dma = pltpu.SemaphoreType.DMA
    vmem = pltpu.VMEM
    exchange = vmem((SIDE, SIDE, PIECE, 256), BF)
    halves = vmem((2, SIDE, SIDE, PIECE, 128), BF)
    part = vmem((SIDE, SIDE, PIECE, 128), BF)
    both = dma((2, SIDE))
    grouped = vmem((GROUPS, 256, 256), BF)
    square = vmem((256, 256), BF)
    quarter = vmem((4, SIDE, PIECE, 256), BF)
    terms = vmem((4, 64, PIECE, 128), BF)
    wide = (D, 256)
    scratch = dict(
        xv=grouped, kv=grouped, cotv=grouped, min_ref=square, mout_ref=square,
        ts_ref=vmem((6, 2, 256), BF), tc_ref=vmem((6, 2, 256), BF), gain_ref=vmem((1, D), BF),
        up_ref=vmem((DG, 1920), BF), down_ref=vmem((DG, 1920), BF),
        outv=vmem(wide, BF), igv=vmem(wide, BF), kgv=vmem(wide, BF),
        ugv=vmem((30, DG), F32), dgv=vmem((30, DG), F32), gnv=vmem((1, 15), F32),
        eye=square, mint=square, moutt=square, twp=vmem((2, 256, 256), F32),
        xg=grouped, cotg=grouped, cotn=grouped,
        upp=vmem((GROUPS, 256, 512), BF), dnp=vmem((GROUPS, 256, 512), BF), ww=vmem((D, 2048), BF),
        acot=vmem((GROUPS, 256, 512), F32), pa=vmem((256, 512), F32), act=vmem((256, 2048), BF),
        pgr=vmem((GROUPS, 256, 512), BF), hg=grouped, ng=grouped, ngr=vmem((GROUPS, 256, 256), F32),
        hgr=grouped, acc=vmem(wide, F32), gaing=vmem((GROUPS, 8, 256), F32), rowscale=vmem((256, 128), F32),
        wsum=vmem((2, 32, 256), F32),
        src1=halves, a1=halves, ks=exchange, kt=exchange, ff=vmem((SIDE, SIDE, PIECE, 128), F32), sp=halves,
        src2=halves, m2=halves, src3=halves, a3=halves, src4=halves, m4=halves, src5=part, m5=part,
        twb=vmem((2, SIDE, SIDE, 12, PIECE, 128), F32),
        kgb=vmem((2, 4, SIDE, PIECE, 256), BF), kra=quarter, kgh=quarter, krb=quarter,
        kgs=vmem((SIDE, PIECE, 256), BF), kgf=exchange,
        gg=vmem((2, 4, 64, PIECE, 128), BF), r1a=terms, h1=terms, r1b=terms,
        fin=vmem((PIECE, 128), F32), rf=vmem((SIDE, PIECE, 128), F32),
        in_s=dma((19,)), out_s=dma((6,)),
        s1=both, v1=both, s2=both, v2=both, s3=both, v3=both, s4=both, v4=both, s5=dma((SIDE,)), v5=dma((SIDE,)),
        ks_s=dma((2,)), ks_v=dma, ka_s=dma((4,)), ka_v=dma((4,)), kb_s=dma((4,)), kb_v=dma((4,)),
        kr_s=dma, kr_v=dma, kc_s=dma((4,)), kc_v=dma((4,)), kf_s=dma((2,)), kf_v=dma,
        kh_s=dma((4,)), kh_v=dma((4,)), ki_s=dma((4,)), ki_v=dma((4,)),
        ga_s=dma, ga_v=dma, gb_s=dma((4,)), gb_v=dma((4,)), gf_s=dma((SIDE,)), gf_v=dma((SIDE,)),
    )
    shape = jax.ShapeDtypeStruct
    results = [shape(wide, BF)] * 3 + [shape((30, DG), F32)] * 2 + [shape((1, 15), F32)]
    held = pl.pallas_call(
        kernel,
        out_shape=results,
        in_specs=[hbm] * 10,
        out_specs=[hbm] * 6,
        scratch_shapes=scratch,
        compiler_params=pltpu.CompilerParams(
            collective_id=0, has_side_effects=True, vmem_limit_bytes=58 * 1024 * 1024
        ),
        cost_estimate=pl.CostEstimate(flops=4_000_000_000, bytes_accessed=6_000_000, transcendentals=600_000),
    )(
        inputs[0].T, cotangent[0].T, kernel_values.T, mix_in, mix_out,
        twiddle_self.transpose(1, 0, 2), twiddle_cross.transpose(1, 0, 2),
        norm_gain[None, :], up_weight, down_weight,
    )
    output, input_grad, kernel_grad, up_grad, down_grad, gain_grad = pl.pallas_call(
        settle,
        out_shape=results,
        in_specs=[hbm] * 6,
        out_specs=[hbm] * 6,
        scratch_shapes=[vmem(result.shape, result.dtype) for result in results] + [dma((2, 6))],
        compiler_params=pltpu.CompilerParams(vmem_limit_bytes=58 * 1024 * 1024),
        cost_estimate=pl.CostEstimate(flops=0, bytes_accessed=3_000_000, transcendentals=0),
    )(*held)
    return output.T[None], input_grad.T[None], kernel_grad.T, up_grad.T, down_grad.T, gain_grad[0]


def solution(mesh):
    in_specs = (
        P("dp", "seq", None),
        P("dp", "seq", None),
        P("seq", None),
        P("seq", None),
        P("seq", None),
        P(None, None, "seq"),
        P(None, None, "seq"),
        P(),
        P(),
        P(),
    )
    out_specs = (
        P("dp", "seq", None),
        P("dp", "seq", None),
        P("seq", None),
        P(None, "seq"),
        P(None, "seq"),
        P("seq"),
    )
    return jax.shard_map(local, mesh=mesh, in_specs=in_specs, out_specs=out_specs, check_vma=False)
```

```python
import jax
import jax.numpy as jnp
from jax import lax
from jax.experimental import pallas as pl
from jax.experimental.pallas import tpu as pltpu
from jax.sharding import PartitionSpec as P

MESH = pl.DeviceIdType.MESH
BF = jnp.bfloat16
F32 = jnp.float32

D = 960
GROUPS = 4
DG = 240
FFG = 480
SIDE = 8
PIECE = 16
ROOT_HALF = 0.7978845608028654
CUBIC = 0.044715
SCALE = 131072.0**-0.5
GAIN_WINDOWS = ((0, 256), (128, 512), (384, 768), (640, 960))
HIDDEN_WINDOWS = ((0, 512), (384, 1024), (896, 1536), (1408, 1920))


def dot(a, b):
    return lax.dot_general(a, b, (((1,), (0,)), ((), ())), preferred_element_type=F32)


def dot_tn(a, b):
    return lax.dot_general(a, b, (((0,), (0,)), ((), ())), preferred_element_type=F32)


def dot_nt(a, b):
    return lax.dot_general(a, b, (((1,), (1,)), ((), ())), preferred_element_type=F32)


def iotas(shape):
    return lax.broadcasted_iota(jnp.int32, shape, 0), lax.broadcasted_iota(jnp.int32, shape, 1)


def ones_where(mask):
    return jnp.where(mask, 1.0, 0.0).astype(BF)


def repeat(count, body, start=0):
    def step(index, carry):
        body(index)
        return carry

    lax.fori_loop(start, count, step, 0)


def wrapped(value):
    return lax.rem(value + 2 * SIDE, SIDE)


def await_bytes(view, sem):
    pltpu.make_async_copy(view, view, sem).wait()


def mix(values, selfs, crosses, bits, transposed):
    for k, bit in bits:
        stride = 1 << bit
        if transposed:
            scaled = [crosses(a, k) * values[a] for a in range(SIDE)]
            values = [selfs(a, k) * values[a] + scaled[a ^ stride] for a in range(SIDE)]
        else:
            values = [selfs(a, k) * values[a] + crosses(a, k) * values[a ^ stride] for a in range(SIDE)]
    return values


def kernel(
    x_hbm, cot_hbm, ker_hbm, min_hbm, mout_hbm, ts_hbm, tc_hbm, gain_hbm, up_hbm, down_hbm,
    out_hbm, ig_hbm, kg_hbm, ug_hbm, dg_hbm, gn_hbm,
    xv, kv, cotv, min_ref, mout_ref, ts_ref, tc_ref, gain_ref, up_ref, down_ref,
    outv, igv, kgv, ugv, dgv, gnv,
    eye, mint, moutt, twp, xg, cotg, cotn, upp, dnp, ww, acot, pa, act, pgr, hg, ng, ngr, hgr, acc, gaing, rowscale, wsum,
    src1, a1, ks, kt, ff, sp, src2, m2, src3, a3, src4, m4, twb, pa1, pa2, pa3, pb1, pb2, pb3, pc,
    kgb, kra, kgh, krb, kgs, kgf, gg, r1a, h1, r1b, fin, rf,
    in_s, out_s, s1, v1, s2, v2, s3, v3, s4, v4, pa_s, pa_v, pb_s, pb_v, pc_s, pc_v, pd_s,
    ks_s, ks_v, ka_s, ka_v, kb_s, kb_v, kr_s, kr_v, kc_s, kc_v, kf_s, kf_v, kh_s, kh_v, ki_s, ki_v,
    ga_s, ga_v, gb_s, gb_v, gf_s, gf_v,
):
    loads = []

    def load(src, dst):
        copy = pltpu.make_async_copy(src, dst, in_s.at[len(loads)])
        copy.start()
        loads.append(copy)
        return copy

    def load_groups(src, dst):
        return [load(src.at[pl.ds(g * DG, DG)], dst.at[g, pl.ds(0, DG)]) for g in range(GROUPS)]

    tw_here = [load(ts_hbm, ts_ref), load(tc_hbm, tc_ref)]
    ker_here = load_groups(ker_hbm, kv)
    x_here = [load(min_hbm, min_ref)] + load_groups(x_hbm, xv)
    rest_here = load_groups(cot_hbm, cotv)
    rest_here += [load(gain_hbm, gain_ref), load(up_hbm, up_ref), load(down_hbm, down_ref), load(mout_hbm, mout_ref)]

    me = lax.axis_index("seq")
    z, y = lax.div(me, SIDE), lax.rem(me, SIDE)
    i = lax.axis_index("dp")
    chip, core = lax.div(i, 2), lax.rem(i, 2)
    mate = i + 1 - 2 * core
    yo = wrapped(i - y)

    barrier = pltpu.get_barrier_semaphore()

    def greet_seq(step):
        pl.semaphore_signal(
            barrier, inc=1, device_id={"seq": lax.rem(me + step, 64)}, device_id_type=MESH
        )

    def greet_dp(step):
        pl.semaphore_signal(barrier, inc=1, device_id={"dp": wrapped(i + step)}, device_id_type=MESH)

    repeat(64, greet_seq, 1)
    repeat(8, greet_dp, 1)

    def send(src, dst, ssem, rsem, device):
        pltpu.make_async_remote_copy(
            src_ref=src, dst_ref=dst, send_sem=ssem, recv_sem=rsem, device_id=device, device_id_type=MESH
        ).start()

    def send_part(part, src, dst, ssem, rsem):
        offsets = ((3, 5, 1, 7), (2, 6, 4, 0))[part]

        def one(dz, dy):
            tz, ty = wrapped(z + dz), wrapped(y + dy)
            send(src(tz, ty), dst, ssem.at[dz], rsem, {"seq": tz * SIDE + ty})

        def pair(t):
            for dy in (3 - t, 5 + t):
                for dz in offsets:
                    one(dz, dy)

        repeat(3, pair)
        for dy in (4, 0):
            for dz in offsets:
                if (dz, dy) != (0, 0):
                    one(dz, dy)
        if part == 1:
            pltpu.make_async_copy(src(z, y), dst, rsem).start()

    def await_sent(buffer, ssem):
        await_bytes(buffer.at[0, pl.ds(0, 7)], ssem.at[0])
        for dz in range(1, SIDE):
            await_bytes(buffer.at[0], ssem.at[dz])

    def store_half(ref, h, pair, value):
        for side in range(2):
            split = value[:, 128 * side : 128 * side + 128].reshape(SIDE, 2, PIECE, 128)
            ref[h, :, 2 * pair + side] = split[:, 0]
            ref[h, :, 4 + 2 * pair + side] = split[:, 1]

    def load_half(ref, h, pair):
        groups = (2 * pair, 2 * pair + 1)
        return jnp.concatenate(
            [jnp.stack([ref[h, :, g], ref[h, :, 4 + g]], axis=1).reshape(256, 128) for g in groups], axis=1
        )

    def half_lanes(ref, h, pair):
        return jnp.concatenate([ref[2 * pair + side, :, 128 * h : 128 * h + 128] for side in range(2)], axis=1)

    def slot(chip_at, core_at):
        return wrapped(2 * chip_at + core_at - y)

    def to_chips(buffer, ssem, rsem):
        send(buffer.at[yo], buffer.at[yo], ssem.at[0], rsem.at[0], {"dp": mate})

        def step_to(step):
            send(
                buffer.at[yo], buffer.at[yo], ssem.at[step], rsem.at[step],
                {"dp": 2 * lax.rem(chip + step, 4) + core},
            )

        repeat(4, step_to, 1)

    def to_mate(buffer, rsem, ssem2, rsem2):
        def step_to(step):
            held = buffer.at[slot(lax.rem(chip + 4 - step, 4), core)]
            await_bytes(held, rsem.at[step])
            send(held, held, ssem2.at[step], rsem2.at[step], {"dp": mate})

        repeat(4, step_to, 1)

    def from_mate(buffer, rsem, rsem2):
        await_bytes(buffer.at[slot(chip, 1 - core)], rsem.at[0])

        def step_from(step):
            await_bytes(buffer.at[slot(lax.rem(chip + 4 - step, 4), 1 - core)], rsem2.at[step])

        repeat(4, step_from, 1)

    r, l = iotas((256, 256))
    eye[...] = ones_where(r == l)
    twp[...] = jnp.zeros_like(twp)
    for copy in tw_here:
        copy.wait()
    for k in range(6):
        for which in range(2):
            twp[which, pl.ds(DG + k, 1)] = ts_ref[k, which : which + 1].astype(F32)
            twp[which, pl.ds(DG + 8 + k, 1)] = tc_ref[k, which : which + 1].astype(F32)
    for copy in ker_here:
        copy.wait()
    for g in range(GROUPS):
        kv[g, pl.ds(DG, PIECE)] = twp[1, pl.ds(DG, PIECE)].astype(BF)
        split = dot_nt(eye[...], kv[g]).astype(BF).reshape(SIDE, 2, PIECE, 256)
        ks[:, g] = split[:, 0]
        ks[:, 4 + g] = split[:, 1]
    columns = dot_nt(eye[...], twp[0].astype(BF))[:, 128:256]
    for copy in x_here:
        copy.wait()
    for g in range(GROUPS):
        xv[g, pl.ds(DG, PIECE)] = jnp.zeros((PIECE, 256), BF)

    def premix(h):
        for pair in range(2):
            rows = jnp.concatenate([xv[2 * pair + side, 128 * h : 128 * h + 128] for side in range(2)], axis=0)
            value = dot_nt(min_ref[...], rows)
            if h == 1:
                value = value + jnp.concatenate([columns, columns], axis=1)
            store_half(src1, h, pair, value.astype(BF))

    premix(1)
    pl.semaphore_wait(barrier, 70)

    def share_kernel(dz):
        tz = wrapped(z + dz)
        send(ks.at[tz, yo], kt.at[y, z], ks_s.at[1], ks_v, {"seq": tz * SIDE + yo})

    repeat(SIDE, share_kernel, 1)

    @pl.when(yo != y)
    def _():
        send(ks.at[z, yo], kt.at[y, z], ks_s.at[0], ks_v, {"seq": z * SIDE + yo})

    @pl.when(yo == y)
    def _():
        pltpu.make_async_copy(ks.at[z, yo], kt.at[y, z], ks_v).start()

    def half_of(h, src, dst, ssem, rsem, at, group):
        return (lambda tz, ty: src.at[h, tz, ty], dst.at[(h,) + at], ssem.at[h], rsem.at[h, group])

    for h in (1, 0):
        first = half_of(h, src1, a1, s1, v1, (z, y), z)
        if h == 0:
            premix(0)
        send_part(0, *first)
        if h == 1:
            await_bytes(kt.at[yo], ks_v)
            to_chips(kt, ka_s, ka_v)
        send_part(1, *first)

    for copy in rest_here:
        copy.wait()
    for g in range(GROUPS):
        xg[g] = dot_nt(eye[...], xv[g]).astype(BF)
        cotv[g, pl.ds(DG, PIECE)] = jnp.zeros((PIECE, 256), BF)
    mint[...] = dot_nt(eye[...], min_ref[...]).astype(BF)
    moutt[...] = dot_nt(eye[...], mout_ref[...]).astype(BF)
    for g in range(GROUPS):
        cotn[g] = dot_nt(eye[...], cotv[g]).astype(BF)
        picked = jnp.zeros((256, 256), F32)
        for part in range(GROUPS):
            j, lane = iotas((256, 256))
            picked = picked + dot(ones_where((part * DG + lane == 4 * j + g) & (lane < DG)), cotv[part])
        cotg[g] = dot_nt(eye[...], picked.astype(BF)).astype(BF)
        low, high = GAIN_WINDOWS[g]
        channel, lane = iotas((high - low, 256))
        gain_rows = jnp.broadcast_to(gain_ref[:, low:high].astype(F32), (PIECE, high - low)).astype(BF)
        gaing[g] = dot(gain_rows, ones_where((channel + low == g * DG + lane) & (lane < DG)))[0:8]
    to_mate(kt, ka_v, kb_s, kb_v)
    for g in range(GROUPS):
        low, high = HIDDEN_WINDOWS[g]
        column, hidden_unit = iotas((high - low, 512))
        chosen = (column + low == g * FFG + hidden_unit - 2 * (hidden_unit >> 5)) & ((hidden_unit & 31) < 30)
        chooser = ones_where(chosen)
        upp[g, 0:DG] = dot(up_ref[:, low:high], chooser).astype(BF)
        dnp[g, 0:DG] = dot(down_ref[:, low:high], chooser).astype(BF)
        upp[g, DG:256] = jnp.zeros((256 - DG, 512), BF)
        dnp[g, DG:256] = jnp.zeros((256 - DG, 512), BF)

    def spread_twiddles(which, p, q, slab):
        wide = slab.astype(F32)
        for k in range(6):
            twb[which, p, q, k] = jnp.broadcast_to(wide[:, 112 + k : 113 + k], (PIECE, 128))
            twb[which, p, q, 6 + k] = jnp.broadcast_to(wide[:, 120 + k : 121 + k], (PIECE, 128))

    def mixed(values, which, shards, bits, transposed):
        def selfs(a, k):
            return twb[which, shards[a][0], shards[a][1], k]

        def crosses(a, k):
            return twb[which, shards[a][0], shards[a][1], 6 + k]

        return mix(values, selfs, crosses, bits, transposed)

    low_bits = ((0, 0), (1, 1), (2, 2))
    high_bits = ((3, 0), (4, 1), (5, 2))
    low_back = tuple(reversed(low_bits))
    high_back = tuple(reversed(high_bits))

    def row_of(sz):
        return [(sz, a) for a in range(SIDE)]

    def column_of(sy):
        return [(a, sy) for a in range(SIDE)]

    def two_at_once(lines, read, which, bits, transposed, write):
        def step(t):
            groups = [lines(2 * t), lines(2 * t + 1)]
            held = [[read(p, q) for p, q in shards] for shards in groups]
            held = [mixed(values, which, shards, bits, transposed) for values, shards in zip(held, groups)]
            for shards, values in zip(groups, held):
                for (p, q), value in zip(shards, values):
                    write(p, q, value)

        repeat(SIDE // 2, step)

    def store_wide(p, q, value):
        ff[p, q] = value

    def load_wide(p, q):
        return ff[p, q]

    from_mate(kt, ka_v, kb_v)

    def spread_output_twiddles(sz):
        for p, q in row_of(sz):
            spread_twiddles(1, p, q, kt[q, p, :, 128:256])

    repeat(SIDE, spread_output_twiddles)

    for h in (1, 0):
        lanes = slice(128 * h, 128 * h + 128)

        def forward_one(step, h=h):
            sz = wrapped(z + step)
            await_bytes(a1.at[h, sz], v1.at[h, sz])
            shards = row_of(sz)
            if h == 1:
                for p, q in shards:
                    spread_twiddles(0, p, q, a1[1, p, q])
            values = mixed([a1[h, p, q].astype(F32) for p, q in shards], 0, shards, low_bits, False)
            for (p, q), value in zip(shards, values):
                ff[p, q] = value

        repeat(SIDE, forward_one)

        def weigh(p, q, value, h=h, lanes=lanes):
            rounded = value.astype(BF)
            sp[h, p, q] = rounded
            ff[p, q] = rounded.astype(F32) * kt[q, p, :, lanes].astype(F32)

        def leave(p, q, value, h=h):
            src2[h, p, q] = value.astype(BF)

        two_at_once(column_of, load_wide, 0, high_bits, False, weigh)
        two_at_once(row_of, load_wide, 1, low_bits, False, store_wide)
        two_at_once(column_of, load_wide, 1, high_bits, False, leave)
        for part in range(2):
            send_part(part, *half_of(h, src2, m2, s2, v2, (z, y), z))

    for g in range(GROUPS):
        acot[g] = dot(cotg[g], dnp[g])
        channel, j = iotas((D, 256))
        spread = ones_where((channel == 4 * j + g) & (j < DG))
        ww[:, pl.ds(g * 512, 512)] = dot(spread, dnp[g]).astype(BF)

    lane_here = (lax.broadcasted_iota(jnp.int32, (256, 256), 1) & 127) < DG - 128
    squares = jnp.zeros((256, 1), F32)
    for h in (1, 0):
        for sz in range(SIDE):
            await_bytes(m2.at[h, sz], v2.at[h, sz])
        for pair in range(2):
            value = half_lanes(xg, h, pair).astype(F32) + dot(mout_ref[...], load_half(m2, h, pair))
            if h == 1:
                value = jnp.where(lane_here, value, 0.0)
            value = value.astype(BF)
            for side in range(2):
                hg[2 * pair + side, :, 128 * h : 128 * h + 128] = value[:, 128 * side : 128 * side + 128]
            wide = value.astype(F32)
            squares = squares + jnp.sum(wide * wide, axis=1, keepdims=True)
    scale_column = lax.rsqrt(squares * (1.0 / D) + 1e-06)
    rowscale[...] = jnp.broadcast_to(scale_column, (256, 128))

    for g in range(GROUPS):
        wide = hg[g].astype(F32)
        ng[g] = (wide * rowscale[:, 0:1] * gaing[g, 0:1]).astype(BF)
        pa[...] = dot(ng[g], upp[g])

        def activate(tile, g=g):
            rows = pl.ds(pl.multiple_of(tile * 64, 64), 64)
            p = pa[rows]
            square = p * p
            tangent = jnp.tanh(p * (ROOT_HALF + (ROOT_HALF * CUBIC) * square))
            half_more = 0.5 + 0.5 * tangent
            act[rows, pl.ds(g * 512, 512)] = (p * half_more).astype(BF)
            inner = ROOT_HALF + (3.0 * ROOT_HALF * CUBIC) * square
            slope = half_more + 0.5 * p * (1.0 - tangent * tangent) * inner
            pgr[g, rows] = (acot[g, rows] * slope).astype(BF)

        repeat(4, activate)
        ngr[g] = dot_nt(pgr[g], upp[g])

    means = jnp.zeros((256, 1), F32)
    for g in range(GROUPS):
        means = means + jnp.sum(ngr[g] * gaing[g, 0:1] * hg[g].astype(F32), axis=1, keepdims=True)
    scale_column = rowscale[:, 0:1]
    means = means * (1.0 / D) * scale_column * scale_column * scale_column
    for h in (1, 0):
        lanes = slice(128 * h, 128 * h + 128)
        for pair in range(2):
            for g in (2 * pair, 2 * pair + 1):
                gained = ngr[g, :, lanes] * gaing[g, 0:1, lanes]
                wide = hg[g, :, lanes].astype(F32)
                hgr[g, :, lanes] = (cotn[g, :, lanes].astype(F32) + scale_column * gained - wide * means).astype(BF)
            store_half(src3, h, pair, dot(moutt[...], half_lanes(hgr, h, pair)).astype(BF))
        for part in range(2):
            send_part(part, *half_of(h, src3, a3, s3, v3, (y, z), y))

    row_here = (lax.broadcasted_iota(jnp.int32, (512, 256), 0) & 31) == 30
    for g in range(GROUPS):
        gain_term = jnp.sum(ngr[g] * hg[g].astype(F32) * rowscale[:, 0:1], axis=0, keepdims=True)
        up_term = jnp.where(row_here, gain_term, dot_tn(pgr[g], ng[g]))
        down_term = dot_tn(act[:, pl.ds(g * 512, 512)], cotg[g])
        for kind, term in ((0, up_term), (1, down_term)):
            split = term.astype(BF).reshape(16, 2, PIECE, 256)
            for half in range(2):
                for side in range(2):
                    gg[side, 2 * kind + half, pl.ds(g * 16, 16)] = split[:, half, :, side * 128 : side * 128 + 128]

    send(gg.at[1 - core], r1a, ga_s, ga_v, {"dp": mate})

    await_bytes(r1a, ga_v)

    def pair_sum(step):
        for slab in range(4):
            part = pl.ds(pl.multiple_of(step * 8, 8), 8)
            both = gg[core, slab, part].astype(F32) + r1a[slab, part].astype(F32)
            h1[slab, part] = both.astype(BF)

    repeat(8, pair_sum)

    def spread_terms(step):
        other = lax.rem(chip + step, 4)
        send(h1.at[other], r1b.at[chip], gb_s.at[step], gb_v.at[step], {"dp": other * 2 + core})

    repeat(4, spread_terms, 1)

    others = [lax.rem(chip + step, 4) for step in (1, 2, 3)]

    for h in (1, 0):
        lanes = slice(128 * h, 128 * h + 128)

        def backward_one(step, h=h):
            sy = wrapped(y + step)
            await_bytes(a3.at[h, sy], v3.at[h, sy])
            shards = column_of(sy)
            values = mixed([a3[h, q, p].astype(F32) for p, q in shards], 1, shards, high_back, True)
            for (p, q), value in zip(shards, values):
                ff[p, q] = value

        repeat(SIDE, backward_one)

        def weigh_back(p, q, value, h=h, lanes=lanes):
            wide = value.astype(BF).astype(F32)
            owner = wrapped(q + y)
            kgb[lax.rem(owner, 2), lax.div(owner, 2), p, :, lanes] = (sp[h, p, q].astype(F32) * wide).astype(BF)
            ff[p, q] = wide * kt[q, p, :, lanes].astype(F32)

        def leave_back(p, q, value, h=h):
            src4[h, p, q] = value.astype(BF)

        two_at_once(row_of, load_wide, 1, low_back, True, weigh_back)
        if h == 0:
            send(kgb.at[1 - core], kra, kr_s, kr_v, {"dp": mate})
        two_at_once(column_of, load_wide, 0, high_back, True, store_wide)
        two_at_once(row_of, load_wide, 0, low_back, True, leave_back)
        last = half_of(h, src4, m4, s4, v4, (z, y), z)
        send_part(0, *last)
        if h == 1:
            send_part(1, *last)

    await_bytes(kra, kr_v)

    def kernel_pair(sz):
        for at in range(4):
            kgh[at, sz] = (kgb[core, at, sz].astype(F32) + kra[at, sz].astype(F32)).astype(BF)

    repeat(SIDE, kernel_pair)

    def spread_kernel_terms(step):
        other = lax.rem(chip + step, 4)
        send(kgh.at[other], krb.at[chip], kc_s.at[step], kc_v.at[step], {"dp": other * 2 + core})

    repeat(4, spread_kernel_terms, 1)

    def terms_here(step):
        await_bytes(r1b.at[lax.rem(chip + 4 - step, 4)], gb_v.at[step])

    repeat(4, terms_here, 1)

    def chip_sum(t):
        for odd in range(2):
            sz = 2 * t + odd
            part = pl.ds(pl.multiple_of(sz * 8, 8), 8)
            four = h1[chip, part].astype(F32)
            for other in others:
                four = four + r1b[other, part].astype(F32)
            four = four.astype(BF)
            for q in range(SIDE):
                if (odd + q) % 2 == 0:
                    pa1[q, t] = four[q]
                else:
                    pb1[sz, q // 2] = four[q]

    repeat(SIDE // 2, chip_sum)

    def along_y(step):
        ty = wrapped(y + step)
        send(pa1.at[ty], pa2.at[y], pa_s.at[step], pa_v.at[step], {"seq": z * SIDE + ty})

    def along_z(step):
        tz = wrapped(z + step)
        send(pb1.at[tz], pb2.at[z], pb_s.at[step], pb_v.at[step], {"seq": tz * SIDE + y})

    def first_step(step):
        along_y(step)
        along_z(step)

    repeat(SIDE, first_step, 1)

    def kernel_terms_here(step):
        await_bytes(krb.at[lax.rem(chip + 4 - step, 4)], kc_v.at[step])

    repeat(4, kernel_terms_here, 1)

    def kernel_sum(sz):
        four = kgh[chip, sz].astype(F32)
        for other in others:
            four = four + krb[other, sz].astype(F32)
        kgs[sz] = four.astype(BF)

    repeat(SIDE, kernel_sum)

    def return_kernel(dz):
        tz = wrapped(z + dz)
        send(kgs.at[tz], kgf.at[y, z], kf_s.at[1], kf_v, {"seq": tz * SIDE + yo})

    repeat(SIDE, return_kernel, 1)

    @pl.when(yo != y)
    def _():
        send(kgs.at[z], kgf.at[y, z], kf_s.at[0], kf_v, {"seq": z * SIDE + yo})

    @pl.when(yo == y)
    def _():
        pltpu.make_async_copy(kgs.at[z], kgf.at[y, z], kf_v).start()

    send_part(1, *last)

    acc[...] = dot_nt(ww[...], act[...])
    for g in range(GROUPS):
        rows = pl.ds(g * DG, DG)
        outv[rows] = (acc[rows] + dot_nt(eye[0:DG], hg[g])).astype(BF)
    pltpu.make_async_copy(outv, out_hbm, out_s.at[0]).start()

    def first_here(step):
        await_bytes(pa2.at[wrapped(y - step)], pa_v.at[step])
        await_bytes(pb2.at[wrapped(z - step)], pb_v.at[step])

    repeat(SIDE, first_here, 1)
    sum_y, sum_z = pa1[y].astype(F32), pb1[z].astype(F32)
    for step in range(1, SIDE):
        sum_y = sum_y + pa2[wrapped(y + step)].astype(F32)
        sum_z = sum_z + pb2[wrapped(z + step)].astype(F32)
    pa3[...] = sum_y.astype(BF)
    pb3[...] = sum_z.astype(BF)
    odd = lax.rem(z + y, 2)

    def second_z(m):
        return 2 * m + lax.rem(y, 2)

    def second_y(m):
        return 2 * m + 1 - lax.rem(z, 2)

    for m in range(4):

        @pl.when(second_z(m) != z)
        def _(m=m):
            send(pa3.at[m], pc.at[z], pc_s.at[m], pc_v.at[z], {"seq": second_z(m) * SIDE + y})

        @pl.when(second_y(m) != y)
        def _(m=m):
            send(pb3.at[m], pc.at[y], pd_s.at[m], pc_v.at[y], {"seq": z * SIDE + second_y(m)})

    @pl.when(odd == 0)
    def _():
        pc[z] = pa3[lax.div(z, 2)]

    @pl.when(odd == 1)
    def _():
        pc[y] = pb3[lax.div(y, 2)]

    await_bytes(kgf.at[yo], kf_v)
    to_chips(kgf, kh_s, kh_v)

    own = z + odd * (y - z)

    def second_here(step):
        at = wrapped(own + step)
        await_bytes(pc.at[at], pc_v.at[at])

    repeat(SIDE, second_here, 1)
    shard_sum = pc[0].astype(F32)
    for at in range(1, SIDE):
        shard_sum = shard_sum + pc[at].astype(F32)
    shard_sum = shard_sum * SCALE
    fin[...] = shard_sum
    rf[i] = shard_sum

    def spread_grads(step):
        send(fin, rf.at[i], gf_s.at[step], gf_v.at[step], {"dp": wrapped(i + step)})

    repeat(SIDE, spread_grads, 1)
    to_mate(kgf, kh_v, ki_s, ki_v)

    for h in (1, 0):
        lanes = slice(128 * h, 128 * h + 128)
        for sz in range(SIDE):
            await_bytes(m4.at[h, sz], v4.at[h, sz])
        for pair in range(2):
            value = half_lanes(hgr, h, pair).astype(F32) + dot(mint[...], load_half(m4, h, pair))
            value = dot_nt(eye[...], value.astype(BF)).astype(BF)
            for side in range(2):
                start = (2 * pair + side) * DG + 128 * h
                rows = DG - 128 if h == 1 else 128
                igv[pl.ds(start, rows)] = value[128 * side : 128 * side + rows]
    pltpu.make_async_copy(igv, ig_hbm, out_s.at[2]).start()

    from_mate(kgf, kh_v, ki_v)
    for g in range(GROUPS):
        held = jnp.stack([kgf[g], kgf[4 + g]], axis=1).reshape(256, 256)
        kgv[pl.ds(g * DG, DG)] = dot_nt(eye[0:DG], held).astype(BF)
    pltpu.make_async_copy(kgv, kg_hbm, out_s.at[1]).start()

    def grads_here(step):
        await_bytes(rf.at[wrapped(i - step)], gf_v.at[step])

    repeat(SIDE, grads_here, 1)
    for share in range(SIDE):
        kind, half, side = share // 4, (share // 2) % 2, share % 2
        wsum[kind, pl.ds(half * PIECE, PIECE), pl.ds(side * 128, 128)] = rf[share]
    ugv[...] = wsum[0, 0:30, 0:DG]
    dgv[...] = wsum[1, 0:30, 0:DG]
    j, lane = iotas((256, 128))
    picker = jnp.where(j == lane + 15 * lax.rem(me, 16), 1.0, 0.0)
    gains = jnp.broadcast_to(wsum[0, 30:31], (8, 256))
    picked = lax.dot_general(
        gains, picker, (((1,), (0,)), ((), ())), precision=lax.Precision.HIGHEST, preferred_element_type=F32
    )
    gnv[...] = picked[0:1, 0:15]
    pltpu.make_async_copy(ugv, ug_hbm, out_s.at[3]).start()
    pltpu.make_async_copy(dgv, dg_hbm, out_s.at[4]).start()
    pltpu.make_async_copy(gnv, gn_hbm, out_s.at[5]).start()

    for buffer, sem in ((src1, s1), (src2, s2), (src3, s3), (src4, s4)):
        for h in range(2):
            await_sent(buffer.at[h], sem.at[h])
    for m in range(4):

        @pl.when(second_z(m) != z)
        def _(m=m):
            await_bytes(pa3.at[m], pc_s.at[m])

        @pl.when(second_y(m) != y)
        def _(m=m):
            await_bytes(pb3.at[m], pd_s.at[m])

    await_bytes(ks.at[0, pl.ds(0, 7)], ks_s.at[1])
    await_bytes(kgs.at[pl.ds(0, 7)], kf_s.at[1])

    @pl.when(yo != y)
    def _():
        await_bytes(ks.at[0, 0], ks_s.at[0])
        await_bytes(kgs.at[0], kf_s.at[0])

    await_bytes(kt.at[0], ka_s.at[0])
    await_bytes(kgf.at[0], kh_s.at[0])
    await_bytes(r1a, ga_s)
    await_bytes(kra, kr_s)

    def chips_left(step):
        await_bytes(kt.at[0], ka_s.at[step])
        await_bytes(kt.at[0], kb_s.at[step])
        await_bytes(kgf.at[0], kh_s.at[step])
        await_bytes(kgf.at[0], ki_s.at[step])
        await_bytes(kgh.at[0], kc_s.at[step])
        await_bytes(h1.at[0], gb_s.at[step])

    repeat(4, chips_left, 1)

    def grads_left(step):
        await_bytes(fin, gf_s.at[step])
        await_bytes(pa1.at[0], pa_s.at[step])
        await_bytes(pb1.at[0], pb_s.at[step])

    repeat(SIDE, grads_left, 1)
    outs = ((outv, out_hbm), (kgv, kg_hbm), (igv, ig_hbm), (ugv, ug_hbm), (dgv, dg_hbm), (gnv, gn_hbm))
    for index, (held, there) in enumerate(outs):
        pltpu.make_async_copy(held, there, out_s.at[index]).wait()


def settle(*refs):
    source, there, held, sems = refs[:6], refs[6:12], refs[12:18], refs[18]
    loads = [pltpu.make_async_copy(source[index], held[index], sems.at[0, index]) for index in range(6)]
    stores = [pltpu.make_async_copy(held[index], there[index], sems.at[1, index]) for index in range(6)]
    for copy in loads:
        copy.start()
    for load, store in zip(loads, stores):
        load.wait()
        store.start()
    for copy in stores:
        copy.wait()


def local(
    inputs, cotangent, kernel_values, mix_in, mix_out, twiddle_self, twiddle_cross, norm_gain, up_weight, down_weight
):
    hbm = pl.BlockSpec(memory_space=pltpu.HBM)
    dma = pltpu.SemaphoreType.DMA
    vmem = pltpu.VMEM
    exchange = vmem((SIDE, SIDE, PIECE, 256), BF)
    halves = vmem((2, SIDE, SIDE, PIECE, 128), BF)
    part = vmem((SIDE, 4, PIECE, 128), BF)
    both = dma((2, SIDE))
    grouped = vmem((GROUPS, 256, 256), BF)
    square = vmem((256, 256), BF)
    quarter = vmem((4, SIDE, PIECE, 256), BF)
    terms = vmem((4, 64, PIECE, 128), BF)
    wide = (D, 256)
    scratch = dict(
        xv=grouped, kv=grouped, cotv=grouped, min_ref=square, mout_ref=square,
        ts_ref=vmem((6, 2, 256), BF), tc_ref=vmem((6, 2, 256), BF), gain_ref=vmem((1, D), BF),
        up_ref=vmem((DG, 1920), BF), down_ref=vmem((DG, 1920), BF),
        outv=vmem(wide, BF), igv=vmem(wide, BF), kgv=vmem(wide, BF),
        ugv=vmem((30, DG), F32), dgv=vmem((30, DG), F32), gnv=vmem((1, 15), F32),
        eye=square, mint=square, moutt=square, twp=vmem((2, 256, 256), F32),
        xg=grouped, cotg=grouped, cotn=grouped,
        upp=vmem((GROUPS, 256, 512), BF), dnp=vmem((GROUPS, 256, 512), BF), ww=vmem((D, 2048), BF),
        acot=vmem((GROUPS, 256, 512), F32), pa=vmem((256, 512), F32), act=vmem((256, 2048), BF),
        pgr=vmem((GROUPS, 256, 512), BF), hg=grouped, ng=grouped, ngr=vmem((GROUPS, 256, 256), F32),
        hgr=grouped, acc=vmem(wide, F32), gaing=vmem((GROUPS, 8, 256), F32), rowscale=vmem((256, 128), F32),
        wsum=vmem((2, 32, 256), F32),
        src1=halves, a1=halves, ks=exchange, kt=exchange, ff=vmem((SIDE, SIDE, PIECE, 128), F32), sp=halves,
        src2=halves, m2=halves, src3=halves, a3=halves, src4=halves, m4=halves,
        pa1=part, pa2=part, pa3=vmem((4, PIECE, 128), BF), pb1=part, pb2=part, pb3=vmem((4, PIECE, 128), BF),
        pc=vmem((SIDE, PIECE, 128), BF),
        twb=vmem((2, SIDE, SIDE, 12, PIECE, 128), F32),
        kgb=vmem((2, 4, SIDE, PIECE, 256), BF), kra=quarter, kgh=quarter, krb=quarter,
        kgs=vmem((SIDE, PIECE, 256), BF), kgf=exchange,
        gg=vmem((2, 4, 64, PIECE, 128), BF), r1a=terms, h1=terms, r1b=terms,
        fin=vmem((PIECE, 128), F32), rf=vmem((SIDE, PIECE, 128), F32),
        in_s=dma((19,)), out_s=dma((6,)),
        s1=both, v1=both, s2=both, v2=both, s3=both, v3=both, s4=both, v4=both,
        pa_s=dma((SIDE,)), pa_v=dma((SIDE,)), pb_s=dma((SIDE,)), pb_v=dma((SIDE,)),
        pc_s=dma((4,)), pc_v=dma((SIDE,)), pd_s=dma((4,)),
        ks_s=dma((2,)), ks_v=dma, ka_s=dma((4,)), ka_v=dma((4,)), kb_s=dma((4,)), kb_v=dma((4,)),
        kr_s=dma, kr_v=dma, kc_s=dma((4,)), kc_v=dma((4,)), kf_s=dma((2,)), kf_v=dma,
        kh_s=dma((4,)), kh_v=dma((4,)), ki_s=dma((4,)), ki_v=dma((4,)),
        ga_s=dma, ga_v=dma, gb_s=dma((4,)), gb_v=dma((4,)), gf_s=dma((SIDE,)), gf_v=dma((SIDE,)),
    )
    shape = jax.ShapeDtypeStruct
    results = [shape(wide, BF)] * 3 + [shape((30, DG), F32)] * 2 + [shape((1, 15), F32)]
    held = pl.pallas_call(
        kernel,
        out_shape=results,
        in_specs=[hbm] * 10,
        out_specs=[hbm] * 6,
        scratch_shapes=scratch,
        compiler_params=pltpu.CompilerParams(
            collective_id=0, has_side_effects=True, vmem_limit_bytes=58 * 1024 * 1024
        ),
        cost_estimate=pl.CostEstimate(flops=4_000_000_000, bytes_accessed=6_000_000, transcendentals=600_000),
    )(
        inputs[0].T, cotangent[0].T, kernel_values.T, mix_in, mix_out,
        twiddle_self.transpose(1, 0, 2), twiddle_cross.transpose(1, 0, 2),
        norm_gain[None, :], up_weight, down_weight,
    )
    output, input_grad, kernel_grad, up_grad, down_grad, gain_grad = pl.pallas_call(
        settle,
        out_shape=results,
        in_specs=[hbm] * 6,
        out_specs=[hbm] * 6,
        scratch_shapes=[vmem(result.shape, result.dtype) for result in results] + [dma((2, 6))],
        compiler_params=pltpu.CompilerParams(vmem_limit_bytes=58 * 1024 * 1024),
        cost_estimate=pl.CostEstimate(flops=0, bytes_accessed=3_000_000, transcendentals=0),
    )(*held)
    return output.T[None], input_grad.T[None], kernel_grad.T, up_grad.T, down_grad.T, gain_grad[0]


def solution(mesh):
    in_specs = (
        P("dp", "seq", None),
        P("dp", "seq", None),
        P("seq", None),
        P("seq", None),
        P("seq", None),
        P(None, None, "seq"),
        P(None, None, "seq"),
        P(),
        P(),
        P(),
    )
    out_specs = (
        P("dp", "seq", None),
        P("dp", "seq", None),
        P("seq", None),
        P(None, "seq"),
        P(None, "seq"),
        P("seq"),
    )
    return jax.shard_map(local, mesh=mesh, in_specs=in_specs, out_specs=out_specs, check_vma=False)
```

```python
import jax
import jax.numpy as jnp
from jax import lax
from jax.experimental import pallas as pl
from jax.experimental.pallas import tpu as pltpu
from jax.sharding import PartitionSpec as P

MESH = pl.DeviceIdType.MESH
BF = jnp.bfloat16
F32 = jnp.float32

D = 960
GROUPS = 4
DG = 240
FFG = 480
SIDE = 8
PIECE = 16
ROOT_HALF = 0.7978845608028654
CUBIC = 0.044715
SCALE = 131072.0**-0.5
GAIN_WINDOWS = ((0, 256), (128, 512), (384, 768), (640, 960))
HIDDEN_WINDOWS = ((0, 512), (384, 1024), (896, 1536), (1408, 1920))


def dot(a, b):
    return lax.dot_general(a, b, (((1,), (0,)), ((), ())), preferred_element_type=F32)


def dot_tn(a, b):
    return lax.dot_general(a, b, (((0,), (0,)), ((), ())), preferred_element_type=F32)


def dot_nt(a, b):
    return lax.dot_general(a, b, (((1,), (1,)), ((), ())), preferred_element_type=F32)


def iotas(shape):
    return lax.broadcasted_iota(jnp.int32, shape, 0), lax.broadcasted_iota(jnp.int32, shape, 1)


def ones_where(mask):
    return jnp.where(mask, 1.0, 0.0).astype(BF)


def repeat(count, body, start=0):
    def step(index, carry):
        body(index)
        return carry

    lax.fori_loop(start, count, step, 0)


def wrapped(value):
    return lax.rem(value + 2 * SIDE, SIDE)


def await_bytes(view, sem):
    pltpu.make_async_copy(view, view, sem).wait()


def mix(values, selfs, crosses, bits, transposed):
    for k, bit in bits:
        stride = 1 << bit
        if transposed:
            scaled = [crosses(a, k) * values[a] for a in range(SIDE)]
            values = [selfs(a, k) * values[a] + scaled[a ^ stride] for a in range(SIDE)]
        else:
            values = [selfs(a, k) * values[a] + crosses(a, k) * values[a ^ stride] for a in range(SIDE)]
    return values


def kernel(
    x_hbm, cot_hbm, ker_hbm, min_hbm, mout_hbm, ts_hbm, tc_hbm, gain_hbm, up_hbm, down_hbm,
    out_hbm, ig_hbm, kg_hbm, ug_hbm, dg_hbm, gn_hbm,
    xv, kv, cotv, min_ref, mout_ref, ts_ref, tc_ref, gain_ref, up_ref, down_ref,
    outv, igv, kgv, ugv, dgv, gnv,
    eye, mint, moutt, twp, xg, cotg, cotn, upp, dnp, ww, acot, pa, act, pgr, hg, ng, ngr, hgr, acc, gaing, rowscale, wsum,
    src1, a1, ks, kt, ff, sp, src2, m2, src3, a3, src4, m4, twb, pa1, pa2, pa3, pb1, pb2, pb3, pc,
    kgb, kra, kgh, krb, kgs, kgf, gg, r1a, h1, r1b, fin, rf,
    in_s, out_s, s1, v1, s2, v2, s3, v3, s4, v4, pa_s, pa_v, pb_s, pb_v, pc_s, pc_v, pd_s,
    ks_s, ks_v, ka_s, ka_v, kb_s, kb_v, kr_s, kr_v, kc_s, kc_v, kf_s, kf_v, kh_s, kh_v, ki_s, ki_v,
    ga_s, ga_v, gb_s, gb_v, gf_s, gf_v,
):
    loads = []

    def load(src, dst):
        copy = pltpu.make_async_copy(src, dst, in_s.at[len(loads)])
        copy.start()
        loads.append(copy)
        return copy

    def load_groups(src, dst):
        return [load(src.at[pl.ds(g * DG, DG)], dst.at[g, pl.ds(0, DG)]) for g in range(GROUPS)]

    tw_here = [load(ts_hbm, ts_ref), load(tc_hbm, tc_ref)]
    ker_here = load_groups(ker_hbm, kv)
    x_here = [load(min_hbm, min_ref)] + load_groups(x_hbm, xv)
    rest_here = load_groups(cot_hbm, cotv)
    rest_here += [load(gain_hbm, gain_ref), load(up_hbm, up_ref), load(down_hbm, down_ref), load(mout_hbm, mout_ref)]

    me = lax.axis_index("seq")
    z, y = lax.div(me, SIDE), lax.rem(me, SIDE)
    i = lax.axis_index("dp")
    chip, core = lax.div(i, 2), lax.rem(i, 2)
    mate = i + 1 - 2 * core
    yo = wrapped(i - y)
    tz_at = [wrapped(z + step) for step in range(SIDE)]
    ty_at = [wrapped(y + step) for step in range(SIDE)]

    barrier = pltpu.get_barrier_semaphore()

    def greet_seq(step):
        pl.semaphore_signal(
            barrier, inc=1, device_id=(i, lax.rem(me + step, 64)), device_id_type=MESH
        )

    def greet_dp(step):
        pl.semaphore_signal(barrier, inc=1, device_id=(wrapped(i + step), me), device_id_type=MESH)

    repeat(64, greet_seq, 1)
    repeat(8, greet_dp, 1)

    def send(src, dst, ssem, rsem, device):
        pltpu.make_async_remote_copy(
            src_ref=src, dst_ref=dst, send_sem=ssem, recv_sem=rsem, device_id=device, device_id_type=MESH
        ).start()

    def send_part(part, src, dst, ssem, rsem):
        offsets = ((3, 5, 1, 7), (2, 6, 4, 0))[part]

        def one(dz, ty):
            tz = tz_at[dz]
            send(src(tz, ty), dst, ssem.at[dz], rsem, (i, tz * SIDE + ty))

        def pair(t):
            for dy in (3 - t, 5 + t):
                ty = wrapped(y + dy)
                for dz in offsets:
                    one(dz, ty)

        repeat(3, pair)
        for dy in (4, 0):
            for dz in offsets:
                if (dz, dy) != (0, 0):
                    one(dz, ty_at[dy])
        if part == 1:
            pltpu.make_async_copy(src(z, y), dst, rsem).start()

    def await_sent(buffer, ssem):
        await_bytes(buffer.at[0, pl.ds(0, 7)], ssem.at[0])
        for dz in range(1, SIDE):
            await_bytes(buffer.at[0], ssem.at[dz])

    def store_half(ref, h, pair, value):
        for side in range(2):
            split = value[:, 128 * side : 128 * side + 128].reshape(SIDE, 2, PIECE, 128)
            ref[h, :, 2 * pair + side] = split[:, 0]
            ref[h, :, 4 + 2 * pair + side] = split[:, 1]

    def load_half(ref, h, pair):
        groups = (2 * pair, 2 * pair + 1)
        return jnp.concatenate(
            [jnp.stack([ref[h, :, g], ref[h, :, 4 + g]], axis=1).reshape(256, 128) for g in groups], axis=1
        )

    def half_lanes(ref, h, pair):
        return jnp.concatenate([ref[2 * pair + side, :, 128 * h : 128 * h + 128] for side in range(2)], axis=1)

    def slot(chip_at, core_at):
        return wrapped(2 * chip_at + core_at - y)

    def to_chips(buffer, ssem, rsem):
        send(buffer.at[yo], buffer.at[yo], ssem.at[0], rsem.at[0], (mate, me))

        def step_to(step):
            send(
                buffer.at[yo], buffer.at[yo], ssem.at[step], rsem.at[step],
                (2 * lax.rem(chip + step, 4) + core, me),
            )

        repeat(4, step_to, 1)

    def to_mate(buffer, rsem, ssem2, rsem2):
        def step_to(step):
            held = buffer.at[slot(lax.rem(chip + 4 - step, 4), core)]
            await_bytes(held, rsem.at[step])
            send(held, held, ssem2.at[step], rsem2.at[step], (mate, me))

        repeat(4, step_to, 1)

    def from_mate(buffer, rsem, rsem2):
        await_bytes(buffer.at[slot(chip, 1 - core)], rsem.at[0])

        def step_from(step):
            await_bytes(buffer.at[slot(lax.rem(chip + 4 - step, 4), 1 - core)], rsem2.at[step])

        repeat(4, step_from, 1)

    r, l = iotas((256, 256))
    eye[...] = ones_where(r == l)
    twp[...] = jnp.zeros_like(twp)
    for copy in tw_here:
        copy.wait()
    for k in range(6):
        for which in range(2):
            twp[which, pl.ds(DG + k, 1)] = ts_ref[k, which : which + 1].astype(F32)
            twp[which, pl.ds(DG + 8 + k, 1)] = tc_ref[k, which : which + 1].astype(F32)
    for copy in ker_here:
        copy.wait()
    for g in range(GROUPS):
        kv[g, pl.ds(DG, PIECE)] = twp[1, pl.ds(DG, PIECE)].astype(BF)
        split = dot_nt(eye[...], kv[g]).astype(BF).reshape(SIDE, 2, PIECE, 256)
        ks[:, g] = split[:, 0]
        ks[:, 4 + g] = split[:, 1]
    columns = dot_nt(eye[...], twp[0].astype(BF))[:, 128:256]
    for copy in x_here:
        copy.wait()
    for g in range(GROUPS):
        xv[g, pl.ds(DG, PIECE)] = jnp.zeros((PIECE, 256), BF)

    def premix(h):
        for pair in range(2):
            rows = jnp.concatenate([xv[2 * pair + side, 128 * h : 128 * h + 128] for side in range(2)], axis=0)
            value = dot_nt(min_ref[...], rows)
            if h == 1:
                value = value + jnp.concatenate([columns, columns], axis=1)
            store_half(src1, h, pair, value.astype(BF))

    premix(1)
    pl.semaphore_wait(barrier, 70)

    def share_kernel(dz):
        tz = wrapped(z + dz)
        send(ks.at[tz, yo], kt.at[y, z], ks_s.at[1], ks_v, (i, tz * SIDE + yo))

    repeat(SIDE, share_kernel, 1)

    @pl.when(yo != y)
    def _():
        send(ks.at[z, yo], kt.at[y, z], ks_s.at[0], ks_v, (i, z * SIDE + yo))

    @pl.when(yo == y)
    def _():
        pltpu.make_async_copy(ks.at[z, yo], kt.at[y, z], ks_v).start()

    def half_of(h, src, dst, ssem, rsem, at, group):
        return (lambda tz, ty: src.at[h, tz, ty], dst.at[(h,) + at], ssem.at[h], rsem.at[h, group])

    for h in (1, 0):
        first = half_of(h, src1, a1, s1, v1, (z, y), z)
        if h == 0:
            to_mate(kt, ka_v, kb_s, kb_v)
            premix(0)
        send_part(0, *first)
        if h == 1:
            await_bytes(kt.at[yo], ks_v)
            to_chips(kt, ka_s, ka_v)
        send_part(1, *first)

    def spread_twiddles(which, p, q, slab):
        wide = slab.astype(F32)
        for k in range(6):
            twb[which, p, q, k] = jnp.broadcast_to(wide[:, 112 + k : 113 + k], (PIECE, 128))
            twb[which, p, q, 6 + k] = jnp.broadcast_to(wide[:, 120 + k : 121 + k], (PIECE, 128))

    def mixed(values, which, shards, bits, transposed):
        def selfs(a, k):
            return twb[which, shards[a][0], shards[a][1], k]

        def crosses(a, k):
            return twb[which, shards[a][0], shards[a][1], 6 + k]

        return mix(values, selfs, crosses, bits, transposed)

    low_bits = ((0, 0), (1, 1), (2, 2))
    high_bits = ((3, 0), (4, 1), (5, 2))
    low_back = tuple(reversed(low_bits))
    high_back = tuple(reversed(high_bits))

    def row_of(sz):
        return [(sz, a) for a in range(SIDE)]

    def column_of(sy):
        return [(a, sy) for a in range(SIDE)]

    def work(groups, read, which, bits, transposed, write):
        held = [[read(p, q) for p, q in shards] for shards in groups]
        held = [mixed(values, which, shards, bits, transposed) for values, shards in zip(held, groups)]
        for shards, values in zip(groups, held):
            for (p, q), value in zip(shards, values):
                write(p, q, value)

    def two_at_once(lines, read, which, bits, transposed, write):
        def step(t):
            work([lines(2 * t), lines(2 * t + 1)], read, which, bits, transposed, write)

        repeat(SIDE // 2, step)

    def store_wide(p, q, value):
        ff[p, q] = value

    def load_wide(p, q):
        return ff[p, q]

    from_mate(kt, ka_v, kb_v)

    def spread_output_twiddles(sz):
        for p, q in row_of(sz):
            spread_twiddles(1, p, q, kt[q, p, :, 128:256])

    repeat(SIDE, spread_output_twiddles)

    for h in (1, 0):
        lanes = slice(128 * h, 128 * h + 128)

        def forward_one(step, h=h):
            sz = wrapped(z + step)
            await_bytes(a1.at[h, sz], v1.at[h, sz])
            shards = row_of(sz)
            if h == 1:
                for p, q in shards:
                    spread_twiddles(0, p, q, a1[1, p, q])
            values = mixed([a1[h, p, q].astype(F32) for p, q in shards], 0, shards, low_bits, False)
            for (p, q), value in zip(shards, values):
                ff[p, q] = value

        repeat(SIDE, forward_one)

        def weigh(p, q, value, h=h, lanes=lanes):
            rounded = value.astype(BF)
            sp[h, p, q] = rounded
            ff[p, q] = rounded.astype(F32) * kt[q, p, :, lanes].astype(F32)

        def leave(p, q, value, h=h):
            src2[h, p, q] = value.astype(BF)

        two_at_once(column_of, load_wide, 0, high_bits, False, weigh)
        two_at_once(row_of, load_wide, 1, low_bits, False, store_wide)

        def forward_four(dys, h=h):
            columns = [wrapped(y + dy) for dy in dys]
            work([column_of(sy) for sy in columns], load_wide, 1, high_bits, False, leave)
            for dy, sy in zip(dys, columns):
                for dz, sz in enumerate(tz_at):
                    if dz == 0 and isinstance(dy, int) and dy == 0:
                        pltpu.make_async_copy(src2.at[h, z, y], m2.at[h, z, y], v2.at[h, z]).start()
                    else:
                        send(src2.at[h, sz, sy], m2.at[h, z, y], s2.at[h, dz], v2.at[h, z], (i, sz * SIDE + sy))

        forward_four((0, 4))
        repeat(4, lambda t: forward_four((t, SIDE - t)), 1)
        if h == 1:
            for copy in rest_here:
                copy.wait()
            for g in range(GROUPS):
                xg[g] = dot_nt(eye[...], xv[g]).astype(BF)
                cotv[g, pl.ds(DG, PIECE)] = jnp.zeros((PIECE, 256), BF)
            mint[...] = dot_nt(eye[...], min_ref[...]).astype(BF)
            moutt[...] = dot_nt(eye[...], mout_ref[...]).astype(BF)
            for g in range(GROUPS):
                cotn[g] = dot_nt(eye[...], cotv[g]).astype(BF)
                picked = jnp.zeros((256, 256), F32)
                for part in range(GROUPS):
                    j, lane = iotas((256, 256))
                    picked = picked + dot(ones_where((part * DG + lane == 4 * j + g) & (lane < DG)), cotv[part])
                cotg[g] = dot_nt(eye[...], picked.astype(BF)).astype(BF)
                low, high = GAIN_WINDOWS[g]
                channel, lane = iotas((high - low, 256))
                gain_rows = jnp.broadcast_to(gain_ref[:, low:high].astype(F32), (PIECE, high - low)).astype(BF)
                gaing[g] = dot(gain_rows, ones_where((channel + low == g * DG + lane) & (lane < DG)))[0:8]


    for g in range(GROUPS):
        low, high = HIDDEN_WINDOWS[g]
        column, hidden_unit = iotas((high - low, 512))
        chosen = (column + low == g * FFG + hidden_unit - 2 * (hidden_unit >> 5)) & ((hidden_unit & 31) < 30)
        chooser = ones_where(chosen)
        upp[g, 0:DG] = dot(up_ref[:, low:high], chooser).astype(BF)
        dnp[g, 0:DG] = dot(down_ref[:, low:high], chooser).astype(BF)
        upp[g, DG:256] = jnp.zeros((256 - DG, 512), BF)
        dnp[g, DG:256] = jnp.zeros((256 - DG, 512), BF)

    for g in range(GROUPS):
        acot[g] = dot(cotg[g], dnp[g])
        channel, j = iotas((D, 256))
        spread = ones_where((channel == 4 * j + g) & (j < DG))
        ww[:, pl.ds(g * 512, 512)] = dot(spread, dnp[g]).astype(BF)

    lane_here = (lax.broadcasted_iota(jnp.int32, (256, 256), 1) & 127) < DG - 128
    squares = jnp.zeros((256, 1), F32)
    for h in (1, 0):
        for sz in range(SIDE):
            await_bytes(m2.at[h, sz], v2.at[h, sz])
        for pair in range(2):
            value = half_lanes(xg, h, pair).astype(F32) + dot(mout_ref[...], load_half(m2, h, pair))
            if h == 1:
                value = jnp.where(lane_here, value, 0.0)
            value = value.astype(BF)
            for side in range(2):
                hg[2 * pair + side, :, 128 * h : 128 * h + 128] = value[:, 128 * side : 128 * side + 128]
            wide = value.astype(F32)
            squares = squares + jnp.sum(wide * wide, axis=1, keepdims=True)
    scale_column = lax.rsqrt(squares * (1.0 / D) + 1e-06)
    rowscale[...] = jnp.broadcast_to(scale_column, (256, 128))

    for g in range(GROUPS):
        wide = hg[g].astype(F32)
        ng[g] = (wide * rowscale[:, 0:1] * gaing[g, 0:1]).astype(BF)
        pa[...] = dot(ng[g], upp[g])

        def activate(tile, g=g):
            rows = pl.ds(pl.multiple_of(tile * 32, 32), 32)
            p = pa[rows]
            square = p * p
            tangent = jnp.tanh(p * (ROOT_HALF + (ROOT_HALF * CUBIC) * square))
            half_more = 0.5 + 0.5 * tangent
            act[rows, pl.ds(g * 512, 512)] = (p * half_more).astype(BF)
            inner = ROOT_HALF + (3.0 * ROOT_HALF * CUBIC) * square
            slope = half_more + 0.5 * p * (1.0 - tangent * tangent) * inner
            pgr[g, rows] = (acot[g, rows] * slope).astype(BF)

        repeat(8, activate)
        ngr[g] = dot_nt(pgr[g], upp[g])

    means = jnp.zeros((256, 1), F32)
    for g in range(GROUPS):
        means = means + jnp.sum(ngr[g] * gaing[g, 0:1] * hg[g].astype(F32), axis=1, keepdims=True)
    scale_column = rowscale[:, 0:1]
    means = means * (1.0 / D) * scale_column * scale_column * scale_column
    for h in (1, 0):
        lanes = slice(128 * h, 128 * h + 128)
        for pair in range(2):
            for g in (2 * pair, 2 * pair + 1):
                gained = ngr[g, :, lanes] * gaing[g, 0:1, lanes]
                wide = hg[g, :, lanes].astype(F32)
                hgr[g, :, lanes] = (cotn[g, :, lanes].astype(F32) + scale_column * gained - wide * means).astype(BF)
            store_half(src3, h, pair, dot(moutt[...], half_lanes(hgr, h, pair)).astype(BF))
        for part in range(2):
            send_part(part, *half_of(h, src3, a3, s3, v3, (y, z), y))

    row_here = (lax.broadcasted_iota(jnp.int32, (512, 256), 0) & 31) == 30
    for g in range(GROUPS):
        gain_term = jnp.sum(ngr[g] * hg[g].astype(F32) * rowscale[:, 0:1], axis=0, keepdims=True)
        up_term = jnp.where(row_here, gain_term, dot_tn(pgr[g], ng[g]))
        down_term = dot_tn(act[:, pl.ds(g * 512, 512)], cotg[g])
        for kind, term in ((0, up_term), (1, down_term)):
            split = term.astype(BF).reshape(16, 2, PIECE, 256)
            for half in range(2):
                for side in range(2):
                    gg[side, 2 * kind + half, pl.ds(g * 16, 16)] = split[:, half, :, side * 128 : side * 128 + 128]

    send(gg.at[1 - core], r1a, ga_s, ga_v, (mate, me))

    others = [lax.rem(chip + step, 4) for step in (1, 2, 3)]

    for h in (1, 0):
        lanes = slice(128 * h, 128 * h + 128)

        def backward_one(step, h=h):
            sy = wrapped(y + step)
            await_bytes(a3.at[h, sy], v3.at[h, sy])
            shards = column_of(sy)
            values = mixed([a3[h, q, p].astype(F32) for p, q in shards], 1, shards, high_back, True)
            for (p, q), value in zip(shards, values):
                ff[p, q] = value

        repeat(SIDE, backward_one)

        def weigh_back(p, q, value, h=h, lanes=lanes):
            wide = value.astype(BF).astype(F32)
            owner = wrapped(q + y)
            kgb[lax.rem(owner, 2), lax.div(owner, 2), p, :, lanes] = (sp[h, p, q].astype(F32) * wide).astype(BF)
            ff[p, q] = wide * kt[q, p, :, lanes].astype(F32)

        def leave_back(p, q, value, h=h):
            src4[h, p, q] = value.astype(BF)

        two_at_once(row_of, load_wide, 1, low_back, True, weigh_back)
        if h == 0:
            send(kgb.at[1 - core], kra, kr_s, kr_v, (mate, me))
        two_at_once(column_of, load_wide, 0, high_back, True, store_wide)

        def send_rows(dzs, h=h):
            for dz in dzs:
                sz = wrapped(z + dz)
                for dy, sy in enumerate(ty_at):
                    if dy == 0 and isinstance(dz, int) and dz == 0:
                        pltpu.make_async_copy(src4.at[h, z, y], m4.at[h, z, y], v4.at[h, z]).start()
                    else:
                        send(src4.at[h, sz, sy], m4.at[h, z, y], s4.at[h, dz], v4.at[h, z], (i, sz * SIDE + sy))

        def backward_four(dzs):
            work([row_of(wrapped(z + dz)) for dz in dzs], load_wide, 0, low_back, True, leave_back)

        def backward_four_sent(dzs):
            backward_four(dzs)
            send_rows(dzs)

        if h == 1:
            await_bytes(r1a, ga_v)

            def pair_sum(step):
                for slab in range(4):
                    part = pl.ds(pl.multiple_of(step * 8, 8), 8)
                    both = gg[core, slab, part].astype(F32) + r1a[slab, part].astype(F32)
                    h1[slab, part] = both.astype(BF)

            repeat(8, pair_sum)

            def spread_terms(step):
                other = lax.rem(chip + step, 4)
                send(h1.at[other], r1b.at[chip], gb_s.at[step], gb_v.at[step], (other * 2 + core, me))

            repeat(4, spread_terms, 1)

        backward_four_sent((0, 4))
        if h == 1:
            repeat(4, lambda t: backward_four_sent((t, SIDE - t)), 1)
        else:
            repeat(2, lambda t: backward_four_sent((t, SIDE - t)), 1)
            repeat(4, lambda t: backward_four((t, SIDE - t)), 2)

    await_bytes(kra, kr_v)

    def kernel_pair(sz):
        for at in range(4):
            kgh[at, sz] = (kgb[core, at, sz].astype(F32) + kra[at, sz].astype(F32)).astype(BF)

    repeat(SIDE, kernel_pair)

    def spread_kernel_terms(step):
        other = lax.rem(chip + step, 4)
        send(kgh.at[other], krb.at[chip], kc_s.at[step], kc_v.at[step], (other * 2 + core, me))

    repeat(4, spread_kernel_terms, 1)

    def terms_here(step):
        await_bytes(r1b.at[lax.rem(chip + 4 - step, 4)], gb_v.at[step])

    repeat(4, terms_here, 1)

    def chip_sum(t):
        for odd in range(2):
            sz = 2 * t + odd
            part = pl.ds(pl.multiple_of(sz * 8, 8), 8)
            four = h1[chip, part].astype(F32)
            for other in others:
                four = four + r1b[other, part].astype(F32)
            four = four.astype(BF)
            for q in range(SIDE):
                if (odd + q) % 2 == 0:
                    pa1[q, t] = four[q]
                else:
                    pb1[sz, q // 2] = four[q]

    repeat(SIDE // 2, chip_sum)

    def along_y(step):
        ty = wrapped(y + step)
        send(pa1.at[ty], pa2.at[y], pa_s.at[step], pa_v.at[step], (i, z * SIDE + ty))

    def along_z(step):
        tz = wrapped(z + step)
        send(pb1.at[tz], pb2.at[z], pb_s.at[step], pb_v.at[step], (i, tz * SIDE + y))

    def first_step(step):
        along_y(step)
        along_z(step)

    repeat(SIDE, first_step, 1)

    def kernel_terms_here(step):
        await_bytes(krb.at[lax.rem(chip + 4 - step, 4)], kc_v.at[step])

    repeat(4, kernel_terms_here, 1)

    def kernel_sum(sz):
        four = kgh[chip, sz].astype(F32)
        for other in others:
            four = four + krb[other, sz].astype(F32)
        kgs[sz] = four.astype(BF)

    repeat(SIDE, kernel_sum)

    def return_kernel(dz):
        tz = wrapped(z + dz)
        send(kgs.at[tz], kgf.at[y, z], kf_s.at[1], kf_v, (i, tz * SIDE + yo))

    repeat(SIDE, return_kernel, 1)

    @pl.when(yo != y)
    def _():
        send(kgs.at[z], kgf.at[y, z], kf_s.at[0], kf_v, (i, z * SIDE + yo))

    @pl.when(yo == y)
    def _():
        pltpu.make_async_copy(kgs.at[z], kgf.at[y, z], kf_v).start()

    repeat(4, lambda t: send_rows((t, SIDE - t)), 2)

    acc[...] = dot_nt(ww[...], act[...])
    for g in range(GROUPS):
        rows = pl.ds(g * DG, DG)
        outv[rows] = (acc[rows] + dot_nt(eye[0:DG], hg[g])).astype(BF)
    pltpu.make_async_copy(outv, out_hbm, out_s.at[0]).start()

    def first_here(step):
        await_bytes(pa2.at[wrapped(y - step)], pa_v.at[step])
        await_bytes(pb2.at[wrapped(z - step)], pb_v.at[step])

    repeat(SIDE, first_here, 1)
    sum_y, sum_z = pa1[y].astype(F32), pb1[z].astype(F32)
    for step in range(1, SIDE):
        sum_y = sum_y + pa2[wrapped(y + step)].astype(F32)
        sum_z = sum_z + pb2[wrapped(z + step)].astype(F32)
    pa3[...] = sum_y.astype(BF)
    pb3[...] = sum_z.astype(BF)
    odd = lax.rem(z + y, 2)

    def second_z(m):
        return 2 * m + lax.rem(y, 2)

    def second_y(m):
        return 2 * m + 1 - lax.rem(z, 2)

    for m in range(4):

        @pl.when(second_z(m) != z)
        def _(m=m):
            send(pa3.at[m], pc.at[z], pc_s.at[m], pc_v.at[z], (i, second_z(m) * SIDE + y))

        @pl.when(second_y(m) != y)
        def _(m=m):
            send(pb3.at[m], pc.at[y], pd_s.at[m], pc_v.at[y], (i, z * SIDE + second_y(m)))

    @pl.when(odd == 0)
    def _():
        pc[z] = pa3[lax.div(z, 2)]

    @pl.when(odd == 1)
    def _():
        pc[y] = pb3[lax.div(y, 2)]

    await_bytes(kgf.at[yo], kf_v)
    to_chips(kgf, kh_s, kh_v)

    own = z + odd * (y - z)

    def second_here(step):
        at = wrapped(own + step)
        await_bytes(pc.at[at], pc_v.at[at])

    repeat(SIDE, second_here, 1)
    shard_sum = pc[0].astype(F32)
    for at in range(1, SIDE):
        shard_sum = shard_sum + pc[at].astype(F32)
    shard_sum = shard_sum * SCALE
    fin[...] = shard_sum
    rf[i] = shard_sum

    def spread_grads(step):
        send(fin, rf.at[i], gf_s.at[step], gf_v.at[step], (wrapped(i + step), me))

    repeat(SIDE, spread_grads, 1)
    to_mate(kgf, kh_v, ki_s, ki_v)

    for h in (1, 0):
        lanes = slice(128 * h, 128 * h + 128)
        for sz in range(SIDE):
            await_bytes(m4.at[h, sz], v4.at[h, sz])
        for pair in range(2):
            value = half_lanes(hgr, h, pair).astype(F32) + dot(mint[...], load_half(m4, h, pair))
            value = dot_nt(eye[...], value.astype(BF)).astype(BF)
            for side in range(2):
                start = (2 * pair + side) * DG + 128 * h
                rows = DG - 128 if h == 1 else 128
                igv[pl.ds(start, rows)] = value[128 * side : 128 * side + rows]
    pltpu.make_async_copy(igv, ig_hbm, out_s.at[2]).start()

    from_mate(kgf, kh_v, ki_v)
    for g in range(GROUPS):
        held = jnp.stack([kgf[g], kgf[4 + g]], axis=1).reshape(256, 256)
        kgv[pl.ds(g * DG, DG)] = dot_nt(eye[0:DG], held).astype(BF)
    pltpu.make_async_copy(kgv, kg_hbm, out_s.at[1]).start()

    def grads_here(step):
        await_bytes(rf.at[wrapped(i - step)], gf_v.at[step])

    repeat(SIDE, grads_here, 1)
    for share in range(SIDE):
        kind, half, side = share // 4, (share // 2) % 2, share % 2
        wsum[kind, pl.ds(half * PIECE, PIECE), pl.ds(side * 128, 128)] = rf[share]
    ugv[...] = wsum[0, 0:30, 0:DG]
    dgv[...] = wsum[1, 0:30, 0:DG]
    j, lane = iotas((256, 128))
    picker = jnp.where(j == lane + 15 * lax.rem(me, 16), 1.0, 0.0)
    gains = jnp.broadcast_to(wsum[0, 30:31], (8, 256))
    picked = lax.dot_general(
        gains, picker, (((1,), (0,)), ((), ())), precision=lax.Precision.HIGHEST, preferred_element_type=F32
    )
    gnv[...] = picked[0:1, 0:15]
    pltpu.make_async_copy(ugv, ug_hbm, out_s.at[3]).start()
    pltpu.make_async_copy(dgv, dg_hbm, out_s.at[4]).start()
    pltpu.make_async_copy(gnv, gn_hbm, out_s.at[5]).start()

    for buffer, sem in ((src1, s1), (src2, s2), (src3, s3), (src4, s4)):
        for h in range(2):
            await_sent(buffer.at[h], sem.at[h])
    for m in range(4):

        @pl.when(second_z(m) != z)
        def _(m=m):
            await_bytes(pa3.at[m], pc_s.at[m])

        @pl.when(second_y(m) != y)
        def _(m=m):
            await_bytes(pb3.at[m], pd_s.at[m])

    await_bytes(ks.at[0, pl.ds(0, 7)], ks_s.at[1])
    await_bytes(kgs.at[pl.ds(0, 7)], kf_s.at[1])

    @pl.when(yo != y)
    def _():
        await_bytes(ks.at[0, 0], ks_s.at[0])
        await_bytes(kgs.at[0], kf_s.at[0])

    await_bytes(kt.at[0], ka_s.at[0])
    await_bytes(kgf.at[0], kh_s.at[0])
    await_bytes(r1a, ga_s)
    await_bytes(kra, kr_s)

    def chips_left(step):
        await_bytes(kt.at[0], ka_s.at[step])
        await_bytes(kt.at[0], kb_s.at[step])
        await_bytes(kgf.at[0], kh_s.at[step])
        await_bytes(kgf.at[0], ki_s.at[step])
        await_bytes(kgh.at[0], kc_s.at[step])
        await_bytes(h1.at[0], gb_s.at[step])

    repeat(4, chips_left, 1)

    def grads_left(step):
        await_bytes(fin, gf_s.at[step])
        await_bytes(pa1.at[0], pa_s.at[step])
        await_bytes(pb1.at[0], pb_s.at[step])

    repeat(SIDE, grads_left, 1)
    outs = ((outv, out_hbm), (kgv, kg_hbm), (igv, ig_hbm), (ugv, ug_hbm), (dgv, dg_hbm), (gnv, gn_hbm))
    for index, (held, there) in enumerate(outs):
        pltpu.make_async_copy(held, there, out_s.at[index]).wait()


def settle(*refs):
    source, there, held, sems = refs[:6], refs[6:12], refs[12:18], refs[18]
    loads = [pltpu.make_async_copy(source[index], held[index], sems.at[0, index]) for index in range(6)]
    stores = [pltpu.make_async_copy(held[index], there[index], sems.at[1, index]) for index in range(6)]
    for copy in loads:
        copy.start()
    for load, store in zip(loads, stores):
        load.wait()
        store.start()
    for copy in stores:
        copy.wait()


def local(
    inputs, cotangent, kernel_values, mix_in, mix_out, twiddle_self, twiddle_cross, norm_gain, up_weight, down_weight
):
    hbm = pl.BlockSpec(memory_space=pltpu.HBM)
    dma = pltpu.SemaphoreType.DMA
    vmem = pltpu.VMEM
    exchange = vmem((SIDE, SIDE, PIECE, 256), BF)
    halves = vmem((2, SIDE, SIDE, PIECE, 128), BF)
    part = vmem((SIDE, 4, PIECE, 128), BF)
    both = dma((2, SIDE))
    grouped = vmem((GROUPS, 256, 256), BF)
    square = vmem((256, 256), BF)
    quarter = vmem((4, SIDE, PIECE, 256), BF)
    terms = vmem((4, 64, PIECE, 128), BF)
    wide = (D, 256)
    scratch = dict(
        xv=grouped, kv=grouped, cotv=grouped, min_ref=square, mout_ref=square,
        ts_ref=vmem((6, 2, 256), BF), tc_ref=vmem((6, 2, 256), BF), gain_ref=vmem((1, D), BF),
        up_ref=vmem((DG, 1920), BF), down_ref=vmem((DG, 1920), BF),
        outv=vmem(wide, BF), igv=vmem(wide, BF), kgv=vmem(wide, BF),
        ugv=vmem((30, DG), F32), dgv=vmem((30, DG), F32), gnv=vmem((1, 15), F32),
        eye=square, mint=square, moutt=square, twp=vmem((2, 256, 256), F32),
        xg=grouped, cotg=grouped, cotn=grouped,
        upp=vmem((GROUPS, 256, 512), BF), dnp=vmem((GROUPS, 256, 512), BF), ww=vmem((D, 2048), BF),
        acot=vmem((GROUPS, 256, 512), F32), pa=vmem((256, 512), F32), act=vmem((256, 2048), BF),
        pgr=vmem((GROUPS, 256, 512), BF), hg=grouped, ng=grouped, ngr=vmem((GROUPS, 256, 256), F32),
        hgr=grouped, acc=vmem(wide, F32), gaing=vmem((GROUPS, 8, 256), F32), rowscale=vmem((256, 128), F32),
        wsum=vmem((2, 32, 256), F32),
        src1=halves, a1=halves, ks=exchange, kt=exchange, ff=vmem((SIDE, SIDE, PIECE, 128), F32), sp=halves,
        src2=halves, m2=halves, src3=halves, a3=halves, src4=halves, m4=halves,
        pa1=part, pa2=part, pa3=vmem((4, PIECE, 128), BF), pb1=part, pb2=part, pb3=vmem((4, PIECE, 128), BF),
        pc=vmem((SIDE, PIECE, 128), BF),
        twb=vmem((2, SIDE, SIDE, 12, PIECE, 128), F32),
        kgb=vmem((2, 4, SIDE, PIECE, 256), BF), kra=quarter, kgh=quarter, krb=quarter,
        kgs=vmem((SIDE, PIECE, 256), BF), kgf=exchange,
        gg=vmem((2, 4, 64, PIECE, 128), BF), r1a=terms, h1=terms, r1b=terms,
        fin=vmem((PIECE, 128), F32), rf=vmem((SIDE, PIECE, 128), F32),
        in_s=dma((19,)), out_s=dma((6,)),
        s1=both, v1=both, s2=both, v2=both, s3=both, v3=both, s4=both, v4=both,
        pa_s=dma((SIDE,)), pa_v=dma((SIDE,)), pb_s=dma((SIDE,)), pb_v=dma((SIDE,)),
        pc_s=dma((4,)), pc_v=dma((SIDE,)), pd_s=dma((4,)),
        ks_s=dma((2,)), ks_v=dma, ka_s=dma((4,)), ka_v=dma((4,)), kb_s=dma((4,)), kb_v=dma((4,)),
        kr_s=dma, kr_v=dma, kc_s=dma((4,)), kc_v=dma((4,)), kf_s=dma((2,)), kf_v=dma,
        kh_s=dma((4,)), kh_v=dma((4,)), ki_s=dma((4,)), ki_v=dma((4,)),
        ga_s=dma, ga_v=dma, gb_s=dma((4,)), gb_v=dma((4,)), gf_s=dma((SIDE,)), gf_v=dma((SIDE,)),
    )
    shape = jax.ShapeDtypeStruct
    results = [shape(wide, BF)] * 3 + [shape((30, DG), F32)] * 2 + [shape((1, 15), F32)]
    held = pl.pallas_call(
        kernel,
        out_shape=results,
        in_specs=[hbm] * 10,
        out_specs=[hbm] * 6,
        scratch_shapes=scratch,
        compiler_params=pltpu.CompilerParams(
            collective_id=0, has_side_effects=True, vmem_limit_bytes=58 * 1024 * 1024
        ),
        cost_estimate=pl.CostEstimate(flops=4_000_000_000, bytes_accessed=6_000_000, transcendentals=600_000),
    )(
        inputs[0].T, cotangent[0].T, kernel_values.T, mix_in, mix_out,
        twiddle_self.transpose(1, 0, 2), twiddle_cross.transpose(1, 0, 2),
        norm_gain[None, :], up_weight, down_weight,
    )
    output, input_grad, kernel_grad, up_grad, down_grad, gain_grad = pl.pallas_call(
        settle,
        out_shape=results,
        in_specs=[hbm] * 6,
        out_specs=[hbm] * 6,
        scratch_shapes=[vmem(result.shape, result.dtype) for result in results] + [dma((2, 6))],
        compiler_params=pltpu.CompilerParams(vmem_limit_bytes=58 * 1024 * 1024),
        cost_estimate=pl.CostEstimate(flops=0, bytes_accessed=3_000_000, transcendentals=0),
    )(*held)
    return output.T[None], input_grad.T[None], kernel_grad.T, up_grad.T, down_grad.T, gain_grad[0]


def solution(mesh):
    in_specs = (
        P("dp", "seq", None),
        P("dp", "seq", None),
        P("seq", None),
        P("seq", None),
        P("seq", None),
        P(None, None, "seq"),
        P(None, None, "seq"),
        P(),
        P(),
        P(),
    )
    out_specs = (
        P("dp", "seq", None),
        P("dp", "seq", None),
        P("seq", None),
        P(None, "seq"),
        P(None, "seq"),
        P("seq"),
    )
    return jax.shard_map(local, mesh=mesh, in_specs=in_specs, out_specs=out_specs, check_vma=False)
```

```python
import jax
import jax.numpy as jnp
from jax import lax
from jax.experimental import pallas as pl
from jax.experimental.pallas import tpu as pltpu
from jax.sharding import PartitionSpec as P

MESH = pl.DeviceIdType.MESH
BF = jnp.bfloat16
F32 = jnp.float32

D = 960
GROUPS = 4
DG = 240
FFG = 480
SIDE = 8
PIECE = 16
ROOT_HALF = 0.7978845608028654
CUBIC = 0.044715
SCALE = 131072.0**-0.5
GAIN_WINDOWS = ((0, 256), (128, 512), (384, 768), (640, 960))
HIDDEN_WINDOWS = ((0, 512), (384, 1024), (896, 1536), (1408, 1920))


def dot(a, b):
    return lax.dot_general(a, b, (((1,), (0,)), ((), ())), preferred_element_type=F32)


def dot_tn(a, b):
    return lax.dot_general(a, b, (((0,), (0,)), ((), ())), preferred_element_type=F32)


def dot_nt(a, b):
    return lax.dot_general(a, b, (((1,), (1,)), ((), ())), preferred_element_type=F32)


def iotas(shape):
    return lax.broadcasted_iota(jnp.int32, shape, 0), lax.broadcasted_iota(jnp.int32, shape, 1)


def ones_where(mask):
    return jnp.where(mask, 1.0, 0.0).astype(BF)


def repeat(count, body, start=0):
    def step(index, carry):
        body(index)
        return carry

    lax.fori_loop(start, count, step, 0)


def wrapped(value):
    return lax.rem(value + 2 * SIDE, SIDE)


def await_bytes(view, sem):
    pltpu.make_async_copy(view, view, sem).wait()


def mix(values, selfs, crosses, bits, transposed):
    for k, bit in bits:
        stride = 1 << bit
        if transposed:
            scaled = [crosses(a, k) * values[a] for a in range(SIDE)]
            values = [selfs(a, k) * values[a] + scaled[a ^ stride] for a in range(SIDE)]
        else:
            values = [selfs(a, k) * values[a] + crosses(a, k) * values[a ^ stride] for a in range(SIDE)]
    return values


def kernel(
    x_hbm, cot_hbm, ker_hbm, min_hbm, mout_hbm, ts_hbm, tc_hbm, gain_hbm, up_hbm, down_hbm,
    out_hbm, ig_hbm, kg_hbm, ug_hbm, dg_hbm, gn_hbm,
    xv, kv, cotv, min_ref, mout_ref, ts_ref, tc_ref, gain_ref, up_ref, down_ref,
    outv, igv, kgv, ugv, dgv, gnv,
    eye, mint, moutt, twp, xg, cotg, cotn, upp, dnp, ww, acot, pa, act, pgr, hg, ng, ngr, hgr, acc, gaing, rowscale, wsum,
    src1, a1, ks, kt, ff, sp, src2, m2, src3, a3, src4, m4, twb, pa1, pa2, pa3, pb1, pb2, pb3, pc,
    kgb, kra, kgh, krb, kgs, kgf, gg, r1a, h1, r1b, fin, rf,
    in_s, out_s, s1, v1, s2, v2, s3, v3, s4, v4, pa_s, pa_v, pb_s, pb_v, pc_s, pc_v, pd_s,
    ks_s, ks_v, ka_s, ka_v, kb_s, kb_v, kr_s, kr_v, kc_s, kc_v, kf_s, kf_v, kh_s, kh_v, ki_s, ki_v,
    ga_s, ga_v, gb_s, gb_v, gf_s, gf_v,
):
    loads = []

    def load(src, dst):
        copy = pltpu.make_async_copy(src, dst, in_s.at[len(loads)])
        copy.start()
        loads.append(copy)
        return copy

    def load_groups(src, dst):
        return [load(src.at[pl.ds(g * DG, DG)], dst.at[g, pl.ds(0, DG)]) for g in range(GROUPS)]

    tw_here = [load(ts_hbm, ts_ref), load(tc_hbm, tc_ref)]
    ker_here = load_groups(ker_hbm, kv)
    x_here = [load(min_hbm, min_ref)] + load_groups(x_hbm, xv)
    rest_here = load_groups(cot_hbm, cotv)
    rest_here += [load(gain_hbm, gain_ref), load(up_hbm, up_ref), load(down_hbm, down_ref), load(mout_hbm, mout_ref)]

    me = lax.axis_index("seq")
    z, y = lax.div(me, SIDE), lax.rem(me, SIDE)
    i = lax.axis_index("dp")
    chip, core = lax.div(i, 2), lax.rem(i, 2)
    mate = i + 1 - 2 * core
    yo = wrapped(i - y)
    tz_at = [wrapped(z + step) for step in range(SIDE)]
    ty_at = [wrapped(y + step) for step in range(SIDE)]

    barrier = pltpu.get_barrier_semaphore()

    def greet_seq(step):
        pl.semaphore_signal(
            barrier, inc=1, device_id=(i, lax.rem(me + step, 64)), device_id_type=MESH
        )

    def greet_dp(step):
        pl.semaphore_signal(barrier, inc=1, device_id=(wrapped(i + step), me), device_id_type=MESH)

    repeat(64, greet_seq, 1)
    repeat(8, greet_dp, 1)

    def send(src, dst, ssem, rsem, device):
        pltpu.make_async_remote_copy(
            src_ref=src, dst_ref=dst, send_sem=ssem, recv_sem=rsem, device_id=device, device_id_type=MESH
        ).start()

    def send_part(part, src, dst, ssem, rsem):
        offsets = ((3, 5, 1, 7), (2, 6, 4, 0))[part]

        def one(dz, ty):
            tz = tz_at[dz]
            send(src(tz, ty), dst, ssem.at[dz], rsem, (i, tz * SIDE + ty))

        def pair(t):
            for dy in (3 - t, 5 + t):
                ty = wrapped(y + dy)
                for dz in offsets:
                    one(dz, ty)

        repeat(3, pair)
        for dy in (4, 0):
            for dz in offsets:
                if (dz, dy) != (0, 0):
                    one(dz, ty_at[dy])
        if part == 1:
            pltpu.make_async_copy(src(z, y), dst, rsem).start()

    def await_sent(buffer, ssem):
        await_bytes(buffer.at[0, pl.ds(0, 7)], ssem.at[0])
        for dz in range(1, SIDE):
            await_bytes(buffer.at[0], ssem.at[dz])

    def store_half(ref, h, pair, value):
        for side in range(2):
            split = value[:, 128 * side : 128 * side + 128].reshape(SIDE, 2, PIECE, 128)
            ref[h, :, 2 * pair + side] = split[:, 0]
            ref[h, :, 4 + 2 * pair + side] = split[:, 1]

    def load_half(ref, h, pair):
        groups = (2 * pair, 2 * pair + 1)
        return jnp.concatenate(
            [jnp.stack([ref[h, :, g], ref[h, :, 4 + g]], axis=1).reshape(256, 128) for g in groups], axis=1
        )

    def half_lanes(ref, h, pair):
        return jnp.concatenate([ref[2 * pair + side, :, 128 * h : 128 * h + 128] for side in range(2)], axis=1)

    def slot(chip_at, core_at):
        return wrapped(2 * chip_at + core_at - y)

    def to_chips(buffer, ssem, rsem):
        send(buffer.at[yo], buffer.at[yo], ssem.at[0], rsem.at[0], (mate, me))

        def step_to(step):
            send(
                buffer.at[yo], buffer.at[yo], ssem.at[step], rsem.at[step],
                (2 * lax.rem(chip + step, 4) + core, me),
            )

        repeat(4, step_to, 1)

    def to_mate(buffer, rsem, ssem2, rsem2):
        def step_to(step):
            held = buffer.at[slot(lax.rem(chip + 4 - step, 4), core)]
            await_bytes(held, rsem.at[step])
            send(held, held, ssem2.at[step], rsem2.at[step], (mate, me))

        repeat(4, step_to, 1)

    def from_mate(buffer, rsem, rsem2):
        await_bytes(buffer.at[slot(chip, 1 - core)], rsem.at[0])

        def step_from(step):
            await_bytes(buffer.at[slot(lax.rem(chip + 4 - step, 4), 1 - core)], rsem2.at[step])

        repeat(4, step_from, 1)

    r, l = iotas((256, 256))
    eye[...] = ones_where(r == l)
    twp[...] = jnp.zeros_like(twp)
    for copy in tw_here:
        copy.wait()
    for k in range(6):
        for which in range(2):
            twp[which, pl.ds(DG + k, 1)] = ts_ref[k, which : which + 1].astype(F32)
            twp[which, pl.ds(DG + 8 + k, 1)] = tc_ref[k, which : which + 1].astype(F32)
    for copy in ker_here:
        copy.wait()
    for g in range(GROUPS):
        kv[g, pl.ds(DG, PIECE)] = twp[1, pl.ds(DG, PIECE)].astype(BF)
        split = dot_nt(eye[...], kv[g]).astype(BF).reshape(SIDE, 2, PIECE, 256)
        ks[:, g] = split[:, 0]
        ks[:, 4 + g] = split[:, 1]
    columns = dot_nt(eye[...], twp[0].astype(BF))[:, 128:256]
    for copy in x_here:
        copy.wait()
    for g in range(GROUPS):
        xv[g, pl.ds(DG, PIECE)] = jnp.zeros((PIECE, 256), BF)

    def premix(h):
        for pair in range(2):
            rows = jnp.concatenate([xv[2 * pair + side, 128 * h : 128 * h + 128] for side in range(2)], axis=0)
            value = dot_nt(min_ref[...], rows)
            if h == 1:
                value = value + jnp.concatenate([columns, columns], axis=1)
            store_half(src1, h, pair, value.astype(BF))

    premix(1)
    pl.semaphore_wait(barrier, 70)

    def share_kernel(dz):
        tz = wrapped(z + dz)
        send(ks.at[tz, yo], kt.at[y, z], ks_s.at[1], ks_v, (i, tz * SIDE + yo))

    repeat(SIDE, share_kernel, 1)

    @pl.when(yo != y)
    def _():
        send(ks.at[z, yo], kt.at[y, z], ks_s.at[0], ks_v, (i, z * SIDE + yo))

    @pl.when(yo == y)
    def _():
        pltpu.make_async_copy(ks.at[z, yo], kt.at[y, z], ks_v).start()

    def half_of(h, src, dst, ssem, rsem, at, group):
        return (lambda tz, ty: src.at[h, tz, ty], dst.at[(h,) + at], ssem.at[h], rsem.at[h, group])

    for h in (1, 0):
        first = half_of(h, src1, a1, s1, v1, (z, y), z)
        if h == 0:
            premix(0)
        send_part(0, *first)
        if h == 1:
            await_bytes(kt.at[yo], ks_v)
            to_chips(kt, ka_s, ka_v)
        else:
            to_mate(kt, ka_v, kb_s, kb_v)
        send_part(1, *first)

    def spread_twiddles(which, p, q, slab):
        wide = slab.astype(F32)
        for k in range(6):
            twb[which, p, q, k] = jnp.broadcast_to(wide[:, 112 + k : 113 + k], (PIECE, 128))
            twb[which, p, q, 6 + k] = jnp.broadcast_to(wide[:, 120 + k : 121 + k], (PIECE, 128))

    def mixed(values, which, shards, bits, transposed):
        def selfs(a, k):
            return twb[which, shards[a][0], shards[a][1], k]

        def crosses(a, k):
            return twb[which, shards[a][0], shards[a][1], 6 + k]

        return mix(values, selfs, crosses, bits, transposed)

    low_bits = ((0, 0), (1, 1), (2, 2))
    high_bits = ((3, 0), (4, 1), (5, 2))
    low_back = tuple(reversed(low_bits))
    high_back = tuple(reversed(high_bits))

    def row_of(sz):
        return [(sz, a) for a in range(SIDE)]

    def column_of(sy):
        return [(a, sy) for a in range(SIDE)]

    def two_at_once(lines, read, which, bits, transposed, write):
        def step(t):
            groups = [lines(2 * t), lines(2 * t + 1)]
            held = [[read(p, q) for p, q in shards] for shards in groups]
            held = [mixed(values, which, shards, bits, transposed) for values, shards in zip(held, groups)]
            for shards, values in zip(groups, held):
                for (p, q), value in zip(shards, values):
                    write(p, q, value)

        repeat(SIDE // 2, step)

    def store_wide(p, q, value):
        ff[p, q] = value

    def load_wide(p, q):
        return ff[p, q]

    from_mate(kt, ka_v, kb_v)

    def spread_output_twiddles(sz):
        for p, q in row_of(sz):
            spread_twiddles(1, p, q, kt[q, p, :, 128:256])

    repeat(SIDE, spread_output_twiddles)

    for h in (1, 0):
        lanes = slice(128 * h, 128 * h + 128)

        def forward_one(step, h=h):
            sz = wrapped(z + step)
            await_bytes(a1.at[h, sz], v1.at[h, sz])
            shards = row_of(sz)
            if h == 1:
                for p, q in shards:
                    spread_twiddles(0, p, q, a1[1, p, q])
            values = mixed([a1[h, p, q].astype(F32) for p, q in shards], 0, shards, low_bits, False)
            for (p, q), value in zip(shards, values):
                ff[p, q] = value

        repeat(SIDE, forward_one)

        def weigh(p, q, value, h=h, lanes=lanes):
            rounded = value.astype(BF)
            sp[h, p, q] = rounded
            ff[p, q] = rounded.astype(F32) * kt[q, p, :, lanes].astype(F32)

        def leave(p, q, value, h=h):
            src2[h, p, q] = value.astype(BF)

        two_at_once(column_of, load_wide, 0, high_bits, False, weigh)
        two_at_once(row_of, load_wide, 1, low_bits, False, store_wide)
        two_at_once(column_of, load_wide, 1, high_bits, False, leave)
        for part in range(2):
            send_part(part, *half_of(h, src2, m2, s2, v2, (z, y), z))
        if h == 1:
            for copy in rest_here:
                copy.wait()
            for g in range(GROUPS):
                xg[g] = dot_nt(eye[...], xv[g]).astype(BF)
                cotv[g, pl.ds(DG, PIECE)] = jnp.zeros((PIECE, 256), BF)
            mint[...] = dot_nt(eye[...], min_ref[...]).astype(BF)
            moutt[...] = dot_nt(eye[...], mout_ref[...]).astype(BF)
            for g in range(GROUPS):
                cotn[g] = dot_nt(eye[...], cotv[g]).astype(BF)
                picked = jnp.zeros((256, 256), F32)
                for part in range(GROUPS):
                    j, lane = iotas((256, 256))
                    picked = picked + dot(ones_where((part * DG + lane == 4 * j + g) & (lane < DG)), cotv[part])
                cotg[g] = dot_nt(eye[...], picked.astype(BF)).astype(BF)
                low, high = GAIN_WINDOWS[g]
                channel, lane = iotas((high - low, 256))
                gain_rows = jnp.broadcast_to(gain_ref[:, low:high].astype(F32), (PIECE, high - low)).astype(BF)
                gaing[g] = dot(gain_rows, ones_where((channel + low == g * DG + lane) & (lane < DG)))[0:8]


    for g in range(GROUPS):
        low, high = HIDDEN_WINDOWS[g]
        column, hidden_unit = iotas((high - low, 512))
        chosen = (column + low == g * FFG + hidden_unit - 2 * (hidden_unit >> 5)) & ((hidden_unit & 31) < 30)
        chooser = ones_where(chosen)
        upp[g, 0:DG] = dot(up_ref[:, low:high], chooser).astype(BF)
        dnp[g, 0:DG] = dot(down_ref[:, low:high], chooser).astype(BF)
        upp[g, DG:256] = jnp.zeros((256 - DG, 512), BF)
        dnp[g, DG:256] = jnp.zeros((256 - DG, 512), BF)

    for g in range(GROUPS):
        acot[g] = dot(cotg[g], dnp[g])
        channel, j = iotas((D, 256))
        spread = ones_where((channel == 4 * j + g) & (j < DG))
        ww[:, pl.ds(g * 512, 512)] = dot(spread, dnp[g]).astype(BF)

    lane_here = (lax.broadcasted_iota(jnp.int32, (256, 256), 1) & 127) < DG - 128
    squares = jnp.zeros((256, 1), F32)
    for h in (1, 0):
        for sz in range(SIDE):
            await_bytes(m2.at[h, sz], v2.at[h, sz])
        for pair in range(2):
            value = half_lanes(xg, h, pair).astype(F32) + dot(mout_ref[...], load_half(m2, h, pair))
            if h == 1:
                value = jnp.where(lane_here, value, 0.0)
            value = value.astype(BF)
            for side in range(2):
                hg[2 * pair + side, :, 128 * h : 128 * h + 128] = value[:, 128 * side : 128 * side + 128]
            wide = value.astype(F32)
            squares = squares + jnp.sum(wide * wide, axis=1, keepdims=True)
    scale_column = lax.rsqrt(squares * (1.0 / D) + 1e-06)
    rowscale[...] = jnp.broadcast_to(scale_column, (256, 128))

    for g in range(GROUPS):
        wide = hg[g].astype(F32)
        ng[g] = (wide * rowscale[:, 0:1] * gaing[g, 0:1]).astype(BF)
        pa[...] = dot(ng[g], upp[g])

        def activate(tile, g=g):
            rows = pl.ds(pl.multiple_of(tile * 64, 64), 64)
            p = pa[rows]
            square = p * p
            tangent = jnp.tanh(p * (ROOT_HALF + (ROOT_HALF * CUBIC) * square))
            half_more = 0.5 + 0.5 * tangent
            act[rows, pl.ds(g * 512, 512)] = (p * half_more).astype(BF)
            inner = ROOT_HALF + (3.0 * ROOT_HALF * CUBIC) * square
            slope = half_more + 0.5 * p * (1.0 - tangent * tangent) * inner
            pgr[g, rows] = (acot[g, rows] * slope).astype(BF)

        repeat(4, activate)
        ngr[g] = dot_nt(pgr[g], upp[g])

    means = jnp.zeros((256, 1), F32)
    for g in range(GROUPS):
        means = means + jnp.sum(ngr[g] * gaing[g, 0:1] * hg[g].astype(F32), axis=1, keepdims=True)
    scale_column = rowscale[:, 0:1]
    means = means * (1.0 / D) * scale_column * scale_column * scale_column
    def split_terms(kind, g, term):
        split = term.astype(BF).reshape(16, 2, PIECE, 256)
        for half in range(2):
            for side in range(2):
                gg[side, 2 * kind + half, pl.ds(g * 16, 16)] = split[:, half, :, side * 128 : side * 128 + 128]

    def weight_terms():
        row_here = (lax.broadcasted_iota(jnp.int32, (512, 256), 0) & 31) == 30
        for g in range(GROUPS):
            split_terms(1, g, dot_tn(act[:, pl.ds(g * 512, 512)], cotg[g]))
        send(gg.at[1 - core, pl.ds(2, 2)], r1a.at[pl.ds(2, 2)], ga_s.at[1], ga_v.at[1], (mate, me))
        for g in range(GROUPS):
            gain_term = jnp.sum(ngr[g] * hg[g].astype(F32) * rowscale[:, 0:1], axis=0, keepdims=True)
            split_terms(0, g, jnp.where(row_here, gain_term, dot_tn(pgr[g], ng[g])))
        send(gg.at[1 - core, pl.ds(0, 2)], r1a.at[pl.ds(0, 2)], ga_s.at[0], ga_v.at[0], (mate, me))

    for h in (1, 0):
        lanes = slice(128 * h, 128 * h + 128)
        for pair in range(2):
            for g in (2 * pair, 2 * pair + 1):
                gained = ngr[g, :, lanes] * gaing[g, 0:1, lanes]
                wide = hg[g, :, lanes].astype(F32)
                hgr[g, :, lanes] = (cotn[g, :, lanes].astype(F32) + scale_column * gained - wide * means).astype(BF)
            store_half(src3, h, pair, dot(moutt[...], half_lanes(hgr, h, pair)).astype(BF))
        for part in range(2):
            send_part(part, *half_of(h, src3, a3, s3, v3, (y, z), y))
        if h == 1:
            weight_terms()

    for kind in (1, 0):
        await_bytes(r1a.at[pl.ds(2 * kind, 2)], ga_v.at[kind])

    def pair_sum(step):
        for slab in range(4):
            part = pl.ds(pl.multiple_of(step * 8, 8), 8)
            both = gg[core, slab, part].astype(F32) + r1a[slab, part].astype(F32)
            h1[slab, part] = both.astype(BF)

    repeat(8, pair_sum)

    def spread_terms(step):
        other = lax.rem(chip + step, 4)
        send(h1.at[other], r1b.at[chip], gb_s.at[step], gb_v.at[step], (other * 2 + core, me))

    repeat(4, spread_terms, 1)

    others = [lax.rem(chip + step, 4) for step in (1, 2, 3)]

    for h in (1, 0):
        lanes = slice(128 * h, 128 * h + 128)

        def backward_one(step, h=h):
            sy = wrapped(y + step)
            await_bytes(a3.at[h, sy], v3.at[h, sy])
            shards = column_of(sy)
            values = mixed([a3[h, q, p].astype(F32) for p, q in shards], 1, shards, high_back, True)
            for (p, q), value in zip(shards, values):
                ff[p, q] = value

        repeat(SIDE, backward_one)

        def weigh_back(p, q, value, h=h, lanes=lanes):
            wide = value.astype(BF).astype(F32)
            owner = wrapped(q + y)
            kgb[lax.rem(owner, 2), lax.div(owner, 2), p, :, lanes] = (sp[h, p, q].astype(F32) * wide).astype(BF)
            ff[p, q] = wide * kt[q, p, :, lanes].astype(F32)

        def leave_back(p, q, value, h=h):
            src4[h, p, q] = value.astype(BF)

        two_at_once(row_of, load_wide, 1, low_back, True, weigh_back)
        if h == 0:
            send(kgb.at[1 - core], kra, kr_s, kr_v, (mate, me))
        two_at_once(column_of, load_wide, 0, high_back, True, store_wide)
        two_at_once(row_of, load_wide, 0, low_back, True, leave_back)
        last = half_of(h, src4, m4, s4, v4, (z, y), z)
        send_part(0, *last)
        if h == 1:
            send_part(1, *last)

    await_bytes(kra, kr_v)

    def kernel_pair(sz):
        for at in range(4):
            kgh[at, sz] = (kgb[core, at, sz].astype(F32) + kra[at, sz].astype(F32)).astype(BF)

    repeat(SIDE, kernel_pair)

    def spread_kernel_terms(step):
        other = lax.rem(chip + step, 4)
        send(kgh.at[other], krb.at[chip], kc_s.at[step], kc_v.at[step], (other * 2 + core, me))

    repeat(4, spread_kernel_terms, 1)

    def kernel_terms_here(step):
        await_bytes(krb.at[lax.rem(chip + 4 - step, 4)], kc_v.at[step])

    repeat(4, kernel_terms_here, 1)

    def kernel_sum(sz):
        four = kgh[chip, sz].astype(F32)
        for other in others:
            four = four + krb[other, sz].astype(F32)
        kgs[sz] = four.astype(BF)

    repeat(SIDE, kernel_sum)

    def return_kernel(dz):
        tz = wrapped(z + dz)
        send(kgs.at[tz], kgf.at[y, z], kf_s.at[1], kf_v, (i, tz * SIDE + yo))

    repeat(SIDE, return_kernel, 1)

    @pl.when(yo != y)
    def _():
        send(kgs.at[z], kgf.at[y, z], kf_s.at[0], kf_v, (i, z * SIDE + yo))

    @pl.when(yo == y)
    def _():
        pltpu.make_async_copy(kgs.at[z], kgf.at[y, z], kf_v).start()

    send_part(1, *last)

    def terms_here(step):
        await_bytes(r1b.at[lax.rem(chip + 4 - step, 4)], gb_v.at[step])

    repeat(4, terms_here, 1)

    def chip_sum(t):
        for odd in range(2):
            sz = 2 * t + odd
            part = pl.ds(pl.multiple_of(sz * 8, 8), 8)
            four = h1[chip, part].astype(F32)
            for other in others:
                four = four + r1b[other, part].astype(F32)
            four = four.astype(BF)
            for q in range(SIDE):
                if (odd + q) % 2 == 0:
                    pa1[q, t] = four[q]
                else:
                    pb1[sz, q // 2] = four[q]

    repeat(SIDE // 2, chip_sum)

    def along_y(step):
        ty = wrapped(y + step)
        send(pa1.at[ty], pa2.at[y], pa_s.at[step], pa_v.at[step], (i, z * SIDE + ty))

    def along_z(step):
        tz = wrapped(z + step)
        send(pb1.at[tz], pb2.at[z], pb_s.at[step], pb_v.at[step], (i, tz * SIDE + y))

    def first_step(step):
        along_y(step)
        along_z(step)

    repeat(SIDE, first_step, 1)

    acc[...] = dot_nt(ww[...], act[...])
    for g in range(GROUPS):
        rows = pl.ds(g * DG, DG)
        outv[rows] = (acc[rows] + dot_nt(eye[0:DG], hg[g])).astype(BF)
    pltpu.make_async_copy(outv, out_hbm, out_s.at[0]).start()

    def first_here(step):
        await_bytes(pa2.at[wrapped(y - step)], pa_v.at[step])
        await_bytes(pb2.at[wrapped(z - step)], pb_v.at[step])

    repeat(SIDE, first_here, 1)
    sum_y, sum_z = pa1[y].astype(F32), pb1[z].astype(F32)
    for step in range(1, SIDE):
        sum_y = sum_y + pa2[wrapped(y + step)].astype(F32)
        sum_z = sum_z + pb2[wrapped(z + step)].astype(F32)
    pa3[...] = sum_y.astype(BF)
    pb3[...] = sum_z.astype(BF)
    odd = lax.rem(z + y, 2)

    def second_z(m):
        return 2 * m + lax.rem(y, 2)

    def second_y(m):
        return 2 * m + 1 - lax.rem(z, 2)

    for m in range(4):

        @pl.when(second_z(m) != z)
        def _(m=m):
            send(pa3.at[m], pc.at[z], pc_s.at[m], pc_v.at[z], (i, second_z(m) * SIDE + y))

        @pl.when(second_y(m) != y)
        def _(m=m):
            send(pb3.at[m], pc.at[y], pd_s.at[m], pc_v.at[y], (i, z * SIDE + second_y(m)))

    @pl.when(odd == 0)
    def _():
        pc[z] = pa3[lax.div(z, 2)]

    @pl.when(odd == 1)
    def _():
        pc[y] = pb3[lax.div(y, 2)]

    await_bytes(kgf.at[yo], kf_v)
    to_chips(kgf, kh_s, kh_v)

    own = z + odd * (y - z)

    def second_here(step):
        at = wrapped(own + step)
        await_bytes(pc.at[at], pc_v.at[at])

    repeat(SIDE, second_here, 1)
    shard_sum = pc[0].astype(F32)
    for at in range(1, SIDE):
        shard_sum = shard_sum + pc[at].astype(F32)
    shard_sum = shard_sum * SCALE
    fin[...] = shard_sum
    rf[i] = shard_sum

    def spread_grads(step):
        send(fin, rf.at[i], gf_s.at[step], gf_v.at[step], (wrapped(i + step), me))

    repeat(SIDE, spread_grads, 1)
    to_mate(kgf, kh_v, ki_s, ki_v)

    for h in (1, 0):
        lanes = slice(128 * h, 128 * h + 128)
        for sz in range(SIDE):
            await_bytes(m4.at[h, sz], v4.at[h, sz])
        for pair in range(2):
            value = half_lanes(hgr, h, pair).astype(F32) + dot(mint[...], load_half(m4, h, pair))
            value = dot_nt(eye[...], value.astype(BF)).astype(BF)
            for side in range(2):
                start = (2 * pair + side) * DG + 128 * h
                rows = DG - 128 if h == 1 else 128
                igv[pl.ds(start, rows)] = value[128 * side : 128 * side + rows]
    pltpu.make_async_copy(igv, ig_hbm, out_s.at[2]).start()

    from_mate(kgf, kh_v, ki_v)
    for g in range(GROUPS):
        held = jnp.stack([kgf[g], kgf[4 + g]], axis=1).reshape(256, 256)
        kgv[pl.ds(g * DG, DG)] = dot_nt(eye[0:DG], held).astype(BF)
    pltpu.make_async_copy(kgv, kg_hbm, out_s.at[1]).start()

    def grads_here(step):
        await_bytes(rf.at[wrapped(i - step)], gf_v.at[step])

    repeat(SIDE, grads_here, 1)
    for share in range(SIDE):
        kind, half, side = share // 4, (share // 2) % 2, share % 2
        wsum[kind, pl.ds(half * PIECE, PIECE), pl.ds(side * 128, 128)] = rf[share]
    ugv[...] = wsum[0, 0:30, 0:DG]
    dgv[...] = wsum[1, 0:30, 0:DG]
    j, lane = iotas((256, 128))
    picker = jnp.where(j == lane + 15 * lax.rem(me, 16), 1.0, 0.0)
    gains = jnp.broadcast_to(wsum[0, 30:31], (8, 256))
    picked = lax.dot_general(
        gains, picker, (((1,), (0,)), ((), ())), precision=lax.Precision.HIGHEST, preferred_element_type=F32
    )
    gnv[...] = picked[0:1, 0:15]
    pltpu.make_async_copy(ugv, ug_hbm, out_s.at[3]).start()
    pltpu.make_async_copy(dgv, dg_hbm, out_s.at[4]).start()
    pltpu.make_async_copy(gnv, gn_hbm, out_s.at[5]).start()

    for buffer, sem in ((src1, s1), (src2, s2), (src3, s3), (src4, s4)):
        for h in range(2):
            await_sent(buffer.at[h], sem.at[h])
    for m in range(4):

        @pl.when(second_z(m) != z)
        def _(m=m):
            await_bytes(pa3.at[m], pc_s.at[m])

        @pl.when(second_y(m) != y)
        def _(m=m):
            await_bytes(pb3.at[m], pd_s.at[m])

    await_bytes(ks.at[0, pl.ds(0, 7)], ks_s.at[1])
    await_bytes(kgs.at[pl.ds(0, 7)], kf_s.at[1])

    @pl.when(yo != y)
    def _():
        await_bytes(ks.at[0, 0], ks_s.at[0])
        await_bytes(kgs.at[0], kf_s.at[0])

    await_bytes(kt.at[0], ka_s.at[0])
    await_bytes(kgf.at[0], kh_s.at[0])
    for kind in range(2):
        await_bytes(r1a.at[pl.ds(0, 2)], ga_s.at[kind])
    await_bytes(kra, kr_s)

    def chips_left(step):
        await_bytes(kt.at[0], ka_s.at[step])
        await_bytes(kt.at[0], kb_s.at[step])
        await_bytes(kgf.at[0], kh_s.at[step])
        await_bytes(kgf.at[0], ki_s.at[step])
        await_bytes(kgh.at[0], kc_s.at[step])
        await_bytes(h1.at[0], gb_s.at[step])

    repeat(4, chips_left, 1)

    def grads_left(step):
        await_bytes(fin, gf_s.at[step])
        await_bytes(pa1.at[0], pa_s.at[step])
        await_bytes(pb1.at[0], pb_s.at[step])

    repeat(SIDE, grads_left, 1)
    outs = ((outv, out_hbm), (kgv, kg_hbm), (igv, ig_hbm), (ugv, ug_hbm), (dgv, dg_hbm), (gnv, gn_hbm))
    for index, (held, there) in enumerate(outs):
        pltpu.make_async_copy(held, there, out_s.at[index]).wait()


def settle(*refs):
    source, there, held, sems = refs[:6], refs[6:12], refs[12:18], refs[18]
    loads = [pltpu.make_async_copy(source[index], held[index], sems.at[0, index]) for index in range(6)]
    stores = [pltpu.make_async_copy(held[index], there[index], sems.at[1, index]) for index in range(6)]
    for copy in loads:
        copy.start()
    for load, store in zip(loads, stores):
        load.wait()
        store.start()
    for copy in stores:
        copy.wait()


def local(
    inputs, cotangent, kernel_values, mix_in, mix_out, twiddle_self, twiddle_cross, norm_gain, up_weight, down_weight
):
    hbm = pl.BlockSpec(memory_space=pltpu.HBM)
    dma = pltpu.SemaphoreType.DMA
    vmem = pltpu.VMEM
    exchange = vmem((SIDE, SIDE, PIECE, 256), BF)
    halves = vmem((2, SIDE, SIDE, PIECE, 128), BF)
    part = vmem((SIDE, 4, PIECE, 128), BF)
    both = dma((2, SIDE))
    grouped = vmem((GROUPS, 256, 256), BF)
    square = vmem((256, 256), BF)
    quarter = vmem((4, SIDE, PIECE, 256), BF)
    terms = vmem((4, 64, PIECE, 128), BF)
    wide = (D, 256)
    scratch = dict(
        xv=grouped, kv=grouped, cotv=grouped, min_ref=square, mout_ref=square,
        ts_ref=vmem((6, 2, 256), BF), tc_ref=vmem((6, 2, 256), BF), gain_ref=vmem((1, D), BF),
        up_ref=vmem((DG, 1920), BF), down_ref=vmem((DG, 1920), BF),
        outv=vmem(wide, BF), igv=vmem(wide, BF), kgv=vmem(wide, BF),
        ugv=vmem((30, DG), F32), dgv=vmem((30, DG), F32), gnv=vmem((1, 15), F32),
        eye=square, mint=square, moutt=square, twp=vmem((2, 256, 256), F32),
        xg=grouped, cotg=grouped, cotn=grouped,
        upp=vmem((GROUPS, 256, 512), BF), dnp=vmem((GROUPS, 256, 512), BF), ww=vmem((D, 2048), BF),
        acot=vmem((GROUPS, 256, 512), F32), pa=vmem((256, 512), F32), act=vmem((256, 2048), BF),
        pgr=vmem((GROUPS, 256, 512), BF), hg=grouped, ng=grouped, ngr=vmem((GROUPS, 256, 256), F32),
        hgr=grouped, acc=vmem(wide, F32), gaing=vmem((GROUPS, 8, 256), F32), rowscale=vmem((256, 128), F32),
        wsum=vmem((2, 32, 256), F32),
        src1=halves, a1=halves, ks=exchange, kt=exchange, ff=vmem((SIDE, SIDE, PIECE, 128), F32), sp=halves,
        src2=halves, m2=halves, src3=halves, a3=halves, src4=halves, m4=halves,
        pa1=part, pa2=part, pa3=vmem((4, PIECE, 128), BF), pb1=part, pb2=part, pb3=vmem((4, PIECE, 128), BF),
        pc=vmem((SIDE, PIECE, 128), BF),
        twb=vmem((2, SIDE, SIDE, 12, PIECE, 128), F32),
        kgb=vmem((2, 4, SIDE, PIECE, 256), BF), kra=quarter, kgh=quarter, krb=quarter,
        kgs=vmem((SIDE, PIECE, 256), BF), kgf=exchange,
        gg=vmem((2, 4, 64, PIECE, 128), BF), r1a=terms, h1=terms, r1b=terms,
        fin=vmem((PIECE, 128), F32), rf=vmem((SIDE, PIECE, 128), F32),
        in_s=dma((19,)), out_s=dma((6,)),
        s1=both, v1=both, s2=both, v2=both, s3=both, v3=both, s4=both, v4=both,
        pa_s=dma((SIDE,)), pa_v=dma((SIDE,)), pb_s=dma((SIDE,)), pb_v=dma((SIDE,)),
        pc_s=dma((4,)), pc_v=dma((SIDE,)), pd_s=dma((4,)),
        ks_s=dma((2,)), ks_v=dma, ka_s=dma((4,)), ka_v=dma((4,)), kb_s=dma((4,)), kb_v=dma((4,)),
        kr_s=dma, kr_v=dma, kc_s=dma((4,)), kc_v=dma((4,)), kf_s=dma((2,)), kf_v=dma,
        kh_s=dma((4,)), kh_v=dma((4,)), ki_s=dma((4,)), ki_v=dma((4,)),
        ga_s=dma((2,)), ga_v=dma((2,)), gb_s=dma((4,)), gb_v=dma((4,)), gf_s=dma((SIDE,)), gf_v=dma((SIDE,)),
    )
    shape = jax.ShapeDtypeStruct
    results = [shape(wide, BF)] * 3 + [shape((30, DG), F32)] * 2 + [shape((1, 15), F32)]
    held = pl.pallas_call(
        kernel,
        out_shape=results,
        in_specs=[hbm] * 10,
        out_specs=[hbm] * 6,
        scratch_shapes=scratch,
        compiler_params=pltpu.CompilerParams(
            collective_id=0, has_side_effects=True, vmem_limit_bytes=58 * 1024 * 1024
        ),
        cost_estimate=pl.CostEstimate(flops=4_000_000_000, bytes_accessed=6_000_000, transcendentals=600_000),
    )(
        inputs[0].T, cotangent[0].T, kernel_values.T, mix_in, mix_out,
        twiddle_self.transpose(1, 0, 2), twiddle_cross.transpose(1, 0, 2),
        norm_gain[None, :], up_weight, down_weight,
    )
    output, input_grad, kernel_grad, up_grad, down_grad, gain_grad = pl.pallas_call(
        settle,
        out_shape=results,
        in_specs=[hbm] * 6,
        out_specs=[hbm] * 6,
        scratch_shapes=[vmem(result.shape, result.dtype) for result in results] + [dma((2, 6))],
        compiler_params=pltpu.CompilerParams(vmem_limit_bytes=58 * 1024 * 1024),
        cost_estimate=pl.CostEstimate(flops=0, bytes_accessed=3_000_000, transcendentals=0),
    )(*held)
    return output.T[None], input_grad.T[None], kernel_grad.T, up_grad.T, down_grad.T, gain_grad[0]


def solution(mesh):
    in_specs = (
        P("dp", "seq", None),
        P("dp", "seq", None),
        P("seq", None),
        P("seq", None),
        P("seq", None),
        P(None, None, "seq"),
        P(None, None, "seq"),
        P(),
        P(),
        P(),
    )
    out_specs = (
        P("dp", "seq", None),
        P("dp", "seq", None),
        P("seq", None),
        P(None, "seq"),
        P(None, "seq"),
        P("seq"),
    )
    return jax.shard_map(local, mesh=mesh, in_specs=in_specs, out_specs=out_specs, check_vma=False)
```

```python
import jax
import jax.numpy as jnp
from jax import lax
from jax.experimental import pallas as pl
from jax.experimental.pallas import tpu as pltpu
from jax.sharding import PartitionSpec as P

MESH = pl.DeviceIdType.MESH
BF = jnp.bfloat16
F32 = jnp.float32

D = 960
GROUPS = 4
DG = 240
FFG = 480
SIDE = 8
PIECE = 16
ROOT_HALF = 0.7978845608028654
CUBIC = 0.044715
SCALE = 131072.0**-0.5
GAIN_WINDOWS = ((0, 256), (128, 512), (384, 768), (640, 960))
HIDDEN_WINDOWS = ((0, 512), (384, 1024), (896, 1536), (1408, 1920))


def dot(a, b):
    return lax.dot_general(a, b, (((1,), (0,)), ((), ())), preferred_element_type=F32)


def dot_tn(a, b):
    return lax.dot_general(a, b, (((0,), (0,)), ((), ())), preferred_element_type=F32)


def dot_nt(a, b):
    return lax.dot_general(a, b, (((1,), (1,)), ((), ())), preferred_element_type=F32)


def iotas(shape):
    return lax.broadcasted_iota(jnp.int32, shape, 0), lax.broadcasted_iota(jnp.int32, shape, 1)


def ones_where(mask):
    return jnp.where(mask, 1.0, 0.0).astype(BF)


def repeat(count, body, start=0):
    def step(index, carry):
        body(index)
        return carry

    lax.fori_loop(start, count, step, 0)


def wrapped(value):
    return lax.rem(value + 2 * SIDE, SIDE)


def await_bytes(view, sem):
    pltpu.make_async_copy(view, view, sem).wait()


def mix(values, selfs, crosses, bits, transposed):
    for k, bit in bits:
        stride = 1 << bit
        if transposed:
            scaled = [crosses(a, k) * values[a] for a in range(SIDE)]
            values = [selfs(a, k) * values[a] + scaled[a ^ stride] for a in range(SIDE)]
        else:
            values = [selfs(a, k) * values[a] + crosses(a, k) * values[a ^ stride] for a in range(SIDE)]
    return values


def kernel(
    x_hbm, cot_hbm, ker_hbm, min_hbm, mout_hbm, ts_hbm, tc_hbm, gain_hbm, up_hbm, down_hbm,
    out_hbm, ig_hbm, kg_hbm, ug_hbm, dg_hbm, gn_hbm,
    xv, kv, cotv, min_ref, mout_ref, ts_ref, tc_ref, gain_ref, up_ref, down_ref,
    outv, igv, kgv, ugv, dgv, gnv,
    eye, mint, moutt, twp, xg, cotg, cotn, upp, dnp, ww, acot, pa, act, pgr, hg, ng, ngr, hgr, acc, gaing, rowscale, wsum,
    src1, a1, ks, kt, ff, sp, src2, m2, src3, a3, src4, m4, twb, pa1, pa2, pa3, pb1, pb2, pb3, pc,
    kgb, kra, kgh, krb, kgs, kgf, gg, r1a, h1, r1b, fin, rf,
    in_s, out_s, s1, v1, s2, v2, s3, v3, s4, v4, pa_s, pa_v, pb_s, pb_v, pc_s, pc_v, pd_s,
    ks_s, ks_v, ka_s, ka_v, kb_s, kb_v, kr_s, kr_v, kc_s, kc_v, kf_s, kf_v, kh_s, kh_v, ki_s, ki_v,
    ga_s, ga_v, gb_s, gb_v, gf_s, gf_v,
):
    loads = []

    def load(src, dst):
        copy = pltpu.make_async_copy(src, dst, in_s.at[len(loads)])
        copy.start()
        loads.append(copy)
        return copy

    def load_groups(src, dst):
        return [load(src.at[pl.ds(g * DG, DG)], dst.at[g, pl.ds(0, DG)]) for g in range(GROUPS)]

    tw_here = [load(ts_hbm, ts_ref), load(tc_hbm, tc_ref)]
    ker_here = load_groups(ker_hbm, kv)
    x_here = [load(min_hbm, min_ref)] + load_groups(x_hbm, xv)
    rest_here = load_groups(cot_hbm, cotv)
    rest_here += [load(gain_hbm, gain_ref), load(up_hbm, up_ref), load(down_hbm, down_ref), load(mout_hbm, mout_ref)]

    me = lax.axis_index("seq")
    z, y = lax.div(me, SIDE), lax.rem(me, SIDE)
    i = lax.axis_index("dp")
    chip, core = lax.div(i, 2), lax.rem(i, 2)
    mate = i + 1 - 2 * core
    yo = wrapped(i - y)
    tz_at = [wrapped(z + step) for step in range(SIDE)]
    ty_at = [wrapped(y + step) for step in range(SIDE)]

    barrier = pltpu.get_barrier_semaphore()

    def greet_seq(step):
        pl.semaphore_signal(
            barrier, inc=1, device_id=(i, lax.rem(me + step, 64)), device_id_type=MESH
        )

    def greet_dp(step):
        pl.semaphore_signal(barrier, inc=1, device_id=(wrapped(i + step), me), device_id_type=MESH)

    repeat(64, greet_seq, 1)
    repeat(8, greet_dp, 1)

    def send(src, dst, ssem, rsem, device):
        pltpu.make_async_remote_copy(
            src_ref=src, dst_ref=dst, send_sem=ssem, recv_sem=rsem, device_id=device, device_id_type=MESH
        ).start()

    def send_part(part, src, dst, ssem, rsem):
        offsets = ((3, 5, 1, 7), (2, 6, 4, 0))[part]

        def one(dz, ty):
            tz = tz_at[dz]
            send(src(tz, ty), dst, ssem.at[dz], rsem, (i, tz * SIDE + ty))

        def pair(t):
            for dy in (3 - t, 5 + t):
                ty = wrapped(y + dy)
                for dz in offsets:
                    one(dz, ty)

        repeat(3, pair)
        for dy in (4, 0):
            for dz in offsets:
                if (dz, dy) != (0, 0):
                    one(dz, ty_at[dy])
        if part == 1:
            pltpu.make_async_copy(src(z, y), dst, rsem).start()

    def await_sent(buffer, ssem):
        await_bytes(buffer.at[0, pl.ds(0, 7)], ssem.at[0])
        for dz in range(1, SIDE):
            await_bytes(buffer.at[0], ssem.at[dz])

    def store_half(ref, h, pair, value):
        for side in range(2):
            split = value[:, 128 * side : 128 * side + 128].reshape(SIDE, 2, PIECE, 128)
            ref[h, :, 2 * pair + side] = split[:, 0]
            ref[h, :, 4 + 2 * pair + side] = split[:, 1]

    def load_half(ref, h, pair):
        groups = (2 * pair, 2 * pair + 1)
        return jnp.concatenate(
            [jnp.stack([ref[h, :, g], ref[h, :, 4 + g]], axis=1).reshape(256, 128) for g in groups], axis=1
        )

    def half_lanes(ref, h, pair):
        return jnp.concatenate([ref[2 * pair + side, :, 128 * h : 128 * h + 128] for side in range(2)], axis=1)

    def slot(chip_at, core_at):
        return wrapped(2 * chip_at + core_at - y)

    def to_chips(buffer, ssem, rsem):
        send(buffer.at[yo], buffer.at[yo], ssem.at[0], rsem.at[0], (mate, me))

        def step_to(step):
            send(
                buffer.at[yo], buffer.at[yo], ssem.at[step], rsem.at[step],
                (2 * lax.rem(chip + step, 4) + core, me),
            )

        repeat(4, step_to, 1)

    def to_mate(buffer, rsem, ssem2, rsem2):
        def step_to(step):
            held = buffer.at[slot(lax.rem(chip + 4 - step, 4), core)]
            await_bytes(held, rsem.at[step])
            send(held, held, ssem2.at[step], rsem2.at[step], (mate, me))

        repeat(4, step_to, 1)

    def from_mate(buffer, rsem, rsem2):
        await_bytes(buffer.at[slot(chip, 1 - core)], rsem.at[0])

        def step_from(step):
            await_bytes(buffer.at[slot(lax.rem(chip + 4 - step, 4), 1 - core)], rsem2.at[step])

        repeat(4, step_from, 1)

    r, l = iotas((256, 256))
    eye[...] = ones_where(r == l)
    twp[...] = jnp.zeros_like(twp)
    for copy in tw_here:
        copy.wait()
    for k in range(6):
        for which in range(2):
            twp[which, pl.ds(DG + k, 1)] = ts_ref[k, which : which + 1].astype(F32)
            twp[which, pl.ds(DG + 8 + k, 1)] = tc_ref[k, which : which + 1].astype(F32)
    for copy in ker_here:
        copy.wait()
    for g in range(GROUPS):
        kv[g, pl.ds(DG, PIECE)] = twp[1, pl.ds(DG, PIECE)].astype(BF)
        split = dot_nt(eye[...], kv[g]).astype(BF).reshape(SIDE, 2, PIECE, 256)
        ks[:, g] = split[:, 0]
        ks[:, 4 + g] = split[:, 1]
    columns = dot_nt(eye[...], twp[0].astype(BF))[:, 128:256]
    for copy in x_here:
        copy.wait()
    for g in range(GROUPS):
        xv[g, pl.ds(DG, PIECE)] = jnp.zeros((PIECE, 256), BF)

    def premix(h):
        for pair in range(2):
            rows = jnp.concatenate([xv[2 * pair + side, 128 * h : 128 * h + 128] for side in range(2)], axis=0)
            value = dot_nt(min_ref[...], rows)
            if h == 1:
                value = value + jnp.concatenate([columns, columns], axis=1)
            store_half(src1, h, pair, value.astype(BF))

    premix(1)
    pl.semaphore_wait(barrier, 70)

    def share_kernel(dz):
        tz = wrapped(z + dz)
        send(ks.at[tz, yo], kt.at[y, z], ks_s.at[1], ks_v, (i, tz * SIDE + yo))

    repeat(SIDE, share_kernel, 1)

    @pl.when(yo != y)
    def _():
        send(ks.at[z, yo], kt.at[y, z], ks_s.at[0], ks_v, (i, z * SIDE + yo))

    @pl.when(yo == y)
    def _():
        pltpu.make_async_copy(ks.at[z, yo], kt.at[y, z], ks_v).start()

    def half_of(h, src, dst, ssem, rsem, at, group):
        return (lambda tz, ty: src.at[h, tz, ty], dst.at[(h,) + at], ssem.at[h], rsem.at[h, group])

    for h in (1, 0):
        first = half_of(h, src1, a1, s1, v1, (z, y), z)
        if h == 0:
            premix(0)
        send_part(0, *first)
        if h == 1:
            await_bytes(kt.at[yo], ks_v)
            to_chips(kt, ka_s, ka_v)
        send_part(1, *first)

    for copy in rest_here:
        copy.wait()
    for g in range(GROUPS):
        xg[g] = dot_nt(eye[...], xv[g]).astype(BF)
        cotv[g, pl.ds(DG, PIECE)] = jnp.zeros((PIECE, 256), BF)
    mint[...] = dot_nt(eye[...], min_ref[...]).astype(BF)
    moutt[...] = dot_nt(eye[...], mout_ref[...]).astype(BF)
    row, lane = iotas((256, 256))
    chosen = ones_where((lane == 4 * (row & 63) + (row >> 6)) & ((row & 63) < 60))
    placed = ones_where((row == 60 * (lane >> 6) + (lane & 63)) & ((lane & 63) < 60))
    chosen_rows = [dot(chosen, cotv[part]).astype(BF) for part in range(GROUPS)]
    gain_rows = jnp.broadcast_to(gain_ref[...].astype(F32).reshape(1, D), (PIECE, D)).astype(BF)
    for g in range(GROUPS):
        cotn[g] = dot_nt(eye[...], cotv[g]).astype(BF)
        lined = jnp.concatenate([chosen_rows[part][64 * g : 64 * g + 64] for part in range(GROUPS)], axis=0)
        cotg[g] = dot_nt(eye[...], dot(placed, lined).astype(BF)).astype(BF)
        low, high = GAIN_WINDOWS[g]
        channel, lane = iotas((high - low, 256))
        gaing[g] = dot(gain_rows[:, low:high], ones_where((channel + low == g * DG + lane) & (lane < DG)))[0:8]
    to_mate(kt, ka_v, kb_s, kb_v)
    for g in range(GROUPS):
        low, high = HIDDEN_WINDOWS[g]
        column, hidden_unit = iotas((high - low, 512))
        chosen = (column + low == g * FFG + hidden_unit - 2 * (hidden_unit >> 5)) & ((hidden_unit & 31) < 30)
        chooser = ones_where(chosen)
        upp[g, 0:DG] = dot(up_ref[:, low:high], chooser).astype(BF)
        dnp[g, 0:DG] = dot(down_ref[:, low:high], chooser).astype(BF)
        upp[g, DG:256] = jnp.zeros((256 - DG, 512), BF)
        dnp[g, DG:256] = jnp.zeros((256 - DG, 512), BF)

    def spread_twiddles(which, p, q, slab):
        wide = slab.astype(F32)
        for k in range(6):
            twb[which, p, q, k] = jnp.broadcast_to(wide[:, 112 + k : 113 + k], (PIECE, 128))
            twb[which, p, q, 6 + k] = jnp.broadcast_to(wide[:, 120 + k : 121 + k], (PIECE, 128))

    def mixed(values, which, shards, bits, transposed):
        def selfs(a, k):
            return twb[which, shards[a][0], shards[a][1], k]

        def crosses(a, k):
            return twb[which, shards[a][0], shards[a][1], 6 + k]

        return mix(values, selfs, crosses, bits, transposed)

    low_bits = ((0, 0), (1, 1), (2, 2))
    high_bits = ((3, 0), (4, 1), (5, 2))
    low_back = tuple(reversed(low_bits))
    high_back = tuple(reversed(high_bits))

    def row_of(sz):
        return [(sz, a) for a in range(SIDE)]

    def column_of(sy):
        return [(a, sy) for a in range(SIDE)]

    def two_at_once(lines, read, which, bits, transposed, write):
        def step(t):
            groups = [lines(2 * t), lines(2 * t + 1)]
            held = [[read(p, q) for p, q in shards] for shards in groups]
            held = [mixed(values, which, shards, bits, transposed) for values, shards in zip(held, groups)]
            for shards, values in zip(groups, held):
                for (p, q), value in zip(shards, values):
                    write(p, q, value)

        repeat(SIDE // 2, step)

    def store_wide(p, q, value):
        ff[p, q] = value

    def load_wide(p, q):
        return ff[p, q]

    from_mate(kt, ka_v, kb_v)

    def spread_output_twiddles(sz):
        for p, q in row_of(sz):
            spread_twiddles(1, p, q, kt[q, p, :, 128:256])

    repeat(SIDE, spread_output_twiddles)

    for h in (1, 0):
        lanes = slice(128 * h, 128 * h + 128)

        def forward_one(step, h=h):
            sz = wrapped(z + step)
            await_bytes(a1.at[h, sz], v1.at[h, sz])
            shards = row_of(sz)
            if h == 1:
                for p, q in shards:
                    spread_twiddles(0, p, q, a1[1, p, q])
            values = mixed([a1[h, p, q].astype(F32) for p, q in shards], 0, shards, low_bits, False)
            for (p, q), value in zip(shards, values):
                ff[p, q] = value

        repeat(SIDE, forward_one)

        def weigh(p, q, value, h=h, lanes=lanes):
            rounded = value.astype(BF)
            sp[h, p, q] = rounded
            ff[p, q] = rounded.astype(F32) * kt[q, p, :, lanes].astype(F32)

        def leave(p, q, value, h=h):
            src2[h, p, q] = value.astype(BF)

        two_at_once(column_of, load_wide, 0, high_bits, False, weigh)
        two_at_once(row_of, load_wide, 1, low_bits, False, store_wide)
        two_at_once(column_of, load_wide, 1, high_bits, False, leave)
        for part in range(2):
            send_part(part, *half_of(h, src2, m2, s2, v2, (z, y), z))

    for g in range(GROUPS):
        acot[g] = dot(cotg[g], dnp[g])
        channel, j = iotas((D, 256))
        spread = ones_where((channel == 4 * j + g) & (j < DG))
        ww[:, pl.ds(g * 512, 512)] = dot(spread, dnp[g]).astype(BF)

    lane_here = (lax.broadcasted_iota(jnp.int32, (256, 256), 1) & 127) < DG - 128
    squares = jnp.zeros((256, 1), F32)
    for h in (1, 0):
        for sz in range(SIDE):
            await_bytes(m2.at[h, sz], v2.at[h, sz])
        for pair in range(2):
            value = half_lanes(xg, h, pair).astype(F32) + dot(mout_ref[...], load_half(m2, h, pair))
            if h == 1:
                value = jnp.where(lane_here, value, 0.0)
            value = value.astype(BF)
            for side in range(2):
                hg[2 * pair + side, :, 128 * h : 128 * h + 128] = value[:, 128 * side : 128 * side + 128]
            wide = value.astype(F32)
            squares = squares + jnp.sum(wide * wide, axis=1, keepdims=True)
    scale_column = lax.rsqrt(squares * (1.0 / D) + 1e-06)
    rowscale[...] = jnp.broadcast_to(scale_column, (256, 128))

    for g in range(GROUPS):
        wide = hg[g].astype(F32)
        ng[g] = (wide * rowscale[:, 0:1] * gaing[g, 0:1]).astype(BF)
        pa[...] = dot(ng[g], upp[g])

        def activate(tile, g=g):
            rows = pl.ds(pl.multiple_of(tile * 64, 64), 64)
            p = pa[rows]
            square = p * p
            tangent = jnp.tanh(p * (ROOT_HALF + (ROOT_HALF * CUBIC) * square))
            half_more = 0.5 + 0.5 * tangent
            act[rows, pl.ds(g * 512, 512)] = (p * half_more).astype(BF)
            inner = ROOT_HALF + (3.0 * ROOT_HALF * CUBIC) * square
            slope = half_more + 0.5 * p * (1.0 - tangent * tangent) * inner
            pgr[g, rows] = (acot[g, rows] * slope).astype(BF)

        repeat(4, activate)
        ngr[g] = dot_nt(pgr[g], upp[g])

    means = jnp.zeros((256, 1), F32)
    for g in range(GROUPS):
        means = means + jnp.sum(ngr[g] * gaing[g, 0:1] * hg[g].astype(F32), axis=1, keepdims=True)
    scale_column = rowscale[:, 0:1]
    means = means * (1.0 / D) * scale_column * scale_column * scale_column
    for h in (1, 0):
        lanes = slice(128 * h, 128 * h + 128)
        for pair in range(2):
            for g in (2 * pair, 2 * pair + 1):
                gained = ngr[g, :, lanes] * gaing[g, 0:1, lanes]
                wide = hg[g, :, lanes].astype(F32)
                hgr[g, :, lanes] = (cotn[g, :, lanes].astype(F32) + scale_column * gained - wide * means).astype(BF)
            store_half(src3, h, pair, dot(moutt[...], half_lanes(hgr, h, pair)).astype(BF))
        for part in range(2):
            send_part(part, *half_of(h, src3, a3, s3, v3, (y, z), y))

    row_here = (lax.broadcasted_iota(jnp.int32, (512, 256), 0) & 31) == 30
    for g in range(GROUPS):
        gain_term = jnp.sum(ngr[g] * hg[g].astype(F32) * rowscale[:, 0:1], axis=0, keepdims=True)
        up_term = jnp.where(row_here, gain_term, dot_tn(pgr[g], ng[g]))
        down_term = dot_tn(act[:, pl.ds(g * 512, 512)], cotg[g])
        for kind, term in ((0, up_term), (1, down_term)):
            split = term.astype(BF).reshape(16, 2, PIECE, 256)
            for half in range(2):
                for side in range(2):
                    gg[side, 2 * kind + half, pl.ds(g * 16, 16)] = split[:, half, :, side * 128 : side * 128 + 128]

    send(gg.at[1 - core], r1a, ga_s, ga_v, (mate, me))

    await_bytes(r1a, ga_v)

    def pair_sum(step):
        for slab in range(4):
            part = pl.ds(pl.multiple_of(step * 8, 8), 8)
            both = gg[core, slab, part].astype(F32) + r1a[slab, part].astype(F32)
            h1[slab, part] = both.astype(BF)

    repeat(8, pair_sum)

    def spread_terms(step):
        other = lax.rem(chip + step, 4)
        send(h1.at[other], r1b.at[chip], gb_s.at[step], gb_v.at[step], (other * 2 + core, me))

    repeat(4, spread_terms, 1)

    others = [lax.rem(chip + step, 4) for step in (1, 2, 3)]

    for h in (1, 0):
        lanes = slice(128 * h, 128 * h + 128)

        def backward_one(step, h=h):
            sy = wrapped(y + step)
            await_bytes(a3.at[h, sy], v3.at[h, sy])
            shards = column_of(sy)
            values = mixed([a3[h, q, p].astype(F32) for p, q in shards], 1, shards, high_back, True)
            for (p, q), value in zip(shards, values):
                ff[p, q] = value

        repeat(SIDE, backward_one)

        def weigh_back(p, q, value, h=h, lanes=lanes):
            wide = value.astype(BF).astype(F32)
            owner = wrapped(q + y)
            kgb[lax.rem(owner, 2), lax.div(owner, 2), p, :, lanes] = (sp[h, p, q].astype(F32) * wide).astype(BF)
            ff[p, q] = wide * kt[q, p, :, lanes].astype(F32)

        def leave_back(p, q, value, h=h):
            src4[h, p, q] = value.astype(BF)

        two_at_once(row_of, load_wide, 1, low_back, True, weigh_back)
        if h == 0:
            send(kgb.at[1 - core], kra, kr_s, kr_v, (mate, me))
        two_at_once(column_of, load_wide, 0, high_back, True, store_wide)
        two_at_once(row_of, load_wide, 0, low_back, True, leave_back)
        last = half_of(h, src4, m4, s4, v4, (z, y), z)
        send_part(0, *last)
        if h == 1:
            send_part(1, *last)

    await_bytes(kra, kr_v)

    def kernel_pair(sz):
        for at in range(4):
            kgh[at, sz] = (kgb[core, at, sz].astype(F32) + kra[at, sz].astype(F32)).astype(BF)

    repeat(SIDE, kernel_pair)

    def spread_kernel_terms(step):
        other = lax.rem(chip + step, 4)
        send(kgh.at[other], krb.at[chip], kc_s.at[step], kc_v.at[step], (other * 2 + core, me))

    repeat(4, spread_kernel_terms, 1)

    def kernel_terms_here(step):
        await_bytes(krb.at[lax.rem(chip + 4 - step, 4)], kc_v.at[step])

    repeat(4, kernel_terms_here, 1)

    def kernel_sum(sz):
        four = kgh[chip, sz].astype(F32)
        for other in others:
            four = four + krb[other, sz].astype(F32)
        kgs[sz] = four.astype(BF)

    repeat(SIDE, kernel_sum)

    def return_kernel(dz):
        tz = wrapped(z + dz)
        send(kgs.at[tz], kgf.at[y, z], kf_s.at[1], kf_v, (i, tz * SIDE + yo))

    repeat(SIDE, return_kernel, 1)

    @pl.when(yo != y)
    def _():
        send(kgs.at[z], kgf.at[y, z], kf_s.at[0], kf_v, (i, z * SIDE + yo))

    @pl.when(yo == y)
    def _():
        pltpu.make_async_copy(kgs.at[z], kgf.at[y, z], kf_v).start()

    send_part(1, *last)

    def terms_here(step):
        await_bytes(r1b.at[lax.rem(chip + 4 - step, 4)], gb_v.at[step])

    repeat(4, terms_here, 1)

    def chip_sum(t):
        for odd in range(2):
            sz = 2 * t + odd
            part = pl.ds(pl.multiple_of(sz * 8, 8), 8)
            four = h1[chip, part].astype(F32)
            for other in others:
                four = four + r1b[other, part].astype(F32)
            four = four.astype(BF)
            for q in range(SIDE):
                if (odd + q) % 2 == 0:
                    pa1[q, t] = four[q]
                else:
                    pb1[sz, q // 2] = four[q]

    repeat(SIDE // 2, chip_sum)

    def along_y(step):
        ty = wrapped(y + step)
        send(pa1.at[ty], pa2.at[y], pa_s.at[step], pa_v.at[step], (i, z * SIDE + ty))

    def along_z(step):
        tz = wrapped(z + step)
        send(pb1.at[tz], pb2.at[z], pb_s.at[step], pb_v.at[step], (i, tz * SIDE + y))

    def first_step(step):
        along_y(step)
        along_z(step)

    repeat(SIDE, first_step, 1)

    acc[...] = dot_nt(ww[...], act[...])
    for g in range(GROUPS):
        rows = pl.ds(g * DG, DG)
        outv[rows] = (acc[rows] + dot_nt(eye[0:DG], hg[g])).astype(BF)
    pltpu.make_async_copy(outv, out_hbm, out_s.at[0]).start()

    def first_here(step):
        await_bytes(pa2.at[wrapped(y - step)], pa_v.at[step])
        await_bytes(pb2.at[wrapped(z - step)], pb_v.at[step])

    repeat(SIDE, first_here, 1)
    sum_y, sum_z = pa1[y].astype(F32), pb1[z].astype(F32)
    for step in range(1, SIDE):
        sum_y = sum_y + pa2[wrapped(y + step)].astype(F32)
        sum_z = sum_z + pb2[wrapped(z + step)].astype(F32)
    pa3[...] = sum_y.astype(BF)
    pb3[...] = sum_z.astype(BF)
    odd = lax.rem(z + y, 2)

    def second_z(m):
        return 2 * m + lax.rem(y, 2)

    def second_y(m):
        return 2 * m + 1 - lax.rem(z, 2)

    for m in range(4):

        @pl.when(second_z(m) != z)
        def _(m=m):
            send(pa3.at[m], pc.at[z], pc_s.at[m], pc_v.at[z], (i, second_z(m) * SIDE + y))

        @pl.when(second_y(m) != y)
        def _(m=m):
            send(pb3.at[m], pc.at[y], pd_s.at[m], pc_v.at[y], (i, z * SIDE + second_y(m)))

    @pl.when(odd == 0)
    def _():
        pc[z] = pa3[lax.div(z, 2)]

    @pl.when(odd == 1)
    def _():
        pc[y] = pb3[lax.div(y, 2)]

    await_bytes(kgf.at[yo], kf_v)
    to_chips(kgf, kh_s, kh_v)

    own = z + odd * (y - z)

    def second_here(step):
        at = wrapped(own + step)
        await_bytes(pc.at[at], pc_v.at[at])

    repeat(SIDE, second_here, 1)
    shard_sum = pc[0].astype(F32)
    for at in range(1, SIDE):
        shard_sum = shard_sum + pc[at].astype(F32)
    shard_sum = shard_sum * SCALE
    fin[...] = shard_sum
    rf[i] = shard_sum

    def spread_grads(step):
        send(fin, rf.at[i], gf_s.at[step], gf_v.at[step], (wrapped(i + step), me))

    repeat(SIDE, spread_grads, 1)
    to_mate(kgf, kh_v, ki_s, ki_v)

    for h in (1, 0):
        lanes = slice(128 * h, 128 * h + 128)
        for sz in range(SIDE):
            await_bytes(m4.at[h, sz], v4.at[h, sz])
        for pair in range(2):
            value = half_lanes(hgr, h, pair).astype(F32) + dot(mint[...], load_half(m4, h, pair))
            value = dot_nt(eye[...], value.astype(BF)).astype(BF)
            for side in range(2):
                start = (2 * pair + side) * DG + 128 * h
                rows = DG - 128 if h == 1 else 128
                igv[pl.ds(start, rows)] = value[128 * side : 128 * side + rows]
    pltpu.make_async_copy(igv, ig_hbm, out_s.at[2]).start()

    from_mate(kgf, kh_v, ki_v)
    for g in range(GROUPS):
        held = jnp.stack([kgf[g], kgf[4 + g]], axis=1).reshape(256, 256)
        kgv[pl.ds(g * DG, DG)] = dot_nt(eye[0:DG], held).astype(BF)
    pltpu.make_async_copy(kgv, kg_hbm, out_s.at[1]).start()

    def grads_here(step):
        await_bytes(rf.at[wrapped(i - step)], gf_v.at[step])

    repeat(SIDE, grads_here, 1)
    for share in range(SIDE):
        kind, half, side = share // 4, (share // 2) % 2, share % 2
        wsum[kind, pl.ds(half * PIECE, PIECE), pl.ds(side * 128, 128)] = rf[share]
    ugv[...] = wsum[0, 0:30, 0:DG]
    dgv[...] = wsum[1, 0:30, 0:DG]
    j, lane = iotas((256, 128))
    picker = jnp.where(j == lane + 15 * lax.rem(me, 16), 1.0, 0.0)
    gains = jnp.broadcast_to(wsum[0, 30:31], (8, 256))
    picked = lax.dot_general(
        gains, picker, (((1,), (0,)), ((), ())), precision=lax.Precision.HIGHEST, preferred_element_type=F32
    )
    gnv[...] = picked[0:1, 0:15]
    pltpu.make_async_copy(ugv, ug_hbm, out_s.at[3]).start()
    pltpu.make_async_copy(dgv, dg_hbm, out_s.at[4]).start()
    pltpu.make_async_copy(gnv, gn_hbm, out_s.at[5]).start()

    for buffer, sem in ((src1, s1), (src2, s2), (src3, s3), (src4, s4)):
        for h in range(2):
            await_sent(buffer.at[h], sem.at[h])
    for m in range(4):

        @pl.when(second_z(m) != z)
        def _(m=m):
            await_bytes(pa3.at[m], pc_s.at[m])

        @pl.when(second_y(m) != y)
        def _(m=m):
            await_bytes(pb3.at[m], pd_s.at[m])

    await_bytes(ks.at[0, pl.ds(0, 7)], ks_s.at[1])
    await_bytes(kgs.at[pl.ds(0, 7)], kf_s.at[1])

    @pl.when(yo != y)
    def _():
        await_bytes(ks.at[0, 0], ks_s.at[0])
        await_bytes(kgs.at[0], kf_s.at[0])

    await_bytes(kt.at[0], ka_s.at[0])
    await_bytes(kgf.at[0], kh_s.at[0])
    await_bytes(r1a, ga_s)
    await_bytes(kra, kr_s)

    def chips_left(step):
        await_bytes(kt.at[0], ka_s.at[step])
        await_bytes(kt.at[0], kb_s.at[step])
        await_bytes(kgf.at[0], kh_s.at[step])
        await_bytes(kgf.at[0], ki_s.at[step])
        await_bytes(kgh.at[0], kc_s.at[step])
        await_bytes(h1.at[0], gb_s.at[step])

    repeat(4, chips_left, 1)

    def grads_left(step):
        await_bytes(fin, gf_s.at[step])
        await_bytes(pa1.at[0], pa_s.at[step])
        await_bytes(pb1.at[0], pb_s.at[step])

    repeat(SIDE, grads_left, 1)
    outs = ((outv, out_hbm), (kgv, kg_hbm), (igv, ig_hbm), (ugv, ug_hbm), (dgv, dg_hbm), (gnv, gn_hbm))
    for index, (held, there) in enumerate(outs):
        pltpu.make_async_copy(held, there, out_s.at[index]).wait()


def settle(*refs):
    source, there, held, sems = refs[:6], refs[6:12], refs[12:18], refs[18]
    loads = [pltpu.make_async_copy(source[index], held[index], sems.at[0, index]) for index in range(6)]
    stores = [pltpu.make_async_copy(held[index], there[index], sems.at[1, index]) for index in range(6)]
    for copy in loads:
        copy.start()
    for load, store in zip(loads, stores):
        load.wait()
        store.start()
    for copy in stores:
        copy.wait()


def local(
    inputs, cotangent, kernel_values, mix_in, mix_out, twiddle_self, twiddle_cross, norm_gain, up_weight, down_weight
):
    hbm = pl.BlockSpec(memory_space=pltpu.HBM)
    dma = pltpu.SemaphoreType.DMA
    vmem = pltpu.VMEM
    exchange = vmem((SIDE, SIDE, PIECE, 256), BF)
    halves = vmem((2, SIDE, SIDE, PIECE, 128), BF)
    part = vmem((SIDE, 4, PIECE, 128), BF)
    both = dma((2, SIDE))
    grouped = vmem((GROUPS, 256, 256), BF)
    square = vmem((256, 256), BF)
    quarter = vmem((4, SIDE, PIECE, 256), BF)
    terms = vmem((4, 64, PIECE, 128), BF)
    wide = (D, 256)
    scratch = dict(
        xv=grouped, kv=grouped, cotv=grouped, min_ref=square, mout_ref=square,
        ts_ref=vmem((6, 2, 256), BF), tc_ref=vmem((6, 2, 256), BF), gain_ref=vmem((D,), BF),
        up_ref=vmem((DG, 1920), BF), down_ref=vmem((DG, 1920), BF),
        outv=vmem(wide, BF), igv=vmem(wide, BF), kgv=vmem(wide, BF),
        ugv=vmem((30, DG), F32), dgv=vmem((30, DG), F32), gnv=vmem((1, 15), F32),
        eye=square, mint=square, moutt=square, twp=vmem((2, 256, 256), F32),
        xg=grouped, cotg=grouped, cotn=grouped,
        upp=vmem((GROUPS, 256, 512), BF), dnp=vmem((GROUPS, 256, 512), BF), ww=vmem((D, 2048), BF),
        acot=vmem((GROUPS, 256, 512), F32), pa=vmem((256, 512), F32), act=vmem((256, 2048), BF),
        pgr=vmem((GROUPS, 256, 512), BF), hg=grouped, ng=grouped, ngr=vmem((GROUPS, 256, 256), F32),
        hgr=grouped, acc=vmem(wide, F32), gaing=vmem((GROUPS, 8, 256), F32), rowscale=vmem((256, 128), F32),
        wsum=vmem((2, 32, 256), F32),
        src1=halves, a1=halves, ks=exchange, kt=exchange, ff=vmem((SIDE, SIDE, PIECE, 128), F32), sp=halves,
        src2=halves, m2=halves, src3=halves, a3=halves, src4=halves, m4=halves,
        pa1=part, pa2=part, pa3=vmem((4, PIECE, 128), BF), pb1=part, pb2=part, pb3=vmem((4, PIECE, 128), BF),
        pc=vmem((SIDE, PIECE, 128), BF),
        twb=vmem((2, SIDE, SIDE, 12, PIECE, 128), F32),
        kgb=vmem((2, 4, SIDE, PIECE, 256), BF), kra=quarter, kgh=quarter, krb=quarter,
        kgs=vmem((SIDE, PIECE, 256), BF), kgf=exchange,
        gg=vmem((2, 4, 64, PIECE, 128), BF), r1a=terms, h1=terms, r1b=terms,
        fin=vmem((PIECE, 128), F32), rf=vmem((SIDE, PIECE, 128), F32),
        in_s=dma((19,)), out_s=dma((6,)),
        s1=both, v1=both, s2=both, v2=both, s3=both, v3=both, s4=both, v4=both,
        pa_s=dma((SIDE,)), pa_v=dma((SIDE,)), pb_s=dma((SIDE,)), pb_v=dma((SIDE,)),
        pc_s=dma((4,)), pc_v=dma((SIDE,)), pd_s=dma((4,)),
        ks_s=dma((2,)), ks_v=dma, ka_s=dma((4,)), ka_v=dma((4,)), kb_s=dma((4,)), kb_v=dma((4,)),
        kr_s=dma, kr_v=dma, kc_s=dma((4,)), kc_v=dma((4,)), kf_s=dma((2,)), kf_v=dma,
        kh_s=dma((4,)), kh_v=dma((4,)), ki_s=dma((4,)), ki_v=dma((4,)),
        ga_s=dma, ga_v=dma, gb_s=dma((4,)), gb_v=dma((4,)), gf_s=dma((SIDE,)), gf_v=dma((SIDE,)),
    )
    shape = jax.ShapeDtypeStruct
    results = [shape(wide, BF)] * 3 + [shape((30, DG), F32)] * 2 + [shape((1, 15), F32)]
    held = pl.pallas_call(
        kernel,
        out_shape=results,
        in_specs=[hbm] * 10,
        out_specs=[hbm] * 6,
        scratch_shapes=scratch,
        compiler_params=pltpu.CompilerParams(
            collective_id=0, has_side_effects=True, vmem_limit_bytes=58 * 1024 * 1024
        ),
        cost_estimate=pl.CostEstimate(flops=4_000_000_000, bytes_accessed=6_000_000, transcendentals=600_000),
    )(
        inputs[0].T, cotangent[0].T, kernel_values.T, mix_in, mix_out,
        twiddle_self.transpose(1, 0, 2), twiddle_cross.transpose(1, 0, 2),
        norm_gain, up_weight, down_weight,
    )
    output, input_grad, kernel_grad, up_grad, down_grad, gain_grad = pl.pallas_call(
        settle,
        out_shape=results,
        in_specs=[hbm] * 6,
        out_specs=[hbm] * 6,
        scratch_shapes=[vmem(result.shape, result.dtype) for result in results] + [dma((2, 6))],
        compiler_params=pltpu.CompilerParams(vmem_limit_bytes=58 * 1024 * 1024),
        cost_estimate=pl.CostEstimate(flops=0, bytes_accessed=3_000_000, transcendentals=0),
    )(*held)
    return output.T[None], input_grad.T[None], kernel_grad.T, up_grad.T, down_grad.T, gain_grad[0]


def solution(mesh):
    in_specs = (
        P("dp", "seq", None),
        P("dp", "seq", None),
        P("seq", None),
        P("seq", None),
        P("seq", None),
        P(None, None, "seq"),
        P(None, None, "seq"),
        P(),
        P(),
        P(),
    )
    out_specs = (
        P("dp", "seq", None),
        P("dp", "seq", None),
        P("seq", None),
        P(None, "seq"),
        P(None, "seq"),
        P("seq"),
    )
    return jax.shard_map(local, mesh=mesh, in_specs=in_specs, out_specs=out_specs, check_vma=False)
```

```python
import jax
import jax.numpy as jnp
from jax import lax
from jax.experimental import pallas as pl
from jax.experimental.pallas import tpu as pltpu
from jax.sharding import PartitionSpec as P

MESH = pl.DeviceIdType.MESH
BF = jnp.bfloat16
F32 = jnp.float32

D = 960
GROUPS = 4
DG = 240
FFG = 480
SIDE = 8
PIECE = 16
ROOT_HALF = 0.7978845608028654
CUBIC = 0.044715
SCALE = 131072.0**-0.5
GAIN_WINDOWS = ((0, 256), (128, 512), (384, 768), (640, 960))
HIDDEN_WINDOWS = ((0, 512), (384, 1024), (896, 1536), (1408, 1920))


def dot(a, b):
    return lax.dot_general(a, b, (((1,), (0,)), ((), ())), preferred_element_type=F32)


def dot_tn(a, b):
    return lax.dot_general(a, b, (((0,), (0,)), ((), ())), preferred_element_type=F32)


def dot_nt(a, b):
    return lax.dot_general(a, b, (((1,), (1,)), ((), ())), preferred_element_type=F32)


def iotas(shape):
    return lax.broadcasted_iota(jnp.int32, shape, 0), lax.broadcasted_iota(jnp.int32, shape, 1)


def ones_where(mask):
    return jnp.where(mask, 1.0, 0.0).astype(BF)


def repeat(count, body, start=0):
    def step(index, carry):
        body(index)
        return carry

    lax.fori_loop(start, count, step, 0)


def wrapped(value):
    return lax.rem(value + 2 * SIDE, SIDE)


def await_bytes(view, sem):
    pltpu.make_async_copy(view, view, sem).wait()


def mix(values, selfs, crosses, bits, transposed):
    for k, bit in bits:
        stride = 1 << bit
        if transposed:
            scaled = [crosses(a, k) * values[a] for a in range(SIDE)]
            values = [selfs(a, k) * values[a] + scaled[a ^ stride] for a in range(SIDE)]
        else:
            values = [selfs(a, k) * values[a] + crosses(a, k) * values[a ^ stride] for a in range(SIDE)]
    return values


def kernel(
    x_hbm, cot_hbm, ker_hbm, min_hbm, mout_hbm, ts_hbm, tc_hbm, gain_hbm, up_hbm, down_hbm,
    out_hbm, ig_hbm, kg_hbm, ug_hbm, dg_hbm, gn_hbm,
    xv, kv, cotv, min_ref, mout_ref, ts_ref, tc_ref, gain_ref, up_ref, down_ref,
    outv, igv, kgv, ugv, dgv, gnv,
    eye, mint, moutt, twp, xg, cotg, cotn, upp, dnp, ww, acot, pa, act, pgr, hg, ng, ngr, hgr, acc, gaing, rowscale, wsum,
    src1, a1, ks, kt, ff, sp, src2, m2, src3, a3, src4, m4, twb, pa1, pa2, pa3, pb1, pb2, pb3, pc,
    kgb, kra, kgh, krb, kgs, kgf, gg, r1a, h1, r1b, fin, rf,
    in_s, out_s, s1, v1, s2, v2, s3, v3, s4, v4, pa_s, pa_v, pb_s, pb_v, pc_s, pc_v, pd_s,
    ks_s, ks_v, ka_s, ka_v, kb_s, kb_v, kr_s, kr_v, kc_s, kc_v, kf_s, kf_v, kh_s, kh_v, ki_s, ki_v,
    ga_s, ga_v, gb_s, gb_v, gf_s, gf_v,
):
    loads = []

    def load(src, dst):
        copy = pltpu.make_async_copy(src, dst, in_s.at[len(loads)])
        copy.start()
        loads.append(copy)
        return copy

    def load_groups(src, dst):
        return [load(src.at[pl.ds(g * DG, DG)], dst.at[g, pl.ds(0, DG)]) for g in range(GROUPS)]

    tw_here = [load(ts_hbm, ts_ref), load(tc_hbm, tc_ref)]
    ker_here = load_groups(ker_hbm, kv)
    x_here = [load(min_hbm, min_ref)] + load_groups(x_hbm, xv)
    rest_here = load_groups(cot_hbm, cotv)
    rest_here += [load(gain_hbm, gain_ref), load(up_hbm, up_ref), load(down_hbm, down_ref), load(mout_hbm, mout_ref)]

    me = lax.axis_index("seq")
    z, y = lax.div(me, SIDE), lax.rem(me, SIDE)
    i = lax.axis_index("dp")
    chip, core = lax.div(i, 2), lax.rem(i, 2)
    mate = i + 1 - 2 * core
    yo = wrapped(i - y)

    barrier = pltpu.get_barrier_semaphore()

    def greet_seq(step):
        pl.semaphore_signal(
            barrier, inc=1, device_id={"seq": lax.rem(me + step, 64)}, device_id_type=MESH
        )

    def greet_dp(step):
        pl.semaphore_signal(barrier, inc=1, device_id={"dp": wrapped(i + step)}, device_id_type=MESH)

    repeat(64, greet_seq, 1)
    repeat(8, greet_dp, 1)

    def send(src, dst, ssem, rsem, device):
        pltpu.make_async_remote_copy(
            src_ref=src, dst_ref=dst, send_sem=ssem, recv_sem=rsem, device_id=device, device_id_type=MESH
        ).start()

    def send_part(part, src, dst, ssem, rsem):
        offsets = ((3, 5, 1, 7), (2, 6, 4, 0))[part]

        def one(dz, dy):
            tz, ty = wrapped(z + dz), wrapped(y + dy)
            send(src(tz, ty), dst, ssem.at[dz], rsem, {"seq": tz * SIDE + ty})

        def pair(t):
            for dy in (3 - t, 5 + t):
                for dz in offsets:
                    one(dz, dy)

        repeat(3, pair)
        for dy in (4, 0):
            for dz in offsets:
                if (dz, dy) != (0, 0):
                    one(dz, dy)
        if part == 1:
            pltpu.make_async_copy(src(z, y), dst, rsem).start()

    def await_sent(buffer, ssem):
        await_bytes(buffer.at[0, pl.ds(0, 7)], ssem.at[0])
        for dz in range(1, SIDE):
            await_bytes(buffer.at[0], ssem.at[dz])

    def store_half(ref, h, pair, value):
        for side in range(2):
            split = value[:, 128 * side : 128 * side + 128].reshape(SIDE, 2, PIECE, 128)
            ref[h, :, 2 * pair + side] = split[:, 0]
            ref[h, :, 4 + 2 * pair + side] = split[:, 1]

    def load_half(ref, h, pair):
        groups = (2 * pair, 2 * pair + 1)
        return jnp.concatenate(
            [jnp.stack([ref[h, :, g], ref[h, :, 4 + g]], axis=1).reshape(256, 128) for g in groups], axis=1
        )

    def half_lanes(ref, h, pair):
        return jnp.concatenate([ref[2 * pair + side, :, 128 * h : 128 * h + 128] for side in range(2)], axis=1)

    def slot(chip_at, core_at):
        return wrapped(2 * chip_at + core_at - y)

    def to_chips(buffer, ssem, rsem):
        send(buffer.at[yo], buffer.at[yo], ssem.at[0], rsem.at[0], {"dp": mate})

        def step_to(step):
            send(
                buffer.at[yo], buffer.at[yo], ssem.at[step], rsem.at[step],
                {"dp": 2 * lax.rem(chip + step, 4) + core},
            )

        repeat(4, step_to, 1)

    def to_mate(buffer, rsem, ssem2, rsem2):
        def step_to(step):
            held = buffer.at[slot(lax.rem(chip + 4 - step, 4), core)]
            await_bytes(held, rsem.at[step])
            send(held, held, ssem2.at[step], rsem2.at[step], {"dp": mate})

        repeat(4, step_to, 1)

    def from_mate(buffer, rsem, rsem2):
        await_bytes(buffer.at[slot(chip, 1 - core)], rsem.at[0])

        def step_from(step):
            await_bytes(buffer.at[slot(lax.rem(chip + 4 - step, 4), 1 - core)], rsem2.at[step])

        repeat(4, step_from, 1)

    r, l = iotas((256, 256))
    eye[...] = ones_where(r == l)
    twp[...] = jnp.zeros_like(twp)
    for copy in tw_here:
        copy.wait()
    for k in range(6):
        for which in range(2):
            twp[which, pl.ds(DG + k, 1)] = ts_ref[k, which : which + 1].astype(F32)
            twp[which, pl.ds(DG + 8 + k, 1)] = tc_ref[k, which : which + 1].astype(F32)
    for copy in ker_here:
        copy.wait()
    for g in range(GROUPS):
        kv[g, pl.ds(DG, PIECE)] = twp[1, pl.ds(DG, PIECE)].astype(BF)
        split = dot_nt(eye[...], kv[g]).astype(BF).reshape(SIDE, 2, PIECE, 256)
        ks[:, g] = split[:, 0]
        ks[:, 4 + g] = split[:, 1]
    columns = dot_nt(eye[...], twp[0].astype(BF))[:, 128:256]
    for copy in x_here:
        copy.wait()
    for g in range(GROUPS):
        xv[g, pl.ds(DG, PIECE)] = jnp.zeros((PIECE, 256), BF)

    def premix(h):
        for pair in range(2):
            rows = jnp.concatenate([xv[2 * pair + side, 128 * h : 128 * h + 128] for side in range(2)], axis=0)
            value = dot_nt(min_ref[...], rows)
            if h == 1:
                value = value + jnp.concatenate([columns, columns], axis=1)
            store_half(src1, h, pair, value.astype(BF))

    premix(1)
    pl.semaphore_wait(barrier, 70)

    def share_kernel(dz):
        tz = wrapped(z + dz)
        send(ks.at[tz, yo], kt.at[y, z], ks_s.at[1], ks_v, {"seq": tz * SIDE + yo})

    repeat(SIDE, share_kernel, 1)

    @pl.when(yo != y)
    def _():
        send(ks.at[z, yo], kt.at[y, z], ks_s.at[0], ks_v, {"seq": z * SIDE + yo})

    @pl.when(yo == y)
    def _():
        pltpu.make_async_copy(ks.at[z, yo], kt.at[y, z], ks_v).start()

    def half_of(h, src, dst, ssem, rsem, at, group):
        return (lambda tz, ty: src.at[h, tz, ty], dst.at[(h,) + at], ssem.at[h], rsem.at[h, group])

    for h in (1, 0):
        first = half_of(h, src1, a1, s1, v1, (z, y), z)
        if h == 0:
            premix(0)
        send_part(0, *first)
        if h == 1:
            await_bytes(kt.at[yo], ks_v)
            to_chips(kt, ka_s, ka_v)
        send_part(1, *first)

    for copy in rest_here:
        copy.wait()
    for g in range(GROUPS):
        xg[g] = dot_nt(eye[...], xv[g]).astype(BF)
        cotv[g, pl.ds(DG, PIECE)] = jnp.zeros((PIECE, 256), BF)
    mint[...] = dot_nt(eye[...], min_ref[...]).astype(BF)
    moutt[...] = dot_nt(eye[...], mout_ref[...]).astype(BF)
    row, lane = iotas((256, 256))
    chosen = ones_where((lane == 4 * (row & 63) + (row >> 6)) & ((row & 63) < 60))
    placed = ones_where((row == 60 * (lane >> 6) + (lane & 63)) & ((lane & 63) < 60))
    chosen_rows = [dot(chosen, cotv[part]).astype(BF) for part in range(GROUPS)]
    gain_rows = jnp.broadcast_to(gain_ref[...].astype(F32).reshape(1, D), (PIECE, D)).astype(BF)
    for g in range(GROUPS):
        cotn[g] = dot_nt(eye[...], cotv[g]).astype(BF)
        lined = jnp.concatenate([chosen_rows[part][64 * g : 64 * g + 64] for part in range(GROUPS)], axis=0)
        cotg[g] = dot_nt(eye[...], dot(placed, lined).astype(BF)).astype(BF)
        low, high = GAIN_WINDOWS[g]
        channel, lane = iotas((high - low, 256))
        gaing[g] = dot(gain_rows[:, low:high], ones_where((channel + low == g * DG + lane) & (lane < DG)))[0:8]
    to_mate(kt, ka_v, kb_s, kb_v)
    for g in range(GROUPS):
        low, high = HIDDEN_WINDOWS[g]
        column, hidden_unit = iotas((high - low, 512))
        chosen = (column + low == g * FFG + hidden_unit - 2 * (hidden_unit >> 5)) & ((hidden_unit & 31) < 30)
        chooser = ones_where(chosen)
        upp[g, 0:DG] = dot(up_ref[:, low:high], chooser).astype(BF)
        dnp[g, 0:DG] = dot(down_ref[:, low:high], chooser).astype(BF)
        upp[g, DG:256] = jnp.zeros((256 - DG, 512), BF)
        dnp[g, DG:256] = jnp.zeros((256 - DG, 512), BF)

    def spread_twiddles(which, p, q, slab):
        wide = slab.astype(F32)
        for k in range(6):
            twb[which, p, q, k] = jnp.broadcast_to(wide[:, 112 + k : 113 + k], (PIECE, 128))
            twb[which, p, q, 6 + k] = jnp.broadcast_to(wide[:, 120 + k : 121 + k], (PIECE, 128))

    def mixed(values, which, shards, bits, transposed):
        def selfs(a, k):
            return twb[which, shards[a][0], shards[a][1], k]

        def crosses(a, k):
            return twb[which, shards[a][0], shards[a][1], 6 + k]

        return mix(values, selfs, crosses, bits, transposed)

    low_bits = ((0, 0), (1, 1), (2, 2))
    high_bits = ((3, 0), (4, 1), (5, 2))
    low_back = tuple(reversed(low_bits))
    high_back = tuple(reversed(high_bits))

    def row_of(sz):
        return [(sz, a) for a in range(SIDE)]

    def column_of(sy):
        return [(a, sy) for a in range(SIDE)]

    def two_at_once(lines, read, which, bits, transposed, write):
        def step(t):
            groups = [lines(2 * t), lines(2 * t + 1)]
            held = [[read(p, q) for p, q in shards] for shards in groups]
            held = [mixed(values, which, shards, bits, transposed) for values, shards in zip(held, groups)]
            for shards, values in zip(groups, held):
                for (p, q), value in zip(shards, values):
                    write(p, q, value)

        repeat(SIDE // 2, step)

    def store_wide(p, q, value):
        ff[p, q] = value

    def load_wide(p, q):
        return ff[p, q]

    from_mate(kt, ka_v, kb_v)

    def spread_output_twiddles(sz):
        for p, q in row_of(sz):
            spread_twiddles(1, p, q, kt[q, p, :, 128:256])

    repeat(SIDE, spread_output_twiddles)

    for h in (1, 0):
        lanes = slice(128 * h, 128 * h + 128)

        def forward_one(step, h=h):
            sz = wrapped(z + step)
            await_bytes(a1.at[h, sz], v1.at[h, sz])
            shards = row_of(sz)
            if h == 1:
                for p, q in shards:
                    spread_twiddles(0, p, q, a1[1, p, q])
            values = mixed([a1[h, p, q].astype(F32) for p, q in shards], 0, shards, low_bits, False)
            for (p, q), value in zip(shards, values):
                ff[p, q] = value

        repeat(SIDE, forward_one)

        def weigh(p, q, value, h=h, lanes=lanes):
            rounded = value.astype(BF)
            sp[h, p, q] = rounded
            ff[p, q] = rounded.astype(F32) * kt[q, p, :, lanes].astype(F32)

        def leave(p, q, value, h=h):
            src2[h, p, q] = value.astype(BF)

        two_at_once(column_of, load_wide, 0, high_bits, False, weigh)
        two_at_once(row_of, load_wide, 1, low_bits, False, store_wide)
        two_at_once(column_of, load_wide, 1, high_bits, False, leave)
        for part in range(2):
            send_part(part, *half_of(h, src2, m2, s2, v2, (z, y), z))

    for g in range(GROUPS):
        acot[g] = dot(cotg[g], dnp[g])
        channel, j = iotas((D, 256))
        spread = ones_where((channel == 4 * j + g) & (j < DG))
        ww[:, pl.ds(g * 512, 512)] = dot(spread, dnp[g]).astype(BF)

    lane_here = (lax.broadcasted_iota(jnp.int32, (256, 256), 1) & 127) < DG - 128
    squares = jnp.zeros((256, 1), F32)
    for h in (1, 0):
        for sz in range(SIDE):
            await_bytes(m2.at[h, sz], v2.at[h, sz])
        for pair in range(2):
            value = half_lanes(xg, h, pair).astype(F32) + dot(mout_ref[...], load_half(m2, h, pair))
            if h == 1:
                value = jnp.where(lane_here, value, 0.0)
            value = value.astype(BF)
            for side in range(2):
                hg[2 * pair + side, :, 128 * h : 128 * h + 128] = value[:, 128 * side : 128 * side + 128]
            wide = value.astype(F32)
            squares = squares + jnp.sum(wide * wide, axis=1, keepdims=True)
    scale_column = lax.rsqrt(squares * (1.0 / D) + 1e-06)
    rowscale[...] = jnp.broadcast_to(scale_column, (256, 128))

    for g in range(GROUPS):
        wide = hg[g].astype(F32)
        ng[g] = (wide * rowscale[:, 0:1] * gaing[g, 0:1]).astype(BF)
        pa[...] = dot(ng[g], upp[g])

        def activate(tile, g=g):
            rows = pl.ds(pl.multiple_of(tile * 64, 64), 64)
            p = pa[rows]
            square = p * p
            tangent = jnp.tanh(p * (ROOT_HALF + (ROOT_HALF * CUBIC) * square))
            half_more = 0.5 + 0.5 * tangent
            act[rows, pl.ds(g * 512, 512)] = (p * half_more).astype(BF)
            inner = ROOT_HALF + (3.0 * ROOT_HALF * CUBIC) * square
            slope = half_more + 0.5 * p * (1.0 - tangent * tangent) * inner
            pgr[g, rows] = (acot[g, rows] * slope).astype(BF)

        repeat(4, activate)
        ngr[g] = dot_nt(pgr[g], upp[g])

    means = jnp.zeros((256, 1), F32)
    for g in range(GROUPS):
        means = means + jnp.sum(ngr[g] * gaing[g, 0:1] * hg[g].astype(F32), axis=1, keepdims=True)
    scale_column = rowscale[:, 0:1]
    means = means * (1.0 / D) * scale_column * scale_column * scale_column
    for h in (1, 0):
        lanes = slice(128 * h, 128 * h + 128)
        for pair in range(2):
            for g in (2 * pair, 2 * pair + 1):
                gained = ngr[g, :, lanes] * gaing[g, 0:1, lanes]
                wide = hg[g, :, lanes].astype(F32)
                hgr[g, :, lanes] = (cotn[g, :, lanes].astype(F32) + scale_column * gained - wide * means).astype(BF)
            store_half(src3, h, pair, dot(moutt[...], half_lanes(hgr, h, pair)).astype(BF))
        for part in range(2):
            send_part(part, *half_of(h, src3, a3, s3, v3, (y, z), y))

    row_here = (lax.broadcasted_iota(jnp.int32, (512, 256), 0) & 31) == 30
    for g in range(GROUPS):
        gain_term = jnp.sum(ngr[g] * hg[g].astype(F32) * rowscale[:, 0:1], axis=0, keepdims=True)
        up_term = jnp.where(row_here, gain_term, dot_tn(pgr[g], ng[g]))
        down_term = dot_tn(act[:, pl.ds(g * 512, 512)], cotg[g])
        for kind, term in ((0, up_term), (1, down_term)):
            split = term.astype(BF).reshape(16, 2, PIECE, 256)
            for half in range(2):
                for side in range(2):
                    gg[side, 2 * kind + half, pl.ds(g * 16, 16)] = split[:, half, :, side * 128 : side * 128 + 128]

    send(gg.at[1 - core], r1a, ga_s, ga_v, {"dp": mate})

    await_bytes(r1a, ga_v)

    def pair_sum(step):
        for slab in range(4):
            part = pl.ds(pl.multiple_of(step * 8, 8), 8)
            both = gg[core, slab, part].astype(F32) + r1a[slab, part].astype(F32)
            h1[slab, part] = both.astype(BF)

    repeat(8, pair_sum)

    def spread_terms(step):
        other = lax.rem(chip + step, 4)
        send(h1.at[other], r1b.at[chip], gb_s.at[step], gb_v.at[step], {"dp": other * 2 + core})

    repeat(4, spread_terms, 1)

    others = [lax.rem(chip + step, 4) for step in (1, 2, 3)]

    for h in (1, 0):
        lanes = slice(128 * h, 128 * h + 128)

        def backward_one(step, h=h):
            sy = wrapped(y + step)
            await_bytes(a3.at[h, sy], v3.at[h, sy])
            shards = column_of(sy)
            values = mixed([a3[h, q, p].astype(F32) for p, q in shards], 1, shards, high_back, True)
            for (p, q), value in zip(shards, values):
                ff[p, q] = value

        repeat(SIDE, backward_one)

        def weigh_back(p, q, value, h=h, lanes=lanes):
            wide = value.astype(BF).astype(F32)
            owner = wrapped(q + y)
            kgb[lax.rem(owner, 2), lax.div(owner, 2), p, :, lanes] = (sp[h, p, q].astype(F32) * wide).astype(BF)
            ff[p, q] = wide * kt[q, p, :, lanes].astype(F32)

        def leave_back(p, q, value, h=h):
            src4[h, p, q] = value.astype(BF)

        two_at_once(row_of, load_wide, 1, low_back, True, weigh_back)
        if h == 0:
            send(kgb.at[1 - core], kra, kr_s, kr_v, {"dp": mate})
        two_at_once(column_of, load_wide, 0, high_back, True, store_wide)
        two_at_once(row_of, load_wide, 0, low_back, True, leave_back)
        last = half_of(h, src4, m4, s4, v4, (z, y), z)
        send_part(0, *last)
        if h == 1:
            send_part(1, *last)

    await_bytes(kra, kr_v)

    def kernel_pair(sz):
        for at in range(4):
            kgh[at, sz] = (kgb[core, at, sz].astype(F32) + kra[at, sz].astype(F32)).astype(BF)

    repeat(SIDE, kernel_pair)

    def spread_kernel_terms(step):
        other = lax.rem(chip + step, 4)
        send(kgh.at[other], krb.at[chip], kc_s.at[step], kc_v.at[step], {"dp": other * 2 + core})

    repeat(4, spread_kernel_terms, 1)

    def terms_here(step):
        await_bytes(r1b.at[lax.rem(chip + 4 - step, 4)], gb_v.at[step])

    repeat(4, terms_here, 1)

    def chip_sum(t):
        for odd in range(2):
            sz = 2 * t + odd
            part = pl.ds(pl.multiple_of(sz * 8, 8), 8)
            four = h1[chip, part].astype(F32)
            for other in others:
                four = four + r1b[other, part].astype(F32)
            four = four.astype(BF)
            for q in range(SIDE):
                if (odd + q) % 2 == 0:
                    pa1[q, t] = four[q]
                else:
                    pb1[sz, q // 2] = four[q]

    repeat(SIDE // 2, chip_sum)

    def along_y(step):
        ty = wrapped(y + step)
        send(pa1.at[ty], pa2.at[y], pa_s.at[step], pa_v.at[step], {"seq": z * SIDE + ty})

    def along_z(step):
        tz = wrapped(z + step)
        send(pb1.at[tz], pb2.at[z], pb_s.at[step], pb_v.at[step], {"seq": tz * SIDE + y})

    def first_step(step):
        along_y(step)
        along_z(step)

    repeat(SIDE, first_step, 1)

    def kernel_terms_here(step):
        await_bytes(krb.at[lax.rem(chip + 4 - step, 4)], kc_v.at[step])

    repeat(4, kernel_terms_here, 1)

    def kernel_sum(sz):
        four = kgh[chip, sz].astype(F32)
        for other in others:
            four = four + krb[other, sz].astype(F32)
        kgs[sz] = four.astype(BF)

    repeat(SIDE, kernel_sum)

    def return_kernel(dz):
        tz = wrapped(z + dz)
        send(kgs.at[tz], kgf.at[y, z], kf_s.at[1], kf_v, {"seq": tz * SIDE + yo})

    repeat(SIDE, return_kernel, 1)

    @pl.when(yo != y)
    def _():
        send(kgs.at[z], kgf.at[y, z], kf_s.at[0], kf_v, {"seq": z * SIDE + yo})

    @pl.when(yo == y)
    def _():
        pltpu.make_async_copy(kgs.at[z], kgf.at[y, z], kf_v).start()

    send_part(1, *last)

    acc[...] = dot_nt(ww[...], act[...])
    for g in range(GROUPS):
        rows = pl.ds(g * DG, DG)
        outv[rows] = (acc[rows] + dot_nt(eye[0:DG], hg[g])).astype(BF)
    pltpu.make_async_copy(outv, out_hbm, out_s.at[0]).start()

    def first_here(step):
        await_bytes(pa2.at[wrapped(y - step)], pa_v.at[step])
        await_bytes(pb2.at[wrapped(z - step)], pb_v.at[step])

    repeat(SIDE, first_here, 1)
    sum_y, sum_z = pa1[y].astype(F32), pb1[z].astype(F32)
    for step in range(1, SIDE):
        sum_y = sum_y + pa2[wrapped(y + step)].astype(F32)
        sum_z = sum_z + pb2[wrapped(z + step)].astype(F32)
    pa3[...] = sum_y.astype(BF)
    pb3[...] = sum_z.astype(BF)
    odd = lax.rem(z + y, 2)

    def second_z(m):
        return 2 * m + lax.rem(y, 2)

    def second_y(m):
        return 2 * m + 1 - lax.rem(z, 2)

    for m in range(4):

        @pl.when(second_z(m) != z)
        def _(m=m):
            send(pa3.at[m], pc.at[z], pc_s.at[m], pc_v.at[z], {"seq": second_z(m) * SIDE + y})

        @pl.when(second_y(m) != y)
        def _(m=m):
            send(pb3.at[m], pc.at[y], pd_s.at[m], pc_v.at[y], {"seq": z * SIDE + second_y(m)})

    @pl.when(odd == 0)
    def _():
        pc[z] = pa3[lax.div(z, 2)]

    @pl.when(odd == 1)
    def _():
        pc[y] = pb3[lax.div(y, 2)]

    await_bytes(kgf.at[yo], kf_v)
    to_chips(kgf, kh_s, kh_v)

    own = z + odd * (y - z)

    def second_here(step):
        at = wrapped(own + step)
        await_bytes(pc.at[at], pc_v.at[at])

    repeat(SIDE, second_here, 1)
    shard_sum = pc[0].astype(F32)
    for at in range(1, SIDE):
        shard_sum = shard_sum + pc[at].astype(F32)
    shard_sum = shard_sum * SCALE
    fin[...] = shard_sum
    rf[i] = shard_sum

    def spread_grads(step):
        send(fin, rf.at[i], gf_s.at[step], gf_v.at[step], {"dp": wrapped(i + step)})

    repeat(SIDE, spread_grads, 1)
    to_mate(kgf, kh_v, ki_s, ki_v)

    for h in (1, 0):
        lanes = slice(128 * h, 128 * h + 128)
        for sz in range(SIDE):
            await_bytes(m4.at[h, sz], v4.at[h, sz])
        for pair in range(2):
            value = half_lanes(hgr, h, pair).astype(F32) + dot(mint[...], load_half(m4, h, pair))
            value = dot_nt(eye[...], value.astype(BF)).astype(BF)
            for side in range(2):
                start = (2 * pair + side) * DG + 128 * h
                rows = DG - 128 if h == 1 else 128
                igv[pl.ds(start, rows)] = value[128 * side : 128 * side + rows]
    pltpu.make_async_copy(igv, ig_hbm, out_s.at[2]).start()

    from_mate(kgf, kh_v, ki_v)
    for g in range(GROUPS):
        held = jnp.stack([kgf[g], kgf[4 + g]], axis=1).reshape(256, 256)
        kgv[pl.ds(g * DG, DG)] = dot_nt(eye[0:DG], held).astype(BF)
    pltpu.make_async_copy(kgv, kg_hbm, out_s.at[1]).start()

    def grads_here(step):
        await_bytes(rf.at[wrapped(i - step)], gf_v.at[step])

    repeat(SIDE, grads_here, 1)
    for share in range(SIDE):
        kind, half, side = share // 4, (share // 2) % 2, share % 2
        wsum[kind, pl.ds(half * PIECE, PIECE), pl.ds(side * 128, 128)] = rf[share]
    ugv[...] = wsum[0, 0:30, 0:DG]
    dgv[...] = wsum[1, 0:30, 0:DG]
    j, lane = iotas((256, 128))
    picker = jnp.where(j == lane + 15 * lax.rem(me, 16), 1.0, 0.0)
    gains = jnp.broadcast_to(wsum[0, 30:31], (8, 256))
    picked = lax.dot_general(
        gains, picker, (((1,), (0,)), ((), ())), precision=lax.Precision.HIGHEST, preferred_element_type=F32
    )
    gnv[...] = picked[0:1, 0:15]
    pltpu.make_async_copy(ugv, ug_hbm, out_s.at[3]).start()
    pltpu.make_async_copy(dgv, dg_hbm, out_s.at[4]).start()
    pltpu.make_async_copy(gnv, gn_hbm, out_s.at[5]).start()

    for buffer, sem in ((src1, s1), (src2, s2), (src3, s3), (src4, s4)):
        for h in range(2):
            await_sent(buffer.at[h], sem.at[h])
    for m in range(4):

        @pl.when(second_z(m) != z)
        def _(m=m):
            await_bytes(pa3.at[m], pc_s.at[m])

        @pl.when(second_y(m) != y)
        def _(m=m):
            await_bytes(pb3.at[m], pd_s.at[m])

    await_bytes(ks.at[0, pl.ds(0, 7)], ks_s.at[1])
    await_bytes(kgs.at[pl.ds(0, 7)], kf_s.at[1])

    @pl.when(yo != y)
    def _():
        await_bytes(ks.at[0, 0], ks_s.at[0])
        await_bytes(kgs.at[0], kf_s.at[0])

    await_bytes(kt.at[0], ka_s.at[0])
    await_bytes(kgf.at[0], kh_s.at[0])
    await_bytes(r1a, ga_s)
    await_bytes(kra, kr_s)

    def chips_left(step):
        await_bytes(kt.at[0], ka_s.at[step])
        await_bytes(kt.at[0], kb_s.at[step])
        await_bytes(kgf.at[0], kh_s.at[step])
        await_bytes(kgf.at[0], ki_s.at[step])
        await_bytes(kgh.at[0], kc_s.at[step])
        await_bytes(h1.at[0], gb_s.at[step])

    repeat(4, chips_left, 1)

    def grads_left(step):
        await_bytes(fin, gf_s.at[step])
        await_bytes(pa1.at[0], pa_s.at[step])
        await_bytes(pb1.at[0], pb_s.at[step])

    repeat(SIDE, grads_left, 1)
    outs = ((outv, out_hbm), (kgv, kg_hbm), (igv, ig_hbm), (ugv, ug_hbm), (dgv, dg_hbm), (gnv, gn_hbm))
    for index, (held, there) in enumerate(outs):
        pltpu.make_async_copy(held, there, out_s.at[index]).wait()


def settle(*refs):
    source, there, held, sems = refs[:6], refs[6:12], refs[12:18], refs[18]
    loads = [pltpu.make_async_copy(source[index], held[index], sems.at[0, index]) for index in range(6)]
    stores = [pltpu.make_async_copy(held[index], there[index], sems.at[1, index]) for index in range(6)]
    for copy in loads:
        copy.start()
    for load, store in zip(loads, stores):
        load.wait()
        store.start()
    for copy in stores:
        copy.wait()


def local(
    inputs, cotangent, kernel_values, mix_in, mix_out, twiddle_self, twiddle_cross, norm_gain, up_weight, down_weight
):
    hbm = pl.BlockSpec(memory_space=pltpu.HBM)
    dma = pltpu.SemaphoreType.DMA
    vmem = pltpu.VMEM
    exchange = vmem((SIDE, SIDE, PIECE, 256), BF)
    halves = vmem((2, SIDE, SIDE, PIECE, 128), BF)
    part = vmem((SIDE, 4, PIECE, 128), BF)
    both = dma((2, SIDE))
    grouped = vmem((GROUPS, 256, 256), BF)
    square = vmem((256, 256), BF)
    quarter = vmem((4, SIDE, PIECE, 256), BF)
    terms = vmem((4, 64, PIECE, 128), BF)
    wide = (D, 256)
    scratch = dict(
        xv=grouped, kv=grouped, cotv=grouped, min_ref=square, mout_ref=square,
        ts_ref=vmem((6, 2, 256), BF), tc_ref=vmem((6, 2, 256), BF), gain_ref=vmem((D,), BF),
        up_ref=vmem((DG, 1920), BF), down_ref=vmem((DG, 1920), BF),
        outv=vmem(wide, BF), igv=vmem(wide, BF), kgv=vmem(wide, BF),
        ugv=vmem((30, DG), F32), dgv=vmem((30, DG), F32), gnv=vmem((1, 15), F32),
        eye=square, mint=square, moutt=square, twp=vmem((2, 256, 256), F32),
        xg=grouped, cotg=grouped, cotn=grouped,
        upp=vmem((GROUPS, 256, 512), BF), dnp=vmem((GROUPS, 256, 512), BF), ww=vmem((D, 2048), BF),
        acot=vmem((GROUPS, 256, 512), F32), pa=vmem((256, 512), F32), act=vmem((256, 2048), BF),
        pgr=vmem((GROUPS, 256, 512), BF), hg=grouped, ng=grouped, ngr=vmem((GROUPS, 256, 256), F32),
        hgr=grouped, acc=vmem(wide, F32), gaing=vmem((GROUPS, 8, 256), F32), rowscale=vmem((256, 128), F32),
        wsum=vmem((2, 32, 256), F32),
        src1=halves, a1=halves, ks=exchange, kt=exchange, ff=vmem((SIDE, SIDE, PIECE, 128), F32), sp=halves,
        src2=halves, m2=halves, src3=halves, a3=halves, src4=halves, m4=halves,
        pa1=part, pa2=part, pa3=vmem((4, PIECE, 128), BF), pb1=part, pb2=part, pb3=vmem((4, PIECE, 128), BF),
        pc=vmem((SIDE, PIECE, 128), BF),
        twb=vmem((2, SIDE, SIDE, 12, PIECE, 128), F32),
        kgb=vmem((2, 4, SIDE, PIECE, 256), BF), kra=quarter, kgh=quarter, krb=quarter,
        kgs=vmem((SIDE, PIECE, 256), BF), kgf=exchange,
        gg=vmem((2, 4, 64, PIECE, 128), BF), r1a=terms, h1=terms, r1b=terms,
        fin=vmem((PIECE, 128), F32), rf=vmem((SIDE, PIECE, 128), F32),
        in_s=dma((19,)), out_s=dma((6,)),
        s1=both, v1=both, s2=both, v2=both, s3=both, v3=both, s4=both, v4=both,
        pa_s=dma((SIDE,)), pa_v=dma((SIDE,)), pb_s=dma((SIDE,)), pb_v=dma((SIDE,)),
        pc_s=dma((4,)), pc_v=dma((SIDE,)), pd_s=dma((4,)),
        ks_s=dma((2,)), ks_v=dma, ka_s=dma((4,)), ka_v=dma((4,)), kb_s=dma((4,)), kb_v=dma((4,)),
        kr_s=dma, kr_v=dma, kc_s=dma((4,)), kc_v=dma((4,)), kf_s=dma((2,)), kf_v=dma,
        kh_s=dma((4,)), kh_v=dma((4,)), ki_s=dma((4,)), ki_v=dma((4,)),
        ga_s=dma, ga_v=dma, gb_s=dma((4,)), gb_v=dma((4,)), gf_s=dma((SIDE,)), gf_v=dma((SIDE,)),
    )
    shape = jax.ShapeDtypeStruct
    results = [shape(wide, BF)] * 3 + [shape((30, DG), F32)] * 2 + [shape((1, 15), F32)]
    held = pl.pallas_call(
        kernel,
        out_shape=results,
        in_specs=[hbm] * 10,
        out_specs=[hbm] * 6,
        scratch_shapes=scratch,
        compiler_params=pltpu.CompilerParams(
            collective_id=0, has_side_effects=True, vmem_limit_bytes=58 * 1024 * 1024
        ),
        cost_estimate=pl.CostEstimate(flops=4_000_000_000, bytes_accessed=6_000_000, transcendentals=600_000),
    )(
        inputs[0].T, cotangent[0].T, kernel_values.T, mix_in, mix_out,
        twiddle_self.transpose(1, 0, 2), twiddle_cross.transpose(1, 0, 2),
        norm_gain, up_weight, down_weight,
    )
    output, input_grad, kernel_grad, up_grad, down_grad, gain_grad = pl.pallas_call(
        settle,
        out_shape=results,
        in_specs=[hbm] * 6,
        out_specs=[hbm] * 6,
        scratch_shapes=[vmem(result.shape, result.dtype) for result in results] + [dma((2, 6))],
        compiler_params=pltpu.CompilerParams(vmem_limit_bytes=58 * 1024 * 1024),
        cost_estimate=pl.CostEstimate(flops=0, bytes_accessed=3_000_000, transcendentals=0),
    )(*held)
    return output.T[None], input_grad.T[None], kernel_grad.T, up_grad.T, down_grad.T, gain_grad[0]


def solution(mesh):
    in_specs = (
        P("dp", "seq", None),
        P("dp", "seq", None),
        P("seq", None),
        P("seq", None),
        P("seq", None),
        P(None, None, "seq"),
        P(None, None, "seq"),
        P(),
        P(),
        P(),
    )
    out_specs = (
        P("dp", "seq", None),
        P("dp", "seq", None),
        P("seq", None),
        P(None, "seq"),
        P(None, "seq"),
        P("seq"),
    )
    return jax.shard_map(local, mesh=mesh, in_specs=in_specs, out_specs=out_specs, check_vma=False)
```
